32 devices in a mesh: dp: 32 (over z, y, x, core).
Axes of the slice: x: 2, y: 2, z: 4, core: 2. Of those that a mesh axis runs over, the one named last changes fastest.
Arguments:
- images: bfloat16 [64, 197, 384], P('dp'), may hold values from -6 to 6
- cotangent: bfloat16 [64, 197, 384], P('dp'), may hold values from -6 to 6
- present: int32 [64], P('dp'), may hold values 0 or 1
- params: float32 [2, 1777664], P(None, 'dp'), as said below
- first_moment: float32 [2, 1777664], P(None, 'dp'), as said below
- second_moment: float32 [2, 1777664], P(None, 'dp'), as said below
Outputs:
- outputs: float32 [64, 197, 384], P('dp')
- input_grad: float32 [64, 197, 384], P('dp')
- new_params: float32 [2, 1777664], P(None, 'dp')
- new_first: float32 [2, 1777664], P(None, 'dp')
- new_second: float32 [2, 1777664], P(None, 'dp')
The draws below stay inside these ranges and needn't reach their ends.
Inputs may be any that keep to these rules, and one draw needn't show every extreme that they name: `params`: gains near 1, weights scaled by their fan-in. `first_moment`: both signs. `second_moment`: every entry positive.
All inputs are finite; a program needn't handle non-finite values. No bound on the sum of `present` on one device may be relied on, other than what follows from the above.
Results may differ from the reference program's by a relative error of at most 0.012.
Values may be sent and summed in bfloat16 or wider, within the bound.
No kernel may reach another device: no remote copies, remote signals or barrier semaphores. Data moves between devices by JAX's collectives and lax.ppermute only.
A program may use at most 128 MiB of HBM per device.

```python
import math
import jax
import jax.numpy as jnp
import numpy as np
from jax import lax

D = 384
FF = 1536
HEADS = 6
HEAD_DIM = 64
SEQ = 197
MICRO = 2
STEP = 10
P_SIZE = 1774080
TOTAL = 1777664
IMAGES = 64
TOK_ALL = 12608


def segment_table():
    return [(D, 0.1, 1.0, 0.3), (D, 0.1, 0.0, 0.3), (3 * D * D, D ** (-0.5), 0.0, 0.3), (D, 0.1, 0.0, 0.3), (D, 0.1, 0.0, 0.3), (D * D, 2.0 * D ** (-0.5), 0.0, 0.3), (D, 0.1, 0.0, 1.0), (D, 0.1, 1.0, 0.5), (D, 0.1, 0.0, 0.5), (D * FF, D ** (-0.5), 0.0, 0.4), (FF, 0.1, 0.0, 0.4), (FF * D, FF ** (-0.5), 0.0, 0.5), (D, 0.1, 0.0, 1.0), (TOTAL - P_SIZE, 0.1, 0.0, 0.3)]


def column_of(field):
    parts = [np.full((entry[0],), entry[field], np.float32) for entry in segment_table()]
    return jnp.asarray(np.concatenate(parts))[None, :]


def draw_params(key, part):
    key = jax.random.fold_in(key, 11)
    base = jax.random.normal(key, (2, TOTAL), jnp.float32)
    return column_of(2) + column_of(1) * base


def draw_first_moment(key, part):
    key = jax.random.fold_in(key, 23)
    typical = column_of(3) * math.sqrt(0.75 * TOK_ALL)
    base = jax.random.normal(key, (2, TOTAL), jnp.float32)
    return 0.111 * typical * base


def draw_second_moment(key, part):
    key = jax.random.fold_in(key, 37)
    typical = column_of(3) * column_of(3) * (0.75 * TOK_ALL)
    factor = jnp.exp(jax.random.uniform(key, (2, TOTAL), jnp.float32, math.log(0.5), math.log(8.0)))
    return 0.001 * typical * factor


def plant(drawn, rng, least, high):
    shape = drawn.shape
    spot = [jax.random.randint(jax.random.fold_in(rng, axis), (), 0, shape[axis]) for axis in range(len(shape))]
    drawn = drawn.at[tuple(spot)].set(least)
    longest = shape.index(max(shape))
    spot[longest] = (spot[longest] + 1) % shape[longest]
    return drawn.at[tuple(spot)].set(high)


def shard_levels(own_key, shape, cuts, low, top_value):
    loudness = 1.0
    for dim, blocks in cuts:
        draws = jax.random.uniform(jax.random.fold_in(jax.random.fold_in(own_key, 6), dim), (blocks,), jnp.float32, low / len(cuts), top_value / len(cuts))
        loudness = loudness * jnp.repeat(jnp.exp(draws), shape[dim] // blocks).reshape((-1,) + (1,) * (len(shape) - 1 - dim))
    return loudness


def normal_values(key, extent, width, most, shards=(), held_as=jnp.bfloat16):
    level = shard_levels(key, extent, shards, -0.22, 0.18) if shards else 1.0
    array = jax.random.normal(key, extent, jnp.float32) * width * level
    return jnp.minimum(jnp.maximum(array, -most), most).astype(held_as)


def setup_inputs(seed: int = 0) -> dict:
    key_of = jax.random.split(jax.random.key(seed), 7)
    images = normal_values(key_of[0], (IMAGES, SEQ, D), 1.0, 6.0, ((0, 32),))
    cotangent = normal_values(key_of[1], (IMAGES, SEQ, D), 1.0, 6.0, ((0, 32),))
    present = plant((jax.random.randint(key_of[2], (IMAGES,), 0, 4) < 3).astype(jnp.int32), jax.random.fold_in(key_of[2], 1), 0, 1)
    params = draw_params(jax.random.fold_in(key_of[6], 71), 0)
    first_moment = draw_first_moment(jax.random.fold_in(key_of[6], 71), 0)
    second_moment = draw_second_moment(jax.random.fold_in(key_of[6], 71), 0)
    return {"images": images, "cotangent": cotangent, "present": present, "params": params, "first_moment": first_moment, "second_moment": second_moment}


@jax.custom_vjp
def low(v):
    return lax.optimization_barrier(v.astype(jnp.bfloat16)).astype(jnp.float32)

@jax.custom_vjp
def low_back(v):
    return v

def low_keep(v):
    return (low(v), None)

def low_pass(kept, grad):
    return (grad,)

def back_keep(v):
    return (v, None)

def back_low(kept, grad):
    return (low(grad),)
low.defvjp(low_keep, low_pass)
low_back.defvjp(back_keep, back_low)
HIGHEST = lax.Precision.HIGHEST
eps_norm = 1e-06
beta_one = 0.9
beta_two = 0.999
adam_eps = 1e-08
rate_matrix = 0.1
rate_vector = 0.5
decay_matrix = 0.05

def layout():
    return [('ln1_gain', (D,)), ('ln1_shift', (D,)), ('w_qkv', (D, 3 * D)), ('bias_query', (D,)), ('bias_value', (D,)), ('w_attn_out', (D, D)), ('bias_attn_out', (D,)), ('ln2_gain', (D,)), ('ln2_shift', (D,)), ('w_lift', (D, FF)), ('bias_lift', (FF,)), ('w_drop', (FF, D)), ('bias_drop', (D,))]

def unflatten(flat_row):
    pieces = {}
    offset = 0
    for label, shape in layout():
        count = math.prod(shape)
        pieces[label] = flat_row[offset:offset + count].reshape(shape)
        offset = offset + count
    return pieces

def matrix_flags(position):
    square = D * D
    lifted = D * FF
    bounds = [(2 * D, 2 * D + 3 * square), (4 * D + 3 * square, 4 * D + 4 * square), (7 * D + 4 * square, 7 * D + 4 * square + lifted), (7 * D + 4 * square + lifted + FF, 7 * D + 4 * square + 2 * lifted + FF)]
    flags = jnp.zeros(position.shape, dtype=bool)
    for lower, upper in bounds:
        flags = flags | (position >= lower) & (position < upper)
    return flags

def normalize(values, gain, shift):
    center = values - lax.optimization_barrier(jnp.mean(values, -1, keepdims=True))
    spread = lax.optimization_barrier(jnp.mean(center * center, -1, keepdims=True))
    return center * lax.rsqrt(spread + eps_norm) * gain + shift

def encoder_layer(weights, state):
    group = state.shape[0]
    normed_one = low(normalize(state, weights['ln1_gain'], weights['ln1_shift']))
    bias = jnp.concatenate([weights['bias_query'], jnp.zeros_like(weights['bias_query']), weights['bias_value']])
    qkv = jnp.einsum('gsd,de->gse', normed_one, weights['w_qkv'], precision=HIGHEST) + bias
    qkv = low_back(low(qkv))
    query = qkv[:, :, :D].reshape(group, SEQ, HEADS, HEAD_DIM)
    key_rows = qkv[:, :, D:2 * D].reshape(group, SEQ, HEADS, HEAD_DIM)
    value_rows = qkv[:, :, 2 * D:].reshape(group, SEQ, HEADS, HEAD_DIM)
    scores = jnp.einsum('gqhd,gkhd->ghqk', query, key_rows, precision=HIGHEST) * HEAD_DIM ** (-0.5)
    scores = low_back(scores)
    probs = jax.nn.softmax(scores, axis=-1)
    mixed = jnp.einsum('ghqk,gkhd->gqhd', low(probs), value_rows, precision=HIGHEST)
    mixed = low_back(low(mixed)).reshape(group, SEQ, D)
    attended = jnp.einsum('gsd,de->gse', mixed, weights['w_attn_out'], precision=HIGHEST) + weights['bias_attn_out']
    hidden = state + low_back(attended)
    normed_two = low(normalize(hidden, weights['ln2_gain'], weights['ln2_shift']))
    lifted = jnp.einsum('gsd,df->gsf', normed_two, weights['w_lift'], precision=HIGHEST) + weights['bias_lift']
    lifted = low_back(lifted)
    active = low(jax.nn.gelu(lifted, approximate=False))
    dropped = jnp.einsum('gsf,fd->gsd', active, weights['w_drop'], precision=HIGHEST) + weights['bias_drop']
    return hidden + low_back(dropped)

def stacked(params, state):
    weights = low(params)
    for layer_at in range(2):
        state = encoder_layer(unflatten(weights[layer_at]), state)
    return state

def reference(images, cotangent, present, params, first_moment, second_moment):
    group = 4 * MICRO
    count = IMAGES // group
    inputs = images.astype(jnp.float32).reshape(count, group, SEQ, D)
    seeds = cotangent.astype(jnp.float32) * present.astype(jnp.float32)[:, None, None]
    seeds = seeds.reshape(count, group, SEQ, D)

    def one_group(total, pair):
        block_in, block_seed = pair
        result, pull = jax.vjp(stacked, params, block_in)
        param_grad, input_part = pull(block_seed)
        return (total + param_grad, (result, input_part))
    grads, (results, input_parts) = lax.scan(one_group, jnp.zeros_like(params), (inputs, seeds))
    outputs = results.reshape(IMAGES, SEQ, D)
    input_grad = input_parts.reshape(IMAGES, SEQ, D)
    position = jnp.arange(TOTAL, dtype=jnp.int32)
    flags = matrix_flags(position)[None, :]
    rate = jnp.where(flags, rate_matrix, rate_vector)
    decay = jnp.where(flags, decay_matrix, 0.0)
    new_first = beta_one * first_moment + (1.0 - beta_one) * grads
    new_second = beta_two * second_moment + (1.0 - beta_two) * grads * grads
    first_hat = new_first / (1.0 - beta_one ** STEP)
    second_hat = new_second / (1.0 - beta_two ** STEP)
    new_params = params - rate * (first_hat / (jnp.sqrt(second_hat) + adam_eps) + decay * params)
    return (outputs, input_grad, new_params, new_first, new_second)
```

```python
import functools
import math

import jax
import jax.numpy as jnp
from jax import lax
from jax.experimental import pallas as pl
from jax.experimental.pallas import tpu as pltpu
from jax.sharding import PartitionSpec as P

D = 384
FF = 1536
HEADS = 6
HEAD_DIM = 64
SEQ = 197
MICRO = 2
STEP = 10
P_SIZE = 1774080

LANES = 128
ROWS = 208
TOKENS = MICRO * ROWS
PAIRS = HEADS // 2
BLOCK = 512

eps_norm = 1e-06
beta_one = 0.9
beta_two = 0.999
adam_eps = 1e-08
rate_matrix = 0.1
rate_vector = 0.5
decay_matrix = 0.05
sqrt_half = 0.7071067811865476
inverse_root_tau = 0.3989422804014327

f32 = jnp.float32
bf16 = jnp.bfloat16


def layout():
    return [
        ("ln1_gain", (D,)),
        ("ln1_shift", (D,)),
        ("w_qkv", (D, 3 * D)),
        ("bias_query", (D,)),
        ("bias_value", (D,)),
        ("w_attn_out", (D, D)),
        ("bias_attn_out", (D,)),
        ("ln2_gain", (D,)),
        ("ln2_shift", (D,)),
        ("w_lift", (D, FF)),
        ("bias_lift", (FF,)),
        ("w_drop", (FF, D)),
        ("bias_drop", (D,)),
    ]


def row_offsets():
    offsets, at = {}, 0
    for label, shape in layout():
        offsets[label] = at
        at += math.prod(shape) // LANES
    offsets["end"] = at
    return offsets


ROW = row_offsets()
MLP_ROW = ROW["ln2_gain"]


def matrix_flags(position):
    square = D * D
    lifted = D * FF
    bounds = [
        (2 * D, 2 * D + 3 * square),
        (4 * D + 3 * square, 4 * D + 4 * square),
        (7 * D + 4 * square, 7 * D + 4 * square + lifted),
        (7 * D + 4 * square + lifted + FF, 7 * D + 4 * square + 2 * lifted + FF),
    ]
    flags = jnp.zeros(position.shape, dtype=bool)
    for lower, upper in bounds:
        flags = flags | (position >= lower) & (position < upper)
    return flags


def round_up(value, step):
    return (value + step - 1) // step * step


def dot(a, b, dims):
    return lax.dot_general(a, b, ((dims[0], dims[1]), ((), ())), preferred_element_type=f32)


def dot_nn(a, b):
    return dot(a, b, ((1,), (0,)))


def dot_nt(a, b):
    return dot(a, b, ((1,), (1,)))


def dot_tn(a, b):
    return dot(a, b, ((0,), (0,)))


def read_vector(flat, row, count):
    parts = [flat[row + i : row + i + 1, :] for i in range(count)]
    return jnp.concatenate(parts, axis=1)


def write_vector(flat, row, values):
    for i in range(values.shape[1] // LANES):
        flat[row + i : row + i + 1, :] = values[:, i * LANES : (i + 1) * LANES]


def read_matrix(flat, row, out, depth, width):
    blocks = width // LANES
    for j in range(blocks):
        part = flat[pl.ds(row + j, depth, stride=blocks), :]
        out[:, j * LANES : (j + 1) * LANES] = part.astype(bf16)


def write_matrix(flat, row, values, blocks):
    depth, width = values.shape
    for j in range(width // LANES):
        flat[pl.ds(row + j, depth, stride=blocks), :] = values[:, j * LANES : (j + 1) * LANES]


def normalize(values):
    center = values - jnp.mean(values, -1, keepdims=True)
    rstd = lax.rsqrt(jnp.mean(center * center, -1, keepdims=True) + eps_norm)
    return center * rstd, rstd


def norm_back(incoming, unit, rstd, gain):
    scaled = incoming * gain
    inner = jnp.mean(scaled * unit, -1, keepdims=True)
    back = rstd * (scaled - jnp.mean(scaled, -1, keepdims=True) - unit * inner)
    gain_grad = jnp.sum(incoming * unit, 0, keepdims=True)
    return back, gain_grad, jnp.sum(incoming, 0, keepdims=True)


def head_mask(head):
    lane = lax.broadcasted_iota(jnp.int32, (1, LANES), 1)
    return lane < HEAD_DIM if head == 0 else lane >= HEAD_DIM


def pair_slices(step):
    image, pair = step // PAIRS, step % PAIRS
    rows = pl.ds(pl.multiple_of(image * ROWS, 16), ROWS)
    cols = [pl.ds(pl.multiple_of(t * D + pair * LANES, LANES), LANES) for t in range(3)]
    return rows, cols


def attention_forward(rows_each, first, *refs):
    place, state, low = refs[:3]
    refs = refs[3:]
    if first:
        kept_state, refs = refs[0], refs[1:]
    w_qkv, w_out, gains, normed_one, qkv, probs, mixed, hidden, flat = refs
    padded = low.shape[1]
    for chunk in range(-(-MLP_ROW // rows_each)):
        flat[chunk * rows_each : chunk * rows_each + padded, :] = low[place[chunk]].astype(f32)
    read_matrix(flat, ROW["w_qkv"], w_qkv, D, 3 * D)
    read_matrix(flat, ROW["w_attn_out"], w_out, D, D)
    gain = read_vector(flat, ROW["ln1_gain"], 3)
    shift = read_vector(flat, ROW["ln1_shift"], 3)
    gains[...] = jnp.broadcast_to(gain, gains.shape)
    if first:
        kept_state[...] = jnp.zeros_like(kept_state)
        for image in range(MICRO):
            kept_state[image * ROWS : image * ROWS + SEQ, :] = state[image].astype(f32)
        x = kept_state[...]
    else:
        x = state[...]
    unit, _ = normalize(x)
    normed_one[...] = (unit * gain + shift).astype(bf16)
    bias_query = read_vector(flat, ROW["bias_query"], 3)
    bias = jnp.concatenate(
        [bias_query, jnp.zeros_like(bias_query), read_vector(flat, ROW["bias_value"], 3)], axis=1
    )
    for t in range(3):
        cols = slice(t * D, (t + 1) * D)
        product = dot_nn(normed_one[...], w_qkv[:, cols]) + bias[:, cols]
        qkv[:, cols] = product.astype(bf16)

    def step(at, carry):
        rows, cols = pair_slices(at)
        query, key_rows, value_rows = qkv[rows, cols[0]], qkv[rows, cols[1]], qkv[rows, cols[2]]
        real = lax.broadcasted_iota(jnp.int32, (ROWS, ROWS), 1) < SEQ
        sides = []
        for head in range(2):
            own_key = jnp.where(head_mask(head), key_rows, jnp.zeros_like(key_rows))
            raw = jnp.where(real, dot_nt(query, own_key), -1e30)
            powers = jnp.exp((raw - jnp.max(raw, -1, keepdims=True)) * HEAD_DIM ** (-0.5))
            weight = powers / jnp.sum(powers, -1, keepdims=True)
            probs[at * 2 + head] = weight
            sides.append(dot_nn(weight.astype(bf16), value_rows))
        mixed[rows, pl.ds(pl.multiple_of((at % PAIRS) * LANES, LANES), LANES)] = jnp.where(
            head_mask(0), sides[0], sides[1]
        ).astype(bf16)
        return carry

    lax.fori_loop(0, MICRO * PAIRS, step, 0)
    hidden[...] = x + dot_nn(mixed[...], w_out[...]) + read_vector(flat, ROW["bias_attn_out"], 3)


def mlp_forward(rows_each, last, *refs):
    place_low, place_high, hidden, low, high = refs[:5]
    w_lift, w_drop, gains, normed_two, active, slope, result, flat = refs[5:]
    padded, count = low.shape[1], low.shape[0]
    begin = MLP_ROW // rows_each
    base = begin * rows_each
    for chunk in range(begin, count):
        at = chunk * rows_each - base
        flat[at : at + padded, :] = low[place_low[chunk]].astype(f32)
    for chunk in range(count):
        at = (count + chunk) * rows_each - base
        flat[at : at + padded, :] = high[place_high[chunk]].astype(f32)
    read_matrix(flat, ROW["w_lift"] - base, w_lift, D, FF)
    read_matrix(flat, ROW["w_drop"] - base, w_drop, FF, D)
    gain = read_vector(flat, ROW["ln2_gain"] - base, 3)
    shift = read_vector(flat, ROW["ln2_shift"] - base, 3)
    gains[...] = jnp.broadcast_to(gain, gains.shape)
    bias_lift = read_vector(flat, ROW["bias_lift"] - base, FF // LANES)
    unit, _ = normalize(hidden[...])
    normed_two[...] = (unit * gain + shift).astype(bf16)
    total = hidden[...] + read_vector(flat, ROW["bias_drop"] - base, 3)
    for at in range(0, FF, BLOCK):
        cols = slice(at, at + BLOCK)
        lifted = dot_nn(normed_two[...], w_lift[:, cols]) + bias_lift[:, cols]
        below = 0.5 * (1.0 + lax.erf(lifted * sqrt_half))
        active[:, cols] = (lifted * below).astype(bf16)
        slope[:, cols] = below + lifted * jnp.exp(-0.5 * lifted * lifted) * inverse_root_tau
        total += dot_nn(active[:, cols], w_drop[cols, :])
    if last:
        for image in range(MICRO):
            result[image] = total[image * ROWS : image * ROWS + SEQ, :]
    else:
        result[...] = total


def pack(flat, base, rows_each, first_chunk, place, out):
    padded, count = out.shape[1], out.shape[0]
    for chunk in range(count):
        at = (first_chunk + chunk) * rows_each - base
        out[place[chunk]] = flat[at : at + padded, :].astype(bf16)


def mlp_backward(rows_each, last, *refs):
    if last:
        present, refs = refs[0], refs[1:]
    place_high, incoming, hidden, w_lift, w_drop, gains, normed_two, active, slope = refs[:9]
    refs = refs[9:]
    carry, high, g_hidden, flat = refs[:4]
    count = high.shape[0]
    if last:
        kept = refs[4]
        kept[...] = jnp.zeros_like(kept)
        for image in range(MICRO):
            seed = incoming[image].astype(f32) * present[image].astype(f32)
            kept[image * ROWS : image * ROWS + SEQ, :] = seed
        g = kept[...]
    else:
        g = incoming[...]
    base = MLP_ROW
    end = ROW["end"] - base
    flat[end:, :] = jnp.zeros((flat.shape[0] - end, LANES), f32)
    g_out = g.astype(bf16)
    write_vector(flat, ROW["bias_drop"] - base, jnp.sum(g_out.astype(f32), 0, keepdims=True))
    d_normed = jnp.zeros((TOKENS, D), f32)
    for at in range(0, FF, BLOCK):
        cols = slice(at, at + BLOCK)
        row = ROW["w_drop"] - base + at * (D // LANES)
        write_matrix(flat, row, dot_tn(active[:, cols], g_out), D // LANES)
        d_lifted = (dot_nt(g_out, w_drop[cols, :]) * slope[:, cols]).astype(bf16)
        row = ROW["bias_lift"] - base + at // LANES
        write_vector(flat, row, jnp.sum(d_lifted.astype(f32), 0, keepdims=True))
        row = ROW["w_lift"] - base + at // LANES
        write_matrix(flat, row, dot_tn(normed_two[...], d_lifted), FF // LANES)
        d_normed += dot_nt(d_lifted, w_lift[:, cols])
    unit, rstd = normalize(hidden[...])
    back, gain_grad, shift_grad = norm_back(d_normed, unit, rstd, gains[0:1, :])
    write_vector(flat, ROW["ln2_gain"] - base, gain_grad)
    write_vector(flat, ROW["ln2_shift"] - base, shift_grad)
    g_hidden[...] = g + back
    carry[...] = flat[: carry.shape[0], :]
    pack(flat, base, rows_each, count, place_high, high)


def attention_backward(rows_each, first, *refs):
    place_low, g_hidden, state, w_qkv, w_out, gains, normed_one, qkv, probs, mixed, carry = refs[:11]
    low, input_grad, flat, d_mixed, d_qkv = refs[11:]
    flat[MLP_ROW : MLP_ROW + carry.shape[0], :] = carry[...]
    g_att = g_hidden[...].astype(bf16)
    write_vector(flat, ROW["bias_attn_out"], jnp.sum(g_att.astype(f32), 0, keepdims=True))
    write_matrix(flat, ROW["w_attn_out"], dot_tn(mixed[...], g_att), D // LANES)
    d_mixed[...] = dot_nt(g_att, w_out[...]).astype(bf16)

    def step(at, carried):
        rows, cols = pair_slices(at)
        query, key_rows, value_rows = qkv[rows, cols[0]], qkv[rows, cols[1]], qkv[rows, cols[2]]
        mixed_grad = d_mixed[rows, pl.ds(pl.multiple_of((at % PAIRS) * LANES, LANES), LANES)]
        d_query, d_key, d_value = [], [], []
        for head in range(2):
            own = jnp.where(head_mask(head), mixed_grad, jnp.zeros_like(mixed_grad))
            weight = probs[at * 2 + head]
            d_value.append(dot_tn(weight.astype(bf16), mixed_grad))
            d_probs = dot_nt(own, value_rows)
            inner = jnp.sum(weight * d_probs, -1, keepdims=True)
            d_scores = (weight * (d_probs - inner)).astype(bf16)
            d_query.append(dot_nn(d_scores, key_rows))
            d_key.append(dot_tn(d_scores, query))
        scale = HEAD_DIM ** (-0.5)
        mask = head_mask(0)
        d_qkv[rows, cols[0]] = (jnp.where(mask, d_query[0], d_query[1]) * scale).astype(bf16)
        d_qkv[rows, cols[1]] = (jnp.where(mask, d_key[0], d_key[1]) * scale).astype(bf16)
        d_qkv[rows, cols[2]] = jnp.where(mask, d_value[0], d_value[1]).astype(bf16)
        return carried

    lax.fori_loop(0, MICRO * PAIRS, step, 0)
    query_sum = jnp.sum(d_qkv[:, :D].astype(f32), 0, keepdims=True)
    write_vector(flat, ROW["bias_query"], query_sum)
    value_sum = jnp.sum(d_qkv[:, 2 * D :].astype(f32), 0, keepdims=True)
    write_vector(flat, ROW["bias_value"], value_sum)
    d_normed = jnp.zeros((TOKENS, D), f32)
    for t in range(3):
        cols = slice(t * D, (t + 1) * D)
        part = d_qkv[:, cols]
        row = ROW["w_qkv"] + t * (D // LANES)
        write_matrix(flat, row, dot_tn(normed_one[...], part), 3 * D // LANES)
        d_normed += dot_nt(part, w_qkv[:, cols])
    unit, rstd = normalize(state[...])
    back, gain_grad, shift_grad = norm_back(d_normed, unit, rstd, gains[0:1, :])
    write_vector(flat, ROW["ln1_gain"], gain_grad)
    write_vector(flat, ROW["ln1_shift"], shift_grad)
    total = g_hidden[...] + back
    if first:
        for image in range(MICRO):
            input_grad[image] = total[image * ROWS : image * ROWS + SEQ, :]
    else:
        input_grad[...] = total
    pack(flat, 0, rows_each, 0, place_low, low)


def call(body, name, inputs, outputs, scratch, scalars=0, flops=0):
    in_specs = [pl.BlockSpec(memory_space=pltpu.SMEM)] * scalars
    in_specs += [pl.BlockSpec(memory_space=pltpu.VMEM)] * (len(inputs) - scalars)
    shapes = [jax.ShapeDtypeStruct(shape, dtype) for shape, dtype in outputs]
    moved = sum(math.prod(s.shape) * s.dtype.itemsize for s in list(inputs) + shapes)
    return pl.pallas_call(
        body,
        name=name,
        out_shape=shapes,
        in_specs=in_specs,
        out_specs=[pl.BlockSpec(memory_space=pltpu.VMEM)] * len(shapes),
        scratch_shapes=scratch,
        compiler_params=pltpu.CompilerParams(vmem_limit_bytes=40 * 1024 * 1024),
        cost_estimate=pl.CostEstimate(flops=flops, bytes_accessed=moved, transcendentals=0),
    )(*inputs)


def xor_permute(values, bit, size):
    return lax.ppermute(values, "dp", [(i, i ^ (1 << bit)) for i in range(size)])


def half_orders(bits):
    top = list(range(bits - 2, 2, -1))
    return (top + [1, 2, 0], top + [2, 1, 0])


def places(me, size, order):
    relative = (me ^ jnp.arange(size // 2, dtype=jnp.int32)) & (size // 2 - 1)
    place = jnp.zeros_like(relative)
    for digit, bit in enumerate(order):
        place = place | (((relative >> bit) & 1) << digit)
    return place


def gather(shard, me, size, bits):
    top = (me >> (bits - 1)) & 1
    other = xor_permute(shard, bits - 1, size)
    halves = [jnp.where(top == 0, shard, other)[None], jnp.where(top == 0, other, shard)[None]]
    orders = half_orders(bits)
    for step in range(bits - 1):
        moved = [xor_permute(halves[h], orders[h][step], size) for h in range(2)]
        halves = [jnp.concatenate([halves[h], moved[h]]) for h in range(2)]
    return halves


def scatter_half(half, order, size):
    for bit in reversed(order):
        middle = half.shape[0] // 2
        received = xor_permute(half[middle:], bit, size)
        half = (half[:middle].astype(f32) + received.astype(f32)).astype(bf16)
    return half[0]


def scatter_top(low, high, me, size, bits):
    top = (me >> (bits - 1)) & 1
    sent = jnp.where(top == 0, high, low)
    kept = jnp.where(top == 0, low, high)
    received = xor_permute(sent, bits - 1, size)
    return kept.astype(f32) + received.astype(f32)


def shards(size, images, cotangent, present, params, first_moment, second_moment):
    bits = size.bit_length() - 1
    width = params.shape[1]
    rows_each = width // LANES
    padded = round_up(rows_each, 16)
    half = size // 2
    me = lax.axis_index("dp")
    orders = half_orders(bits)
    place = [places(me, size, order) for order in orders]

    compact = params.astype(bf16).reshape(2, rows_each, LANES)
    compact = jnp.pad(compact, ((0, 0), (0, padded - rows_each), (0, 0)))
    low, high = [None, None], [None, None]
    for layer in range(2):
        low[layer], high[layer] = gather(compact[layer], me, size, bits)

    low_flat = pltpu.VMEM((-(-MLP_ROW // rows_each) * rows_each + padded, LANES), f32)
    begin = MLP_ROW // rows_each
    high_flat = pltpu.VMEM(((size - begin) * rows_each + padded, LANES), f32)
    square = TOKENS * D * D
    core_flops = 2 * 2 * MICRO * HEADS * ROWS * ROWS * HEAD_DIM

    state = images
    saved = []
    for layer in range(2):
        first = layer == 0
        outputs = [((TOKENS, D), f32)] if first else []
        outputs += [
            ((D, 3 * D), bf16),
            ((D, D), bf16),
            ((8, D), f32),
            ((TOKENS, D), bf16),
            ((TOKENS, 3 * D), bf16),
            ((MICRO * HEADS, ROWS, ROWS), f32),
            ((TOKENS, D), bf16),
            ((TOKENS, D), f32),
        ]
        made = call(
            functools.partial(attention_forward, rows_each, first),
            "attention_forward",
            [place[0], state, low[layer]],
            outputs,
            [low_flat],
            scalars=1,
            flops=8 * square + core_flops,
        )
        if first:
            state, made = made[0], made[1:]
        w_qkv, w_out, gains_one, normed_one, qkv, probs, mixed, hidden = made
        last = layer == 1
        w_lift, w_drop, gains_two, normed_two, active, slope, result = call(
            functools.partial(mlp_forward, rows_each, last),
            "mlp_forward",
            [place[0], place[1], hidden, low[layer], high[layer]],
            [
                ((D, FF), bf16),
                ((FF, D), bf16),
                ((8, D), f32),
                ((TOKENS, D), bf16),
                ((TOKENS, FF), bf16),
                ((TOKENS, FF), f32),
                ((MICRO, SEQ, D) if last else (TOKENS, D), f32),
            ],
            [high_flat],
            scalars=2,
            flops=16 * square,
        )
        one = (state, w_qkv, w_out, gains_one, normed_one, qkv, probs, mixed)
        two = (hidden, w_lift, w_drop, gains_two, normed_two, active, slope)
        saved.append((one, two))
        state = result
    outputs = state

    carry_rows = round_up(half * rows_each - MLP_ROW + padded - rows_each, 8)
    incoming = cotangent
    owned = [None, None]
    for layer in (1, 0):
        first, last = layer == 0, layer == 1
        one, two = saved[layer]
        scratch = [pltpu.VMEM((size * rows_each + padded - MLP_ROW, LANES), f32)]
        if last:
            scratch.append(pltpu.VMEM((TOKENS, D), f32))
        inputs = [present] if last else []
        carry, high_grads, g_hidden = call(
            functools.partial(mlp_backward, rows_each, last),
            "mlp_backward",
            inputs + [place[1], incoming, *two],
            [((carry_rows, LANES), f32), ((half, padded, LANES), bf16), ((TOKENS, D), f32)],
            scratch,
            scalars=2 if last else 1,
            flops=32 * square,
        )
        low_grads, incoming = call(
            functools.partial(attention_backward, rows_each, first),
            "attention_backward",
            [place[0], g_hidden, *one, carry],
            [
                ((half, padded, LANES), bf16),
                ((MICRO, SEQ, D) if first else (TOKENS, D), f32),
            ],
            [
                pltpu.VMEM((MLP_ROW + carry_rows, LANES), f32),
                pltpu.VMEM((TOKENS, D), bf16),
                pltpu.VMEM((TOKENS, 3 * D), bf16),
            ],
            scalars=1,
            flops=16 * square + 2 * core_flops,
        )
        owned_high = scatter_half(high_grads, orders[1], size)
        owned_low = scatter_half(low_grads, orders[0], size)
        total = scatter_top(owned_low, owned_high, me, size, bits)
        owned[layer] = total[:rows_each].reshape(width)

    grads = jnp.stack(owned)
    position = me * width + jnp.arange(width, dtype=jnp.int32)
    flags = matrix_flags(position)[None, :]
    rate = jnp.where(flags, rate_matrix, rate_vector)
    decay = jnp.where(flags, decay_matrix, 0.0)
    new_first = beta_one * first_moment + (1.0 - beta_one) * grads
    new_second = beta_two * second_moment + (1.0 - beta_two) * grads * grads
    first_hat = new_first / (1.0 - beta_one**STEP)
    second_hat = new_second / (1.0 - beta_two**STEP)
    new_params = params - rate * (first_hat / (jnp.sqrt(second_hat) + adam_eps) + decay * params)
    return (outputs, incoming, new_params, new_first, new_second)


def solution(mesh):
    in_specs = (
        P("dp", None, None),
        P("dp", None, None),
        P("dp"),
        P(None, "dp"),
        P(None, "dp"),
        P(None, "dp"),
    )
    out_specs = (
        P("dp", None, None),
        P("dp", None, None),
        P(None, "dp"),
        P(None, "dp"),
        P(None, "dp"),
    )
    body = functools.partial(shards, mesh.shape["dp"])
    return jax.shard_map(body, mesh=mesh, in_specs=in_specs, out_specs=out_specs, check_vma=False)
```

```python
import functools
import math

import jax
import jax.numpy as jnp
from jax import lax
from jax.experimental import pallas as pl
from jax.experimental.pallas import tpu as pltpu
from jax.sharding import PartitionSpec as P

D = 384
FF = 1536
HEADS = 6
HEAD_DIM = 64
SEQ = 197
MICRO = 2
STEP = 10
P_SIZE = 1774080

LANES = 128
ROWS = 208
TOKENS = MICRO * ROWS
PAIRS = HEADS // 2
COST = 1
VMEM_LIMIT = 10 * 1024 * 1024
BLOCK = 512

eps_norm = 1e-06
beta_one = 0.9
beta_two = 0.999
adam_eps = 1e-08
rate_matrix = 0.1
rate_vector = 0.5
decay_matrix = 0.05
sqrt_half = 0.7071067811865476
inverse_root_tau = 0.3989422804014327

f32 = jnp.float32
bf16 = jnp.bfloat16


def layout():
    return [
        ("ln1_gain", (D,)),
        ("ln1_shift", (D,)),
        ("w_qkv", (D, 3 * D)),
        ("bias_query", (D,)),
        ("bias_value", (D,)),
        ("w_attn_out", (D, D)),
        ("bias_attn_out", (D,)),
        ("ln2_gain", (D,)),
        ("ln2_shift", (D,)),
        ("w_lift", (D, FF)),
        ("bias_lift", (FF,)),
        ("w_drop", (FF, D)),
        ("bias_drop", (D,)),
    ]


def row_offsets():
    offsets, at = {}, 0
    for label, shape in layout():
        offsets[label] = at
        at += math.prod(shape) // LANES
    offsets["end"] = at
    return offsets


ROW = row_offsets()
MLP_ROW = ROW["ln2_gain"]


def matrix_flags(position):
    square = D * D
    lifted = D * FF
    bounds = [
        (2 * D, 2 * D + 3 * square),
        (4 * D + 3 * square, 4 * D + 4 * square),
        (7 * D + 4 * square, 7 * D + 4 * square + lifted),
        (7 * D + 4 * square + lifted + FF, 7 * D + 4 * square + 2 * lifted + FF),
    ]
    flags = jnp.zeros(position.shape, dtype=bool)
    for lower, upper in bounds:
        flags = flags | (position >= lower) & (position < upper)
    return flags


def round_up(value, step):
    return (value + step - 1) // step * step


def dot(a, b, dims):
    return lax.dot_general(a, b, ((dims[0], dims[1]), ((), ())), preferred_element_type=f32)


def dot_nn(a, b):
    return dot(a, b, ((1,), (0,)))


def dot_nt(a, b):
    return dot(a, b, ((1,), (1,)))


def dot_tn(a, b):
    return dot(a, b, ((0,), (0,)))


def read_vector(flat, row, count):
    parts = [flat[row + i : row + i + 1, :] for i in range(count)]
    return jnp.concatenate(parts, axis=1)


def write_vector(flat, row, values):
    for i in range(values.shape[1] // LANES):
        flat[row + i : row + i + 1, :] = values[:, i * LANES : (i + 1) * LANES]


def read_matrix(flat, row, out, depth, width):
    blocks = width // LANES
    for j in range(blocks):
        part = flat[pl.ds(row + j, depth, stride=blocks), :]
        out[:, j * LANES : (j + 1) * LANES] = part.astype(bf16)


def write_matrix(flat, row, values, blocks):
    depth, width = values.shape
    for j in range(width // LANES):
        flat[pl.ds(row + j, depth, stride=blocks), :] = values[:, j * LANES : (j + 1) * LANES]


def normalize(values):
    center = values - jnp.mean(values, -1, keepdims=True)
    rstd = lax.rsqrt(jnp.mean(center * center, -1, keepdims=True) + eps_norm)
    return center * rstd, rstd


def norm_back(incoming, unit, rstd, gain):
    scaled = incoming * gain
    inner = jnp.mean(scaled * unit, -1, keepdims=True)
    back = rstd * (scaled - jnp.mean(scaled, -1, keepdims=True) - unit * inner)
    gain_grad = jnp.sum(incoming * unit, 0, keepdims=True)
    return back, gain_grad, jnp.sum(incoming, 0, keepdims=True)


def head_mask(head):
    lane = lax.broadcasted_iota(jnp.int32, (1, LANES), 1)
    return lane < HEAD_DIM if head == 0 else lane >= HEAD_DIM


def pair_slices(step):
    image, pair = step // PAIRS, step % PAIRS
    rows = pl.ds(pl.multiple_of(image * ROWS, 16), ROWS)
    cols = [pl.ds(pl.multiple_of(t * D + pair * LANES, LANES), LANES) for t in range(3)]
    return rows, cols


def unpack(rows_each, base, first_chunk, place, near, far, flat):
    count, padded = near.shape[0], near.shape[1]
    for chunk in range(first_chunk[0], first_chunk[1]):
        at = place[chunk]
        own = lax.rem(at, count)
        rows = jnp.where(at < count, near[own].astype(f32), far[own].astype(f32))
        begin = (first_chunk[2] + chunk) * rows_each - base
        flat[begin : begin + padded, :] = rows


def attention_forward(rows_each, first, place, near, far, state, *refs):
    if first:
        kept_state, refs = refs[0], refs[1:]
    w_qkv, w_out, vectors, normed_one, qkv, probs, mixed, hidden, flat = refs
    unpack(rows_each, 0, (0, -(-MLP_ROW // rows_each), 0), place, near, far, flat)
    read_matrix(flat, ROW["w_qkv"], w_qkv, D, 3 * D)
    read_matrix(flat, ROW["w_attn_out"], w_out, D, D)
    labels = ["ln1_gain", "ln1_shift", "bias_query", "bias_value", "bias_attn_out"]
    for at, label in enumerate(labels):
        vectors[at : at + 1, :] = read_vector(flat, ROW[label], 3)
    gain, shift = vectors[0:1, :], vectors[1:2, :]
    if first:
        kept_state[...] = jnp.zeros_like(kept_state)
        for image in range(MICRO):
            kept_state[image * ROWS : image * ROWS + SEQ, :] = state[image].astype(f32)
        x = kept_state[...]
    else:
        x = state[...]
    unit, _ = normalize(x)
    normed_one[...] = (unit * gain + shift).astype(bf16)
    bias_query = vectors[2:3, :]
    bias = jnp.concatenate([bias_query, jnp.zeros_like(bias_query), vectors[3:4, :]], axis=1)
    for t in range(3):
        cols = slice(t * D, (t + 1) * D)
        product = dot_nn(normed_one[...], w_qkv[:, cols]) + bias[:, cols]
        qkv[:, cols] = product.astype(bf16)

    def step(at, carry):
        rows, cols = pair_slices(at)
        query, key_rows, value_rows = qkv[rows, cols[0]], qkv[rows, cols[1]], qkv[rows, cols[2]]
        real = lax.broadcasted_iota(jnp.int32, (ROWS, ROWS), 1) < SEQ
        sides = []
        for head in range(2):
            own_key = jnp.where(head_mask(head), key_rows, jnp.zeros_like(key_rows))
            raw = jnp.where(real, dot_nt(query, own_key), -1e30)
            powers = jnp.exp((raw - jnp.max(raw, -1, keepdims=True)) * HEAD_DIM ** (-0.5))
            weight = powers / jnp.sum(powers, -1, keepdims=True)
            weight = weight.astype(bf16)
            probs[at * 2 + head] = weight
            sides.append(dot_nn(weight, value_rows))
        mixed[rows, pl.ds(pl.multiple_of((at % PAIRS) * LANES, LANES), LANES)] = jnp.where(
            head_mask(0), sides[0], sides[1]
        ).astype(bf16)
        return carry

    lax.fori_loop(0, MICRO * PAIRS, step, 0)
    hidden[...] = x + dot_nn(mixed[...], w_out[...]) + vectors[4:5, :]


def mlp_forward(rows_each, last, place_low, place_high, low_near, low_far, near, far, hidden, *refs):
    w_lift, w_drop, vectors, normed_two, active, slope, result, flat = refs
    count = 2 * near.shape[0]
    begin = MLP_ROW // rows_each
    base = begin * rows_each
    unpack(rows_each, base, (begin, count, 0), place_low, low_near, low_far, flat)
    unpack(rows_each, base, (0, count, count), place_high, near, far, flat)
    read_matrix(flat, ROW["w_lift"] - base, w_lift, D, FF)
    read_matrix(flat, ROW["w_drop"] - base, w_drop, FF, D)
    for at, label in enumerate(["ln2_gain", "ln2_shift", "bias_drop"]):
        vectors[at : at + 1, :] = read_vector(flat, ROW[label] - base, 3)
    bias_lift = read_vector(flat, ROW["bias_lift"] - base, FF // LANES)
    gain, shift = vectors[0:1, :], vectors[1:2, :]
    unit, _ = normalize(hidden[...])
    normed_two[...] = (unit * gain + shift).astype(bf16)
    total = hidden[...] + vectors[2:3, :]
    for at in range(0, FF, BLOCK):
        cols = slice(at, at + BLOCK)
        lifted = dot_nn(normed_two[...], w_lift[:, cols]) + bias_lift[:, cols]
        below = 0.5 * (1.0 + lax.erf(lifted * sqrt_half))
        active[:, cols] = (lifted * below).astype(bf16)
        bell = jnp.exp(-0.5 * lifted * lifted) * inverse_root_tau
        slope[:, cols] = (below + lifted * bell).astype(bf16)
        total += dot_nn(active[:, cols], w_drop[cols, :])
    if last:
        for image in range(MICRO):
            result[image] = total[image * ROWS : image * ROWS + SEQ, :]
    else:
        result[...] = total


def pack(flat, base, rows_each, first_chunk, places, near, far):
    count, padded = near.shape[1], near.shape[2]
    even = places[0][0] < count
    for parity in range(2):

        @pl.when(even if parity == 0 else jnp.logical_not(even))
        def _():
            for quarter, place in enumerate(places):
                for chunk in range(2 * count):
                    at = (first_chunk + quarter * 2 * count + chunk) * rows_each - base
                    out = near if chunk % 2 == parity else far
                    out[quarter, lax.rem(place[chunk], count)] = flat[at : at + padded, :].astype(bf16)


def mlp_backward(rows_each, last, *refs):
    if last:
        present, refs = refs[0], refs[1:]
    places, refs = refs[:2], refs[2:]
    incoming, hidden, w_lift, w_drop, vectors, normed_two, active, slope = refs[:8]
    refs = refs[8:]
    carry, near, far, g_hidden, flat = refs[:5]
    count = 4 * near.shape[1]
    if last:
        kept = refs[5]
        kept[...] = jnp.zeros_like(kept)
        for image in range(MICRO):
            seed = incoming[image].astype(f32) * present[image].astype(f32)
            kept[image * ROWS : image * ROWS + SEQ, :] = seed
        g = kept[...]
    else:
        g = incoming[...]
    base = MLP_ROW
    end = ROW["end"] - base
    flat[end:, :] = jnp.zeros((flat.shape[0] - end, LANES), f32)
    g_out = g.astype(bf16)
    write_vector(flat, ROW["bias_drop"] - base, jnp.sum(g_out.astype(f32), 0, keepdims=True))
    d_normed = jnp.zeros((TOKENS, D), f32)
    for at in range(0, FF, BLOCK):
        cols = slice(at, at + BLOCK)
        row = ROW["w_drop"] - base + at * (D // LANES)
        write_matrix(flat, row, dot_tn(active[:, cols], g_out), D // LANES)
        d_lifted = (dot_nt(g_out, w_drop[cols, :]) * slope[:, cols].astype(f32)).astype(bf16)
        row = ROW["bias_lift"] - base + at // LANES
        write_vector(flat, row, jnp.sum(d_lifted.astype(f32), 0, keepdims=True))
        row = ROW["w_lift"] - base + at // LANES
        write_matrix(flat, row, dot_tn(normed_two[...], d_lifted), FF // LANES)
        d_normed += dot_nt(d_lifted, w_lift[:, cols])
    unit, rstd = normalize(hidden[...])
    back, gain_grad, shift_grad = norm_back(d_normed, unit, rstd, vectors[0:1, :])
    write_vector(flat, ROW["ln2_gain"] - base, gain_grad)
    write_vector(flat, ROW["ln2_shift"] - base, shift_grad)
    g_hidden[...] = g + back
    carry[...] = flat[: carry.shape[0], :]
    pack(flat, base, rows_each, count, places, near, far)


def attention_backward(g_hidden, w_out, qkv, probs, mixed, d_qkv, d_out, bias_out, d_mixed):
    g_att = g_hidden[...].astype(bf16)
    bias_out[...] = jnp.broadcast_to(jnp.sum(g_att.astype(f32), 0, keepdims=True), bias_out.shape)
    d_out[...] = dot_tn(mixed[...], g_att)
    d_mixed[...] = dot_nt(g_att, w_out[...]).astype(bf16)

    def step(at, carried):
        rows, cols = pair_slices(at)
        query, key_rows, value_rows = qkv[rows, cols[0]], qkv[rows, cols[1]], qkv[rows, cols[2]]
        mixed_grad = d_mixed[rows, pl.ds(pl.multiple_of((at % PAIRS) * LANES, LANES), LANES)]
        d_query, d_key, d_value = [], [], []
        for head in range(2):
            own = jnp.where(head_mask(head), mixed_grad, jnp.zeros_like(mixed_grad))
            weight = probs[at * 2 + head]
            d_value.append(dot_tn(weight, mixed_grad))
            weight = weight.astype(f32)
            d_probs = dot_nt(own, value_rows)
            inner = jnp.sum(weight * d_probs, -1, keepdims=True)
            d_scores = (weight * (d_probs - inner)).astype(bf16)
            d_query.append(dot_nn(d_scores, key_rows))
            d_key.append(dot_tn(d_scores, query))
        scale = HEAD_DIM ** (-0.5)
        mask = head_mask(0)
        d_qkv[rows, cols[0]] = (jnp.where(mask, d_query[0], d_query[1]) * scale).astype(bf16)
        d_qkv[rows, cols[1]] = (jnp.where(mask, d_key[0], d_key[1]) * scale).astype(bf16)
        d_qkv[rows, cols[2]] = jnp.where(mask, d_value[0], d_value[1]).astype(bf16)
        return carried

    lax.fori_loop(0, MICRO * PAIRS, step, 0)

def projection_backward(rows_each, first, *refs):
    places, refs = refs[:2], refs[2:]
    g_hidden, state, w_qkv, vectors, normed_one, d_qkv, d_out, bias_out, carry = refs[:9]
    near, far, input_grad, flat = refs[9:]
    flat[MLP_ROW : MLP_ROW + carry.shape[0], :] = carry[...]
    write_vector(flat, ROW["bias_attn_out"], bias_out[0:1, :])
    write_matrix(flat, ROW["w_attn_out"], d_out[...], D // LANES)
    query_sum = jnp.sum(d_qkv[:, :D].astype(f32), 0, keepdims=True)
    write_vector(flat, ROW["bias_query"], query_sum)
    value_sum = jnp.sum(d_qkv[:, 2 * D :].astype(f32), 0, keepdims=True)
    write_vector(flat, ROW["bias_value"], value_sum)
    d_normed = jnp.zeros((TOKENS, D), f32)
    for t in range(3):
        cols = slice(t * D, (t + 1) * D)
        part = d_qkv[:, cols]
        row = ROW["w_qkv"] + t * (D // LANES)
        write_matrix(flat, row, dot_tn(normed_one[...], part), 3 * D // LANES)
        d_normed += dot_nt(part, w_qkv[:, cols])
    unit, rstd = normalize(state[...])
    back, gain_grad, shift_grad = norm_back(d_normed, unit, rstd, vectors[0:1, :])
    write_vector(flat, ROW["ln1_gain"], gain_grad)
    write_vector(flat, ROW["ln1_shift"], shift_grad)
    total = g_hidden[...] + back
    if first:
        for image in range(MICRO):
            input_grad[image] = total[image * ROWS : image * ROWS + SEQ, :]
    else:
        input_grad[...] = total
    pack(flat, 0, rows_each, 0, places, near, far)


def call(body, name, inputs, outputs, scratch, scalars=0, flops=0):
    in_specs = [pl.BlockSpec(memory_space=pltpu.SMEM)] * scalars
    in_specs += [pl.BlockSpec(memory_space=pltpu.VMEM)] * (len(inputs) - scalars)
    shapes = [jax.ShapeDtypeStruct(shape, dtype) for shape, dtype in outputs]
    moved = sum(math.prod(s.shape) * s.dtype.itemsize for s in list(inputs) + shapes)
    return pl.pallas_call(
        body,
        name=name,
        out_shape=shapes,
        in_specs=in_specs,
        out_specs=[pl.BlockSpec(memory_space=pltpu.VMEM)] * len(shapes),
        scratch_shapes=scratch,
        compiler_params=pltpu.CompilerParams(vmem_limit_bytes=VMEM_LIMIT),
        cost_estimate=pl.CostEstimate(flops=flops // COST, bytes_accessed=moved // COST, transcendentals=0),
    )(*inputs)


def tie(values, *before):
    return lax.optimization_barrier((values, before))[0]


def together(*values):
    return lax.optimization_barrier(values)


def swap(values, size, mask):
    return lax.ppermute(values, "dp", [(i, i ^ mask) for i in range(size)])


def gather_masks(bits):
    chain = [1 << bit for bit in range(bits - 2, 2, -1)]
    return [chain + [2, 4, 1], chain + [4, 2, 1]]


def places(me, size, masks):
    relative = me ^ jnp.arange(size // 2, dtype=jnp.int32)
    place = jnp.zeros_like(relative)
    for digit, mask in enumerate(masks):
        place = place | jnp.where(relative & mask != 0, 1 << digit, 0)
    return place


def sent(part, size, mask):
    middle = part.shape[0] // 2
    return part[:middle], swap(part[middle:], size, mask)


def added(pair):
    return (pair[0].astype(f32) + pair[1].astype(f32)).astype(bf16)


def shards(size, images, cotangent, present, params, first_moment, second_moment):
    bits = size.bit_length() - 1
    width = params.shape[1]
    rows_each = width // LANES
    padded = round_up(rows_each, 16)
    half = size // 2
    me = lax.axis_index("dp")
    chain = [1 << bit for bit in range(bits - 2, 2, -1)]
    planes = [(2, 4), (4, 2)]
    place_low, place_high = [places(me, size, chain + [mask, 6 - mask, 1]) for mask in planes[0]]
    place = [places(me, size // 2, chain[1:] + [mask, 6 - mask, 1]) for mask in planes[0]]

    is_low, is_first = (me >> (bits - 1)) & 1 == 0, (me >> (bits - 2)) & 1 == 0
    flags = matrix_flags(me * width + jnp.arange(width, dtype=jnp.int32)).astype(f32)
    early = together(params, is_low, is_first, flags, place_low, place_high, *place)
    params, is_low, is_first, flags, place_low, place_high, *place = early
    compact = params.astype(bf16).reshape(2, rows_each, LANES)
    compact = jnp.pad(compact, ((0, 0), (0, padded - rows_each), (0, 0)))

    low_flat = pltpu.VMEM((-(-MLP_ROW // rows_each) * rows_each + padded, LANES), f32)
    begin = MLP_ROW // rows_each
    high_flat = pltpu.VMEM(((size - begin) * rows_each + padded, LANES), f32)
    square = TOKENS * D * D
    core_flops = 2 * 2 * MICRO * HEADS * ROWS * ROWS * HEAD_DIM

    def attend(first, near, far, state):
        outputs = [((TOKENS, D), f32)] if first else []
        outputs += [
            ((D, 3 * D), bf16),
            ((D, D), bf16),
            ((8, D), f32),
            ((TOKENS, D), bf16),
            ((TOKENS, 3 * D), bf16),
            ((MICRO * HEADS, ROWS, ROWS), bf16),
            ((TOKENS, D), bf16),
            ((TOKENS, D), f32),
        ]
        made = call(
            functools.partial(attention_forward, rows_each, first),
            "attention_forward",
            [place_low, near, far, state],
            outputs,
            [low_flat],
            scalars=1,
            flops=8 * square + core_flops,
        )
        made = made if first else [state, *made]
        return made[:-1], made[-1]

    def lift(last, low_near, low_far, near, far, hidden):
        made = call(
            functools.partial(mlp_forward, rows_each, last),
            "mlp_forward",
            [place_low, place_high, low_near, low_far, near, far, hidden],
            [
                ((D, FF), bf16),
                ((FF, D), bf16),
                ((8, D), f32),
                ((TOKENS, D), bf16),
                ((TOKENS, FF), bf16),
                ((TOKENS, FF), bf16),
                ((MICRO, SEQ, D) if last else (TOKENS, D), f32),
            ],
            [high_flat],
            scalars=2,
            flops=16 * square,
        )
        return (hidden, *made[:-1]), made[-1]

    grads_shape = ((2, size // 8, padded, LANES), bf16)

    def lift_back(last, incoming, kept):
        scratch = [pltpu.VMEM((size * rows_each + padded - MLP_ROW, LANES), f32)]
        if last:
            scratch.append(pltpu.VMEM((TOKENS, D), f32))
        return call(
            functools.partial(mlp_backward, rows_each, last),
            "mlp_backward",
            ([present] if last else []) + [*place, incoming, *kept],
            [((carry_rows, LANES), f32), grads_shape, grads_shape, ((TOKENS, D), f32)],
            scratch,
            scalars=3 if last else 2,
            flops=32 * square,
        )

    def attend_back(g_hidden, kept):
        state, w_qkv, w_out, vectors, normed_one, qkv, probs, mixed = kept
        return call(
            attention_backward,
            "attention_backward",
            [g_hidden, w_out, qkv, probs, mixed],
            [((TOKENS, 3 * D), bf16), ((D, D), f32), ((8, D), f32)],
            [pltpu.VMEM((TOKENS, D), bf16)],
            flops=4 * square + 2 * core_flops,
        )

    def project_back(first, g_hidden, kept, *made):
        state, w_qkv, w_out, vectors, normed_one, qkv, probs, mixed = kept
        return call(
            functools.partial(projection_backward, rows_each, first),
            "projection_backward",
            [*place, g_hidden, state, w_qkv, vectors, normed_one, *made],
            [grads_shape, grads_shape, ((MICRO, SEQ, D) if first else (TOKENS, D), f32)],
            [pltpu.VMEM((MLP_ROW + carry_rows, LANES), f32)],
            scalars=2,
            flops=12 * square,
        )

    def top_gathered(shard, other):
        return jnp.stack([jnp.where(is_low, shard, other), jnp.where(is_low, other, shard)])[None]

    def moved(parts, step):
        return [swap(part, size, mask) for part, mask in zip(parts, planes[step])]

    def joined(parts, received):
        return [jnp.concatenate(pair) for pair in zip(parts, received)]

    def chained(chunks):
        for mask in chain[:-1]:
            chunks = jnp.concatenate([chunks, swap(chunks, size, mask)])
        return chunks, swap(chunks, size, chain[-1])

    def halved(chunks, received):
        chunks = jnp.concatenate([chunks, received])
        return chunks[:, 0], chunks[:, 1]

    top0 = top_gathered(compact[0], swap(compact[0], size, size // 2))
    half0 = halved(*chained(top0))
    received0 = moved(half0, 0)
    row1, *received0 = together(compact[1], *received0)
    half0 = joined(half0, received0)
    received0 = moved(half0, 1)
    chunks1, received1 = chained(top_gathered(row1, swap(row1, size, size // 2)))
    *received0, received1 = together(*received0, received1)
    near0 = joined(half0, received0)
    half1 = halved(chunks1, received1)
    far0 = [swap(part, size, 1) for part in near0]
    received1 = moved(half1, 0)
    *far0, received1[0], received1[1] = together(*far0, *received1)
    half1 = joined(half1, received1)
    received1 = moved(half1, 1)
    one0, hidden = attend(True, near0[0], far0[0], images)
    hidden, *received1 = together(hidden, *received1)
    near1 = joined(half1, received1)
    far1 = [swap(part, size, 1) for part in near1]
    two0, state = lift(False, near0[0], far0[0], near0[1], far0[1], hidden)
    state, *far1 = together(state, *far1)
    one1, hidden = attend(False, near1[0], far1[0], state)
    two1, outputs = lift(True, near1[0], far1[0], near1[1], far1[1], hidden)

    carry_rows = round_up(half * rows_each - MLP_ROW + padded - rows_each, 8)

    def to_plane(pairs, step):
        return [sent(added(pair), size, mask) for pair, mask in zip(pairs, planes[step])]

    def to_core(near, far):
        received = swap(far, size, 1)
        return [(near[quarter], received[quarter]) for quarter in range(2)]

    def along(pairs):
        parts = [added(pair) for pair in pairs]
        for mask in reversed(chain[1:]):
            parts = [added(sent(part, size, mask)) for part in parts]
        return parts

    def hold(pairs, *others):
        values = together(*[value for pair in pairs for value in pair], *others)
        count = 2 * len(pairs)
        return [values[i : i + 2] for i in range(0, count, 2)], *values[count:]

    def to_inner(low, high):
        kept = jnp.concatenate([jnp.where(is_first, *part) for part in (low, high)])
        given = jnp.concatenate([jnp.where(is_first, *part[::-1]) for part in (low, high)])
        return kept, swap(given, size, size // 4)

    def to_top(halves):
        kept = jnp.where(is_low, halves[0], halves[1])
        return kept, swap(jnp.where(is_low, halves[1], halves[0]), size, size // 2)

    carry, near, far, g_hidden = lift_back(True, cotangent, two1)
    high1 = to_core(near, far)
    made = attend_back(g_hidden, one1)
    high1, *made = hold(high1, *made)
    near, far, incoming = project_back(False, g_hidden, one1, *made, carry)
    high1 = to_plane(high1, 1)
    low1 = to_core(near, far)
    carry, near, far, g_hidden = lift_back(False, incoming, two0)
    held, g_hidden = hold(high1 + low1, g_hidden)
    high1, low1 = to_plane(held[:2], 0), to_plane(held[2:], 1)
    high0 = to_core(near, far)
    made = attend_back(g_hidden, one0)
    held, *made = hold(high1 + low1 + high0, *made)
    high1, low1, high0 = along(held[:2]), to_plane(held[2:4], 0), to_plane(held[4:], 1)
    near, far, input_grad = project_back(True, g_hidden, one0, *made, carry)
    low0 = to_core(near, far)
    held, = hold(low0 + low1 + high0)
    low0, low1, high0 = to_plane(held[:2], 1), along(held[2:4]), to_plane(held[4:], 0)
    inner1 = to_inner(low1, high1)
    held, = hold(low0 + high0 + [inner1])
    low0, high0, inner1 = to_plane(held[:2], 0), along(held[2:4]), added(held[4])
    top1 = to_top(inner1)
    held, = hold(low0 + [top1])
    low0, top1 = along(held[:2]), held[2]
    top0 = to_top(added(to_inner(low0, high0)))
    sum0, sum1 = [pair[0].astype(f32) + pair[1].astype(f32) for pair in (top0, top1)]
    owned = [total[:rows_each].reshape(width) for total in (sum0, sum1)]

    grads = jnp.stack(owned)
    flags = flags[None, :] > 0
    rate = jnp.where(flags, rate_matrix, rate_vector)
    decay = jnp.where(flags, decay_matrix, 0.0)
    new_first = beta_one * first_moment + (1.0 - beta_one) * grads
    new_second = beta_two * second_moment + (1.0 - beta_two) * grads * grads
    first_hat = new_first / (1.0 - beta_one**STEP)
    second_hat = new_second / (1.0 - beta_two**STEP)
    new_params = params - rate * (first_hat / (jnp.sqrt(second_hat) + adam_eps) + decay * params)
    return (outputs, input_grad, new_params, new_first, new_second)


def solution(mesh):
    in_specs = (
        P("dp", None, None),
        P("dp", None, None),
        P("dp"),
        P(None, "dp"),
        P(None, "dp"),
        P(None, "dp"),
    )
    out_specs = (
        P("dp", None, None),
        P("dp", None, None),
        P(None, "dp"),
        P(None, "dp"),
        P(None, "dp"),
    )
    body = functools.partial(shards, mesh.shape["dp"])
    return jax.shard_map(body, mesh=mesh, in_specs=in_specs, out_specs=out_specs, check_vma=False)
```

```python
import functools
import math

import jax
import jax.numpy as jnp
from jax import lax
from jax.experimental import pallas as pl
from jax.experimental.pallas import tpu as pltpu
from jax.sharding import PartitionSpec as P

D = 384
FF = 1536
HEADS = 6
HEAD_DIM = 64
SEQ = 197
MICRO = 2
STEP = 10
P_SIZE = 1774080

LANES = 128
ROWS = 208
TOKENS = MICRO * ROWS
PAIRS = HEADS // 2
COST = 1
UNROLL = 6
VMEM_LIMIT = 10 * 1024 * 1024
BLOCK = 512

eps_norm = 1e-06
beta_one = 0.9
beta_two = 0.999
adam_eps = 1e-08
rate_matrix = 0.1
rate_vector = 0.5
decay_matrix = 0.05
sqrt_half = 0.7071067811865476
inverse_root_tau = 0.3989422804014327

f32 = jnp.float32
bf16 = jnp.bfloat16


def layout():
    return [
        ("ln1_gain", (D,)),
        ("ln1_shift", (D,)),
        ("w_qkv", (D, 3 * D)),
        ("bias_query", (D,)),
        ("bias_value", (D,)),
        ("w_attn_out", (D, D)),
        ("bias_attn_out", (D,)),
        ("ln2_gain", (D,)),
        ("ln2_shift", (D,)),
        ("w_lift", (D, FF)),
        ("bias_lift", (FF,)),
        ("w_drop", (FF, D)),
        ("bias_drop", (D,)),
    ]


def row_offsets():
    offsets, at = {}, 0
    for label, shape in layout():
        offsets[label] = at
        at += math.prod(shape) // LANES
    offsets["end"] = at
    return offsets


ROW = row_offsets()
MLP_ROW = ROW["ln2_gain"]


def matrix_flags(position):
    square = D * D
    lifted = D * FF
    bounds = [
        (2 * D, 2 * D + 3 * square),
        (4 * D + 3 * square, 4 * D + 4 * square),
        (7 * D + 4 * square, 7 * D + 4 * square + lifted),
        (7 * D + 4 * square + lifted + FF, 7 * D + 4 * square + 2 * lifted + FF),
    ]
    flags = jnp.zeros(position.shape, dtype=bool)
    for lower, upper in bounds:
        flags = flags | (position >= lower) & (position < upper)
    return flags


def round_up(value, step):
    return (value + step - 1) // step * step


def dot(a, b, dims):
    return lax.dot_general(a, b, ((dims[0], dims[1]), ((), ())), preferred_element_type=f32)


def dot_nn(a, b):
    return dot(a, b, ((1,), (0,)))


def dot_nt(a, b):
    return dot(a, b, ((1,), (1,)))


def dot_tn(a, b):
    return dot(a, b, ((0,), (0,)))


def read_vector(flat, row, count):
    parts = [flat[row + i : row + i + 1, :] for i in range(count)]
    return jnp.concatenate(parts, axis=1)


def write_vector(flat, row, values):
    for i in range(values.shape[1] // LANES):
        flat[row + i : row + i + 1, :] = values[:, i * LANES : (i + 1) * LANES]


def read_matrix(flat, row, out, depth, width):
    blocks = width // LANES
    for j in range(blocks):
        part = flat[pl.ds(row + j, depth, stride=blocks), :]
        out[:, j * LANES : (j + 1) * LANES] = part.astype(bf16)


def write_matrix(flat, row, values, blocks):
    depth, width = values.shape
    for j in range(width // LANES):
        flat[pl.ds(row + j, depth, stride=blocks), :] = values[:, j * LANES : (j + 1) * LANES]


def normalize(values):
    center = values - jnp.mean(values, -1, keepdims=True)
    rstd = lax.rsqrt(jnp.mean(center * center, -1, keepdims=True) + eps_norm)
    return center * rstd, rstd


def norm_back(incoming, unit, rstd, gain):
    scaled = incoming * gain
    inner = jnp.mean(scaled * unit, -1, keepdims=True)
    back = rstd * (scaled - jnp.mean(scaled, -1, keepdims=True) - unit * inner)
    gain_grad = jnp.sum(incoming * unit, 0, keepdims=True)
    return back, gain_grad, jnp.sum(incoming, 0, keepdims=True)


def head_mask(head):
    lane = lax.broadcasted_iota(jnp.int32, (1, LANES), 1)
    return lane < HEAD_DIM if head == 0 else lane >= HEAD_DIM


def pair_slices(step):
    image, pair = step // PAIRS, step % PAIRS
    rows = pl.ds(pl.multiple_of(image * ROWS, 16), ROWS)
    cols = [pl.ds(pl.multiple_of(t * D + pair * LANES, LANES), LANES) for t in range(3)]
    return rows, cols


def unpack(rows_each, base, first_chunk, place, near, far, flat):
    count, padded = near.shape[0], near.shape[1]
    for chunk in range(first_chunk[0], first_chunk[1]):
        at = place[chunk]
        own = lax.rem(at, count)
        rows = jnp.where(at < count, near[own].astype(f32), far[own].astype(f32))
        begin = (first_chunk[2] + chunk) * rows_each - base
        flat[begin : begin + padded, :] = rows


def attention_forward(rows_each, first, place, near, far, state, *refs):
    if first:
        kept_state, refs = refs[0], refs[1:]
    w_qkv, w_out, vectors, normed_one, qkv, probs, mixed, hidden, flat = refs
    unpack(rows_each, 0, (0, -(-MLP_ROW // rows_each), 0), place, near, far, flat)
    read_matrix(flat, ROW["w_qkv"], w_qkv, D, 3 * D)
    read_matrix(flat, ROW["w_attn_out"], w_out, D, D)
    labels = ["ln1_gain", "ln1_shift", "bias_query", "bias_value", "bias_attn_out"]
    for at, label in enumerate(labels):
        vectors[at : at + 1, :] = read_vector(flat, ROW[label], 3)
    gain, shift = vectors[0:1, :], vectors[1:2, :]
    if first:
        kept_state[...] = jnp.zeros_like(kept_state)
        for image in range(MICRO):
            kept_state[image * ROWS : image * ROWS + SEQ, :] = state[image].astype(f32)
        x = kept_state[...]
    else:
        x = state[...]
    unit, _ = normalize(x)
    normed_one[...] = (unit * gain + shift).astype(bf16)
    bias_query = vectors[2:3, :]
    bias = jnp.concatenate([bias_query, jnp.zeros_like(bias_query), vectors[3:4, :]], axis=1)
    for t in range(3):
        cols = slice(t * D, (t + 1) * D)
        product = dot_nn(normed_one[...], w_qkv[:, cols]) + bias[:, cols]
        qkv[:, cols] = product.astype(bf16)

    def step(at, carry):
        rows, cols = pair_slices(at)
        query, key_rows, value_rows = qkv[rows, cols[0]], qkv[rows, cols[1]], qkv[rows, cols[2]]
        real = lax.broadcasted_iota(jnp.int32, (ROWS, ROWS), 1) < SEQ
        sides = []
        for head in range(2):
            own_key = jnp.where(head_mask(head), key_rows, jnp.zeros_like(key_rows))
            raw = jnp.where(real, dot_nt(query, own_key), -1e30)
            powers = jnp.exp((raw - jnp.max(raw, -1, keepdims=True)) * HEAD_DIM ** (-0.5))
            weight = powers / jnp.sum(powers, -1, keepdims=True)
            weight = weight.astype(bf16)
            probs[at * 2 + head] = weight
            sides.append(dot_nn(weight, value_rows))
        mixed[rows, pl.ds(pl.multiple_of((at % PAIRS) * LANES, LANES), LANES)] = jnp.where(
            head_mask(0), sides[0], sides[1]
        ).astype(bf16)
        return carry

    lax.fori_loop(0, MICRO * PAIRS, step, 0, unroll=UNROLL)
    hidden[...] = x + dot_nn(mixed[...], w_out[...]) + vectors[4:5, :]


def mlp_forward(rows_each, last, place_low, place_high, low_near, low_far, near, far, hidden, *refs):
    w_lift, w_drop, vectors, normed_two, active, slope, result, flat = refs
    count = 2 * near.shape[0]
    begin = MLP_ROW // rows_each
    base = begin * rows_each
    unpack(rows_each, base, (begin, count, 0), place_low, low_near, low_far, flat)
    unpack(rows_each, base, (0, count, count), place_high, near, far, flat)
    read_matrix(flat, ROW["w_lift"] - base, w_lift, D, FF)
    read_matrix(flat, ROW["w_drop"] - base, w_drop, FF, D)
    for at, label in enumerate(["ln2_gain", "ln2_shift", "bias_drop"]):
        vectors[at : at + 1, :] = read_vector(flat, ROW[label] - base, 3)
    bias_lift = read_vector(flat, ROW["bias_lift"] - base, FF // LANES)
    gain, shift = vectors[0:1, :], vectors[1:2, :]
    unit, _ = normalize(hidden[...])
    normed_two[...] = (unit * gain + shift).astype(bf16)
    total = hidden[...] + vectors[2:3, :]
    for at in range(0, FF, BLOCK):
        cols = slice(at, at + BLOCK)
        lifted = dot_nn(normed_two[...], w_lift[:, cols]) + bias_lift[:, cols]
        below = 0.5 * (1.0 + lax.erf(lifted * sqrt_half))
        active[:, cols] = (lifted * below).astype(bf16)
        bell = jnp.exp(-0.5 * lifted * lifted) * inverse_root_tau
        slope[:, cols] = (below + lifted * bell).astype(bf16)
        total += dot_nn(active[:, cols], w_drop[cols, :])
    if last:
        for image in range(MICRO):
            result[image] = total[image * ROWS : image * ROWS + SEQ, :]
    else:
        result[...] = total


def pack(flat, base, rows_each, first_chunk, places, near, far):
    count, padded = near.shape[1], near.shape[2]
    even = places[0][0] < count
    for parity in range(2):

        @pl.when(even if parity == 0 else jnp.logical_not(even))
        def _():
            for quarter, place in enumerate(places):
                for chunk in range(2 * count):
                    at = (first_chunk + quarter * 2 * count + chunk) * rows_each - base
                    out = near if chunk % 2 == parity else far
                    out[quarter, lax.rem(place[chunk], count)] = flat[at : at + padded, :].astype(bf16)


def mlp_backward(rows_each, last, *refs):
    if last:
        present, refs = refs[0], refs[1:]
    places, refs = refs[:2], refs[2:]
    incoming, hidden, w_lift, w_drop, vectors, normed_two, active, slope = refs[:8]
    refs = refs[8:]
    carry, near, far, g_hidden, flat = refs[:5]
    count = 4 * near.shape[1]
    if last:
        kept = refs[5]
        kept[...] = jnp.zeros_like(kept)
        for image in range(MICRO):
            seed = incoming[image].astype(f32) * present[image].astype(f32)
            kept[image * ROWS : image * ROWS + SEQ, :] = seed
        g = kept[...]
    else:
        g = incoming[...]
    base = MLP_ROW
    end = ROW["end"] - base
    flat[end:, :] = jnp.zeros((flat.shape[0] - end, LANES), f32)
    g_out = g.astype(bf16)
    write_vector(flat, ROW["bias_drop"] - base, jnp.sum(g_out.astype(f32), 0, keepdims=True))
    d_normed = jnp.zeros((TOKENS, D), f32)
    for at in range(0, FF, BLOCK):
        cols = slice(at, at + BLOCK)
        row = ROW["w_drop"] - base + at * (D // LANES)
        write_matrix(flat, row, dot_tn(active[:, cols], g_out), D // LANES)
        d_lifted = (dot_nt(g_out, w_drop[cols, :]) * slope[:, cols].astype(f32)).astype(bf16)
        row = ROW["bias_lift"] - base + at // LANES
        write_vector(flat, row, jnp.sum(d_lifted.astype(f32), 0, keepdims=True))
        row = ROW["w_lift"] - base + at // LANES
        write_matrix(flat, row, dot_tn(normed_two[...], d_lifted), FF // LANES)
        d_normed += dot_nt(d_lifted, w_lift[:, cols])
    unit, rstd = normalize(hidden[...])
    back, gain_grad, shift_grad = norm_back(d_normed, unit, rstd, vectors[0:1, :])
    write_vector(flat, ROW["ln2_gain"] - base, gain_grad)
    write_vector(flat, ROW["ln2_shift"] - base, shift_grad)
    g_hidden[...] = g + back
    carry[...] = flat[: carry.shape[0], :]
    pack(flat, base, rows_each, count, places, near, far)


def attention_backward(g_hidden, w_out, qkv, probs, mixed, d_qkv, d_out, bias_out, d_mixed):
    g_att = g_hidden[...].astype(bf16)
    bias_out[...] = jnp.broadcast_to(jnp.sum(g_att.astype(f32), 0, keepdims=True), bias_out.shape)
    d_out[...] = dot_tn(mixed[...], g_att)
    d_mixed[...] = dot_nt(g_att, w_out[...]).astype(bf16)

    def step(at, carried):
        rows, cols = pair_slices(at)
        query, key_rows, value_rows = qkv[rows, cols[0]], qkv[rows, cols[1]], qkv[rows, cols[2]]
        mixed_grad = d_mixed[rows, pl.ds(pl.multiple_of((at % PAIRS) * LANES, LANES), LANES)]
        d_query, d_key, d_value = [], [], []
        for head in range(2):
            own = jnp.where(head_mask(head), mixed_grad, jnp.zeros_like(mixed_grad))
            weight = probs[at * 2 + head]
            d_value.append(dot_tn(weight, mixed_grad))
            weight = weight.astype(f32)
            d_probs = dot_nt(own, value_rows)
            inner = jnp.sum(weight * d_probs, -1, keepdims=True)
            d_scores = (weight * (d_probs - inner)).astype(bf16)
            d_query.append(dot_nn(d_scores, key_rows))
            d_key.append(dot_tn(d_scores, query))
        scale = HEAD_DIM ** (-0.5)
        mask = head_mask(0)
        d_qkv[rows, cols[0]] = (jnp.where(mask, d_query[0], d_query[1]) * scale).astype(bf16)
        d_qkv[rows, cols[1]] = (jnp.where(mask, d_key[0], d_key[1]) * scale).astype(bf16)
        d_qkv[rows, cols[2]] = jnp.where(mask, d_value[0], d_value[1]).astype(bf16)
        return carried

    lax.fori_loop(0, MICRO * PAIRS, step, 0, unroll=UNROLL)

def projection_backward(rows_each, first, *refs):
    places, refs = refs[:2], refs[2:]
    g_hidden, state, w_qkv, vectors, normed_one, d_qkv, d_out, bias_out, carry = refs[:9]
    near, far, input_grad, flat = refs[9:]
    flat[MLP_ROW : MLP_ROW + carry.shape[0], :] = carry[...]
    write_vector(flat, ROW["bias_attn_out"], bias_out[0:1, :])
    write_matrix(flat, ROW["w_attn_out"], d_out[...], D // LANES)
    query_sum = jnp.sum(d_qkv[:, :D].astype(f32), 0, keepdims=True)
    write_vector(flat, ROW["bias_query"], query_sum)
    value_sum = jnp.sum(d_qkv[:, 2 * D :].astype(f32), 0, keepdims=True)
    write_vector(flat, ROW["bias_value"], value_sum)
    d_normed = jnp.zeros((TOKENS, D), f32)
    for t in range(3):
        cols = slice(t * D, (t + 1) * D)
        part = d_qkv[:, cols]
        row = ROW["w_qkv"] + t * (D // LANES)
        write_matrix(flat, row, dot_tn(normed_one[...], part), 3 * D // LANES)
        d_normed += dot_nt(part, w_qkv[:, cols])
    unit, rstd = normalize(state[...])
    back, gain_grad, shift_grad = norm_back(d_normed, unit, rstd, vectors[0:1, :])
    write_vector(flat, ROW["ln1_gain"], gain_grad)
    write_vector(flat, ROW["ln1_shift"], shift_grad)
    total = g_hidden[...] + back
    if first:
        for image in range(MICRO):
            input_grad[image] = total[image * ROWS : image * ROWS + SEQ, :]
    else:
        input_grad[...] = total
    pack(flat, 0, rows_each, 0, places, near, far)


def call(body, name, inputs, outputs, scratch, scalars=0, flops=0):
    in_specs = [pl.BlockSpec(memory_space=pltpu.SMEM)] * scalars
    in_specs += [pl.BlockSpec(memory_space=pltpu.VMEM)] * (len(inputs) - scalars)
    shapes = [jax.ShapeDtypeStruct(shape, dtype) for shape, dtype in outputs]
    moved = sum(math.prod(s.shape) * s.dtype.itemsize for s in list(inputs) + shapes)
    return pl.pallas_call(
        body,
        name=name,
        out_shape=shapes,
        in_specs=in_specs,
        out_specs=[pl.BlockSpec(memory_space=pltpu.VMEM)] * len(shapes),
        scratch_shapes=scratch,
        compiler_params=pltpu.CompilerParams(vmem_limit_bytes=VMEM_LIMIT),
        cost_estimate=pl.CostEstimate(flops=flops // COST, bytes_accessed=moved // COST, transcendentals=0),
    )(*inputs)


def tie(values, *before):
    return lax.optimization_barrier((values, before))[0]


def together(*values):
    return lax.optimization_barrier(values)


def swap(values, size, mask):
    return lax.ppermute(values, "dp", [(i, i ^ mask) for i in range(size)])


def gather_masks(bits):
    chain = [1 << bit for bit in range(bits - 2, 2, -1)]
    return [chain + [2, 4, 1], chain + [4, 2, 1]]


def places(me, size, masks):
    relative = me ^ jnp.arange(size // 2, dtype=jnp.int32)
    place = jnp.zeros_like(relative)
    for digit, mask in enumerate(masks):
        place = place | jnp.where(relative & mask != 0, 1 << digit, 0)
    return place


def sent(part, size, mask):
    middle = part.shape[0] // 2
    return part[:middle], swap(part[middle:], size, mask)


def added(pair):
    return (pair[0].astype(f32) + pair[1].astype(f32)).astype(bf16)


def shards(size, images, cotangent, present, params, first_moment, second_moment):
    bits = size.bit_length() - 1
    width = params.shape[1]
    rows_each = width // LANES
    padded = round_up(rows_each, 16)
    half = size // 2
    me = lax.axis_index("dp")
    chain = [1 << bit for bit in range(bits - 2, 2, -1)]
    planes = [(2, 4), (4, 2)]
    place_low, place_high = [places(me, size, chain + [mask, 6 - mask, 1]) for mask in planes[0]]
    place = [places(me, size // 2, chain[1:] + [mask, 6 - mask, 1]) for mask in planes[0]]

    is_low, is_first = (me >> (bits - 1)) & 1 == 0, (me >> (bits - 2)) & 1 == 0
    flags = matrix_flags(me * width + jnp.arange(width, dtype=jnp.int32)).astype(f32)
    early = together(params, is_low, is_first, flags, place_low, place_high, *place)
    params, is_low, is_first, flags, place_low, place_high, *place = early
    compact = params.astype(bf16).reshape(2, rows_each, LANES)
    compact = jnp.pad(compact, ((0, 0), (0, padded - rows_each), (0, 0)))

    low_flat = pltpu.VMEM((-(-MLP_ROW // rows_each) * rows_each + padded, LANES), f32)
    begin = MLP_ROW // rows_each
    high_flat = pltpu.VMEM(((size - begin) * rows_each + padded, LANES), f32)
    square = TOKENS * D * D
    core_flops = 2 * 2 * MICRO * HEADS * ROWS * ROWS * HEAD_DIM

    def attend(first, near, far, state):
        outputs = [((TOKENS, D), f32)] if first else []
        outputs += [
            ((D, 3 * D), bf16),
            ((D, D), bf16),
            ((8, D), f32),
            ((TOKENS, D), bf16),
            ((TOKENS, 3 * D), bf16),
            ((MICRO * HEADS, ROWS, ROWS), bf16),
            ((TOKENS, D), bf16),
            ((TOKENS, D), f32),
        ]
        made = call(
            functools.partial(attention_forward, rows_each, first),
            "attention_forward",
            [place_low, near, far, state],
            outputs,
            [low_flat],
            scalars=1,
            flops=8 * square + core_flops,
        )
        made = made if first else [state, *made]
        return made[:-1], made[-1]

    def lift(last, low_near, low_far, near, far, hidden):
        made = call(
            functools.partial(mlp_forward, rows_each, last),
            "mlp_forward",
            [place_low, place_high, low_near, low_far, near, far, hidden],
            [
                ((D, FF), bf16),
                ((FF, D), bf16),
                ((8, D), f32),
                ((TOKENS, D), bf16),
                ((TOKENS, FF), bf16),
                ((TOKENS, FF), bf16),
                ((MICRO, SEQ, D) if last else (TOKENS, D), f32),
            ],
            [high_flat],
            scalars=2,
            flops=16 * square,
        )
        return (hidden, *made[:-1]), made[-1]

    grads_shape = ((2, size // 8, padded, LANES), bf16)

    def lift_back(last, incoming, kept):
        scratch = [pltpu.VMEM((size * rows_each + padded - MLP_ROW, LANES), f32)]
        if last:
            scratch.append(pltpu.VMEM((TOKENS, D), f32))
        return call(
            functools.partial(mlp_backward, rows_each, last),
            "mlp_backward",
            ([present] if last else []) + [*place, incoming, *kept],
            [((carry_rows, LANES), f32), grads_shape, grads_shape, ((TOKENS, D), f32)],
            scratch,
            scalars=3 if last else 2,
            flops=32 * square,
        )

    def attend_back(g_hidden, kept):
        state, w_qkv, w_out, vectors, normed_one, qkv, probs, mixed = kept
        return call(
            attention_backward,
            "attention_backward",
            [g_hidden, w_out, qkv, probs, mixed],
            [((TOKENS, 3 * D), bf16), ((D, D), f32), ((8, D), f32)],
            [pltpu.VMEM((TOKENS, D), bf16)],
            flops=4 * square + 2 * core_flops,
        )

    def project_back(first, g_hidden, kept, *made):
        state, w_qkv, w_out, vectors, normed_one, qkv, probs, mixed = kept
        return call(
            functools.partial(projection_backward, rows_each, first),
            "projection_backward",
            [*place, g_hidden, state, w_qkv, vectors, normed_one, *made],
            [grads_shape, grads_shape, ((MICRO, SEQ, D) if first else (TOKENS, D), f32)],
            [pltpu.VMEM((MLP_ROW + carry_rows, LANES), f32)],
            scalars=2,
            flops=12 * square,
        )

    def top_gathered(shard, other):
        return jnp.stack([jnp.where(is_low, shard, other), jnp.where(is_low, other, shard)])[None]

    def moved(parts, step):
        return [swap(part, size, mask) for part, mask in zip(parts, planes[step])]

    def joined(parts, received):
        return [jnp.concatenate(pair) for pair in zip(parts, received)]

    def chained(chunks):
        for mask in chain[:-1]:
            chunks = jnp.concatenate([chunks, swap(chunks, size, mask)])
        return chunks, swap(chunks, size, chain[-1])

    def halved(chunks, received):
        chunks = jnp.concatenate([chunks, received])
        return chunks[:, 0], chunks[:, 1]

    other0 = swap(compact[0], size, size // 2)
    row1, other0 = together(compact[1], other0)
    other1 = swap(row1, size, size // 2)
    half0 = halved(*chained(top_gathered(compact[0], other0)))
    received0 = moved(half0, 0)
    *received0, other1 = together(*received0, other1)
    half0 = joined(half0, received0)
    received0 = moved(half0, 1)
    half1 = halved(*chained(top_gathered(row1, other1)))
    received1 = moved(half1, 0)
    *received0, received1[0], received1[1] = together(*received0, *received1)
    near0 = joined(half0, received0)
    far0 = [swap(part, size, 1) for part in near0]
    half1 = joined(half1, received1)
    received1 = moved(half1, 1)
    one0, hidden = attend(True, near0[0], far0[0], images)
    hidden, *received1 = together(hidden, *received1)
    near1 = joined(half1, received1)
    far1 = [swap(part, size, 1) for part in near1]
    two0, state = lift(False, near0[0], far0[0], near0[1], far0[1], hidden)
    state, *far1 = together(state, *far1)
    one1, hidden = attend(False, near1[0], far1[0], state)
    two1, outputs = lift(True, near1[0], far1[0], near1[1], far1[1], hidden)

    carry_rows = round_up(half * rows_each - MLP_ROW + padded - rows_each, 8)

    def to_plane(pairs, step):
        return [sent(added(pair), size, mask) for pair, mask in zip(pairs, planes[step])]

    def to_core(near, far):
        received = swap(far, size, 1)
        return [(near[quarter], received[quarter]) for quarter in range(2)]

    def along(pairs):
        parts = [added(pair) for pair in pairs]
        for mask in reversed(chain[1:]):
            parts = [added(sent(part, size, mask)) for part in parts]
        return parts

    def hold(pairs, *others):
        values = together(*[value for pair in pairs for value in pair], *others)
        count = 2 * len(pairs)
        return [values[i : i + 2] for i in range(0, count, 2)], *values[count:]

    def to_inner(low, high):
        kept = jnp.concatenate([jnp.where(is_first, *part) for part in (low, high)])
        given = jnp.concatenate([jnp.where(is_first, *part[::-1]) for part in (low, high)])
        return kept, swap(given, size, size // 4)

    def to_top(halves):
        kept = jnp.where(is_low, halves[0], halves[1])
        return kept, swap(jnp.where(is_low, halves[1], halves[0]), size, size // 2)

    carry, near, far, g_hidden = lift_back(True, cotangent, two1)
    high1 = to_core(near, far)
    made = attend_back(g_hidden, one1)
    high1, *made = hold(high1, *made)
    near, far, incoming = project_back(False, g_hidden, one1, *made, carry)
    high1 = to_plane(high1, 1)
    low1 = to_core(near, far)
    carry, near, far, g_hidden = lift_back(False, incoming, two0)
    held, g_hidden = hold(high1 + low1, g_hidden)
    high1, low1 = to_plane(held[:2], 0), to_plane(held[2:], 1)
    high0 = to_core(near, far)
    made = attend_back(g_hidden, one0)
    held, *made = hold(high1 + low1 + high0, *made)
    high1, low1, high0 = along(held[:2]), to_plane(held[2:4], 0), to_plane(held[4:], 1)
    near, far, input_grad = project_back(True, g_hidden, one0, *made, carry)
    low1, near, far = hold(low1, near, far)
    low0 = to_core(near, far)
    high0 = to_plane(high0, 0)
    inner1 = to_inner(along(low1), high1)
    low0, = hold(low0)
    low0 = to_plane(low0, 1)
    held, = hold(low0 + high0 + [inner1])
    low0, high0, top1 = to_plane(held[:2], 0), along(held[2:4]), to_top(added(held[4]))
    held, *high0 = hold(low0, *high0)
    inner0 = to_inner(along(held), high0)
    held, outputs, input_grad = hold([inner0, top1], outputs, input_grad)
    inner0, top1 = held
    top0 = to_top(added(inner0))
    sum0, sum1 = [pair[0].astype(f32) + pair[1].astype(f32) for pair in (top0, top1)]
    owned = [total[:rows_each].reshape(width) for total in (sum0, sum1)]

    grads = jnp.stack(owned)
    flags = flags[None, :] > 0
    rate = jnp.where(flags, rate_matrix, rate_vector)
    decay = jnp.where(flags, decay_matrix, 0.0)
    new_first = beta_one * first_moment + (1.0 - beta_one) * grads
    new_second = beta_two * second_moment + (1.0 - beta_two) * grads * grads
    first_hat = new_first / (1.0 - beta_one**STEP)
    second_hat = new_second / (1.0 - beta_two**STEP)
    new_params = params - rate * (first_hat / (jnp.sqrt(second_hat) + adam_eps) + decay * params)
    return (outputs, input_grad, new_params, new_first, new_second)


def solution(mesh):
    in_specs = (
        P("dp", None, None),
        P("dp", None, None),
        P("dp"),
        P(None, "dp"),
        P(None, "dp"),
        P(None, "dp"),
    )
    out_specs = (
        P("dp", None, None),
        P("dp", None, None),
        P(None, "dp"),
        P(None, "dp"),
        P(None, "dp"),
    )
    body = functools.partial(shards, mesh.shape["dp"])
    return jax.shard_map(body, mesh=mesh, in_specs=in_specs, out_specs=out_specs, check_vma=False)
```

```python
import functools
import math

import jax
import jax.numpy as jnp
from jax import lax
from jax.experimental import pallas as pl
from jax.experimental.pallas import tpu as pltpu
from jax.sharding import PartitionSpec as P

D = 384
FF = 1536
HEADS = 6
HEAD_DIM = 64
SEQ = 197
MICRO = 2
STEP = 10
P_SIZE = 1774080

LANES = 128
ROWS = 208
TOKENS = MICRO * ROWS
PAIRS = HEADS // 2
COST = 1
FORWARD_UNROLL = 6
BACKWARD_UNROLL = 2
VMEM_LIMIT = 10 * 1024 * 1024
BLOCK = 512

eps_norm = 1e-06
beta_one = 0.9
beta_two = 0.999
adam_eps = 1e-08
rate_matrix = 0.1
rate_vector = 0.5
decay_matrix = 0.05
sqrt_half = 0.7071067811865476
inverse_root_tau = 0.3989422804014327

f32 = jnp.float32
bf16 = jnp.bfloat16


def layout():
    return [
        ("ln1_gain", (D,)),
        ("ln1_shift", (D,)),
        ("w_qkv", (D, 3 * D)),
        ("bias_query", (D,)),
        ("bias_value", (D,)),
        ("w_attn_out", (D, D)),
        ("bias_attn_out", (D,)),
        ("ln2_gain", (D,)),
        ("ln2_shift", (D,)),
        ("w_lift", (D, FF)),
        ("bias_lift", (FF,)),
        ("w_drop", (FF, D)),
        ("bias_drop", (D,)),
    ]


def row_offsets():
    offsets, at = {}, 0
    for label, shape in layout():
        offsets[label] = at
        at += math.prod(shape) // LANES
    offsets["end"] = at
    return offsets


ROW = row_offsets()
MLP_ROW = ROW["ln2_gain"]


def matrix_flags(position):
    square = D * D
    lifted = D * FF
    bounds = [
        (2 * D, 2 * D + 3 * square),
        (4 * D + 3 * square, 4 * D + 4 * square),
        (7 * D + 4 * square, 7 * D + 4 * square + lifted),
        (7 * D + 4 * square + lifted + FF, 7 * D + 4 * square + 2 * lifted + FF),
    ]
    flags = jnp.zeros(position.shape, dtype=bool)
    for lower, upper in bounds:
        flags = flags | (position >= lower) & (position < upper)
    return flags


def round_up(value, step):
    return (value + step - 1) // step * step


def dot(a, b, dims):
    return lax.dot_general(a, b, ((dims[0], dims[1]), ((), ())), preferred_element_type=f32)


def dot_nn(a, b):
    return dot(a, b, ((1,), (0,)))


def dot_nt(a, b):
    return dot(a, b, ((1,), (1,)))


def dot_tn(a, b):
    return dot(a, b, ((0,), (0,)))


def read_vector(flat, row, count):
    parts = [flat[row + i : row + i + 1, :] for i in range(count)]
    return jnp.concatenate(parts, axis=1)


def write_vector(flat, row, values):
    for i in range(values.shape[1] // LANES):
        flat[row + i : row + i + 1, :] = values[:, i * LANES : (i + 1) * LANES]


def read_matrix(flat, row, out, depth, width):
    blocks = width // LANES
    for j in range(blocks):
        part = flat[pl.ds(row + j, depth, stride=blocks), :]
        out[:, j * LANES : (j + 1) * LANES] = part.astype(bf16)


def write_matrix(flat, row, values, blocks):
    depth, width = values.shape
    for j in range(width // LANES):
        flat[pl.ds(row + j, depth, stride=blocks), :] = values[:, j * LANES : (j + 1) * LANES]


def normalize(values):
    center = values - jnp.mean(values, -1, keepdims=True)
    rstd = lax.rsqrt(jnp.mean(center * center, -1, keepdims=True) + eps_norm)
    return center * rstd, rstd


def norm_back(incoming, unit, rstd, gain):
    scaled = incoming * gain
    inner = jnp.mean(scaled * unit, -1, keepdims=True)
    back = rstd * (scaled - jnp.mean(scaled, -1, keepdims=True) - unit * inner)
    gain_grad = jnp.sum(incoming * unit, 0, keepdims=True)
    return back, gain_grad, jnp.sum(incoming, 0, keepdims=True)


def head_mask(head):
    lane = lax.broadcasted_iota(jnp.int32, (1, LANES), 1)
    return lane < HEAD_DIM if head == 0 else lane >= HEAD_DIM


def pair_slices(step):
    image, pair = step // PAIRS, step % PAIRS
    rows = pl.ds(pl.multiple_of(image * ROWS, 16), ROWS)
    cols = [pl.ds(pl.multiple_of(t * D + pair * LANES, LANES), LANES) for t in range(3)]
    return rows, cols


def unpack(rows_each, base, chunks, place, near, far, flat):
    count, padded = near.shape[0], near.shape[1]

    def step(chunk, carry):
        at = place[chunk]
        own = lax.rem(at, count)
        rows = jnp.where(at < count, near[own].astype(f32), far[own].astype(f32))
        flat[pl.ds((chunks[2] + chunk) * rows_each - base, padded), :] = rows
        return carry

    lax.fori_loop(chunks[0], chunks[1], step, 0)


def attention_forward(rows_each, first, place, near, far, state, *refs):
    if first:
        kept_state, refs = refs[0], refs[1:]
    w_qkv, w_out, vectors, normed_one, qkv, probs, mixed, hidden, flat = refs
    unpack(rows_each, 0, (0, -(-MLP_ROW // rows_each), 0), place, near, far, flat)
    read_matrix(flat, ROW["w_qkv"], w_qkv, D, 3 * D)
    read_matrix(flat, ROW["w_attn_out"], w_out, D, D)
    labels = ["ln1_gain", "ln1_shift", "bias_query", "bias_value", "bias_attn_out"]
    for at, label in enumerate(labels):
        vectors[at : at + 1, :] = read_vector(flat, ROW[label], 3)
    gain, shift = vectors[0:1, :], vectors[1:2, :]
    if first:
        kept_state[...] = jnp.zeros_like(kept_state)
        for image in range(MICRO):
            kept_state[image * ROWS : image * ROWS + SEQ, :] = state[image].astype(f32)
        x = kept_state[...]
    else:
        x = state[...]
    unit, _ = normalize(x)
    normed_one[...] = (unit * gain + shift).astype(bf16)
    bias_query = vectors[2:3, :]
    bias = jnp.concatenate([bias_query, jnp.zeros_like(bias_query), vectors[3:4, :]], axis=1)
    for t in range(3):
        cols = slice(t * D, (t + 1) * D)
        product = dot_nn(normed_one[...], w_qkv[:, cols]) + bias[:, cols]
        qkv[:, cols] = product.astype(bf16)

    def step(at, carry):
        rows, cols = pair_slices(at)
        query, key_rows, value_rows = qkv[rows, cols[0]], qkv[rows, cols[1]], qkv[rows, cols[2]]
        real = lax.broadcasted_iota(jnp.int32, (ROWS, ROWS), 1) < SEQ
        sides = []
        for head in range(2):
            own_key = jnp.where(head_mask(head), key_rows, jnp.zeros_like(key_rows))
            raw = jnp.where(real, dot_nt(query, own_key), -1e30)
            powers = jnp.exp((raw - jnp.max(raw, -1, keepdims=True)) * HEAD_DIM ** (-0.5))
            weight = powers / jnp.sum(powers, -1, keepdims=True)
            weight = weight.astype(bf16)
            probs[at * 2 + head] = weight
            sides.append(dot_nn(weight, value_rows))
        mixed[rows, pl.ds(pl.multiple_of((at % PAIRS) * LANES, LANES), LANES)] = jnp.where(
            head_mask(0), sides[0], sides[1]
        ).astype(bf16)
        return carry

    lax.fori_loop(0, MICRO * PAIRS, step, 0, unroll=FORWARD_UNROLL)
    hidden[...] = x + dot_nn(mixed[...], w_out[...]) + vectors[4:5, :]


def mlp_forward(rows_each, last, place_low, place_high, low_near, low_far, near, far, hidden, *refs):
    w_lift, w_drop, vectors, normed_two, active, slope, result, flat = refs
    count = 2 * near.shape[0]
    begin = MLP_ROW // rows_each
    base = begin * rows_each
    unpack(rows_each, base, (begin, count, 0), place_low, low_near, low_far, flat)
    unpack(rows_each, base, (0, count, count), place_high, near, far, flat)
    read_matrix(flat, ROW["w_lift"] - base, w_lift, D, FF)
    read_matrix(flat, ROW["w_drop"] - base, w_drop, FF, D)
    for at, label in enumerate(["ln2_gain", "ln2_shift", "bias_drop"]):
        vectors[at : at + 1, :] = read_vector(flat, ROW[label] - base, 3)
    bias_lift = read_vector(flat, ROW["bias_lift"] - base, FF // LANES)
    gain, shift = vectors[0:1, :], vectors[1:2, :]
    unit, _ = normalize(hidden[...])
    normed_two[...] = (unit * gain + shift).astype(bf16)
    total = hidden[...] + vectors[2:3, :]
    for at in range(0, FF, BLOCK):
        cols = slice(at, at + BLOCK)
        lifted = dot_nn(normed_two[...], w_lift[:, cols]) + bias_lift[:, cols]
        below = 0.5 * (1.0 + lax.erf(lifted * sqrt_half))
        active[:, cols] = (lifted * below).astype(bf16)
        bell = jnp.exp(-0.5 * lifted * lifted) * inverse_root_tau
        slope[:, cols] = (below + lifted * bell).astype(bf16)
        total += dot_nn(active[:, cols], w_drop[cols, :])
    if last:
        for image in range(MICRO):
            result[image] = total[image * ROWS : image * ROWS + SEQ, :]
    else:
        result[...] = total


def pack(flat, base, rows_each, first_chunk, places, near, far):
    count, padded = near.shape[1], near.shape[2]
    for quarter, place in enumerate(places):

        def step(chunk, carry):
            at = (first_chunk + quarter * 2 * count + chunk) * rows_each - base
            index = lax.rem(place[chunk], count)

            @pl.when(place[chunk] < count)
            def _():
                near[quarter, index] = flat[pl.ds(at, padded), :].astype(bf16)

            @pl.when(place[chunk] >= count)
            def _():
                far[quarter, index] = flat[pl.ds(at, padded), :].astype(bf16)

            return carry

        lax.fori_loop(0, 2 * count, step, 0)


def mlp_backward(rows_each, last, *refs):
    if last:
        present, refs = refs[0], refs[1:]
    places, refs = refs[:2], refs[2:]
    incoming, hidden, w_lift, w_drop, vectors, normed_two, active, slope = refs[:8]
    refs = refs[8:]
    carry, near, far, g_hidden, flat = refs[:5]
    count = 4 * near.shape[1]
    if last:
        kept = refs[5]
        kept[...] = jnp.zeros_like(kept)
        for image in range(MICRO):
            seed = incoming[image].astype(f32) * present[image].astype(f32)
            kept[image * ROWS : image * ROWS + SEQ, :] = seed
        g = kept[...]
    else:
        g = incoming[...]
    base = MLP_ROW
    end = ROW["end"] - base
    flat[end:, :] = jnp.zeros((flat.shape[0] - end, LANES), f32)
    g_out = g.astype(bf16)
    write_vector(flat, ROW["bias_drop"] - base, jnp.sum(g_out.astype(f32), 0, keepdims=True))
    d_normed = jnp.zeros((TOKENS, D), f32)
    for at in range(0, FF, BLOCK):
        cols = slice(at, at + BLOCK)
        row = ROW["w_drop"] - base + at * (D // LANES)
        write_matrix(flat, row, dot_tn(active[:, cols], g_out), D // LANES)
        d_lifted = (dot_nt(g_out, w_drop[cols, :]) * slope[:, cols].astype(f32)).astype(bf16)
        row = ROW["bias_lift"] - base + at // LANES
        write_vector(flat, row, jnp.sum(d_lifted.astype(f32), 0, keepdims=True))
        row = ROW["w_lift"] - base + at // LANES
        write_matrix(flat, row, dot_tn(normed_two[...], d_lifted), FF // LANES)
        d_normed += dot_nt(d_lifted, w_lift[:, cols])
    unit, rstd = normalize(hidden[...])
    back, gain_grad, shift_grad = norm_back(d_normed, unit, rstd, vectors[0:1, :])
    write_vector(flat, ROW["ln2_gain"] - base, gain_grad)
    write_vector(flat, ROW["ln2_shift"] - base, shift_grad)
    g_hidden[...] = g + back
    carry[...] = flat[: carry.shape[0], :]
    pack(flat, base, rows_each, count, places, near, far)


def attention_backward(g_hidden, w_out, qkv, probs, mixed, d_qkv, d_out, bias_out, d_mixed):
    g_att = g_hidden[...].astype(bf16)
    bias_out[...] = jnp.broadcast_to(jnp.sum(g_att.astype(f32), 0, keepdims=True), bias_out.shape)
    d_out[...] = dot_tn(mixed[...], g_att)
    d_mixed[...] = dot_nt(g_att, w_out[...]).astype(bf16)

    def step(at, carried):
        rows, cols = pair_slices(at)
        query, key_rows, value_rows = qkv[rows, cols[0]], qkv[rows, cols[1]], qkv[rows, cols[2]]
        mixed_grad = d_mixed[rows, pl.ds(pl.multiple_of((at % PAIRS) * LANES, LANES), LANES)]
        d_query, d_key, d_value = [], [], []
        for head in range(2):
            own = jnp.where(head_mask(head), mixed_grad, jnp.zeros_like(mixed_grad))
            weight = probs[at * 2 + head]
            d_value.append(dot_tn(weight, mixed_grad))
            weight = weight.astype(f32)
            d_probs = dot_nt(own, value_rows)
            inner = jnp.sum(weight * d_probs, -1, keepdims=True)
            d_scores = (weight * (d_probs - inner)).astype(bf16)
            d_query.append(dot_nn(d_scores, key_rows))
            d_key.append(dot_tn(d_scores, query))
        scale = HEAD_DIM ** (-0.5)
        mask = head_mask(0)
        d_qkv[rows, cols[0]] = (jnp.where(mask, d_query[0], d_query[1]) * scale).astype(bf16)
        d_qkv[rows, cols[1]] = (jnp.where(mask, d_key[0], d_key[1]) * scale).astype(bf16)
        d_qkv[rows, cols[2]] = jnp.where(mask, d_value[0], d_value[1]).astype(bf16)
        return carried

    lax.fori_loop(0, MICRO * PAIRS, step, 0, unroll=BACKWARD_UNROLL)

def projection_backward(rows_each, first, *refs):
    places, refs = refs[:2], refs[2:]
    g_hidden, state, w_qkv, vectors, normed_one, d_qkv, d_out, bias_out, carry = refs[:9]
    near, far, input_grad, flat = refs[9:]
    flat[MLP_ROW : MLP_ROW + carry.shape[0], :] = carry[...]
    write_vector(flat, ROW["bias_attn_out"], bias_out[0:1, :])
    write_matrix(flat, ROW["w_attn_out"], d_out[...], D // LANES)
    query_sum = jnp.sum(d_qkv[:, :D].astype(f32), 0, keepdims=True)
    write_vector(flat, ROW["bias_query"], query_sum)
    value_sum = jnp.sum(d_qkv[:, 2 * D :].astype(f32), 0, keepdims=True)
    write_vector(flat, ROW["bias_value"], value_sum)
    d_normed = jnp.zeros((TOKENS, D), f32)
    for t in range(3):
        cols = slice(t * D, (t + 1) * D)
        part = d_qkv[:, cols]
        row = ROW["w_qkv"] + t * (D // LANES)
        write_matrix(flat, row, dot_tn(normed_one[...], part), 3 * D // LANES)
        d_normed += dot_nt(part, w_qkv[:, cols])
    unit, rstd = normalize(state[...])
    back, gain_grad, shift_grad = norm_back(d_normed, unit, rstd, vectors[0:1, :])
    write_vector(flat, ROW["ln1_gain"], gain_grad)
    write_vector(flat, ROW["ln1_shift"], shift_grad)
    total = g_hidden[...] + back
    if first:
        for image in range(MICRO):
            input_grad[image] = total[image * ROWS : image * ROWS + SEQ, :]
    else:
        input_grad[...] = total
    pack(flat, 0, rows_each, 0, places, near, far)


def call(body, name, inputs, outputs, scratch, scalars=0, flops=0):
    in_specs = [pl.BlockSpec(memory_space=pltpu.SMEM)] * scalars
    in_specs += [pl.BlockSpec(memory_space=pltpu.VMEM)] * (len(inputs) - scalars)
    shapes = [jax.ShapeDtypeStruct(shape, dtype) for shape, dtype in outputs]
    moved = sum(math.prod(s.shape) * s.dtype.itemsize for s in list(inputs) + shapes)
    return pl.pallas_call(
        body,
        name=name,
        out_shape=shapes,
        in_specs=in_specs,
        out_specs=[pl.BlockSpec(memory_space=pltpu.VMEM)] * len(shapes),
        scratch_shapes=scratch,
        compiler_params=pltpu.CompilerParams(vmem_limit_bytes=VMEM_LIMIT),
        cost_estimate=pl.CostEstimate(flops=flops // COST, bytes_accessed=moved // COST, transcendentals=0),
    )(*inputs)


def tie(values, *before):
    return lax.optimization_barrier((values, before))[0]


def together(*values):
    return lax.optimization_barrier(values)


def swap(values, size, mask):
    return lax.ppermute(values, "dp", [(i, i ^ mask) for i in range(size)])


def gather_masks(bits):
    chain = [1 << bit for bit in range(bits - 2, 2, -1)]
    return [chain + [2, 4, 1], chain + [4, 2, 1]]


def places(me, size, masks):
    relative = me ^ jnp.arange(size // 2, dtype=jnp.int32)
    place = jnp.zeros_like(relative)
    for digit, mask in enumerate(masks):
        place = place | jnp.where(relative & mask != 0, 1 << digit, 0)
    return place


def sent(part, size, mask):
    middle = part.shape[0] // 2
    return part[:middle], swap(part[middle:], size, mask)


def added(pair):
    return (pair[0].astype(f32) + pair[1].astype(f32)).astype(bf16)


def shards(size, images, cotangent, present, params, first_moment, second_moment):
    bits = size.bit_length() - 1
    width = params.shape[1]
    rows_each = width // LANES
    padded = round_up(rows_each, 16)
    half = size // 2
    me = lax.axis_index("dp")
    chain = [1 << bit for bit in range(bits - 2, 2, -1)]
    planes = [(2, 4), (4, 2)]
    place_low, place_high = [places(me, size, chain + [mask, 6 - mask, 1]) for mask in planes[0]]
    place = [places(me, size // 2, chain[1:] + [mask, 6 - mask, 1]) for mask in planes[0]]

    is_low, is_first = (me >> (bits - 1)) & 1 == 0, (me >> (bits - 2)) & 1 == 0
    flags = matrix_flags(me * width + jnp.arange(width, dtype=jnp.int32)).astype(f32)
    early = together(params, is_low, is_first, flags, place_low, place_high, *place)
    params, is_low, is_first, flags, place_low, place_high, *place = early
    compact = params.astype(bf16).reshape(2, rows_each, LANES)
    compact = jnp.pad(compact, ((0, 0), (0, padded - rows_each), (0, 0)))

    low_flat = pltpu.VMEM((-(-MLP_ROW // rows_each) * rows_each + padded, LANES), f32)
    begin = MLP_ROW // rows_each
    high_flat = pltpu.VMEM(((size - begin) * rows_each + padded, LANES), f32)
    square = TOKENS * D * D
    core_flops = 2 * 2 * MICRO * HEADS * ROWS * ROWS * HEAD_DIM

    def attend(first, near, far, state):
        outputs = [((TOKENS, D), f32)] if first else []
        outputs += [
            ((D, 3 * D), bf16),
            ((D, D), bf16),
            ((8, D), f32),
            ((TOKENS, D), bf16),
            ((TOKENS, 3 * D), bf16),
            ((MICRO * HEADS, ROWS, ROWS), bf16),
            ((TOKENS, D), bf16),
            ((TOKENS, D), f32),
        ]
        made = call(
            functools.partial(attention_forward, rows_each, first),
            "attention_forward",
            [place_low, near, far, state],
            outputs,
            [low_flat],
            scalars=1,
            flops=8 * square + core_flops,
        )
        made = made if first else [state, *made]
        return made[:-1], made[-1]

    def lift(last, low_near, low_far, near, far, hidden):
        made = call(
            functools.partial(mlp_forward, rows_each, last),
            "mlp_forward",
            [place_low, place_high, low_near, low_far, near, far, hidden],
            [
                ((D, FF), bf16),
                ((FF, D), bf16),
                ((8, D), f32),
                ((TOKENS, D), bf16),
                ((TOKENS, FF), bf16),
                ((TOKENS, FF), bf16),
                ((MICRO, SEQ, D) if last else (TOKENS, D), f32),
            ],
            [high_flat],
            scalars=2,
            flops=16 * square,
        )
        return (hidden, *made[:-1]), made[-1]

    grads_shape = ((2, size // 8, padded, LANES), bf16)

    def lift_back(last, incoming, kept):
        scratch = [pltpu.VMEM((size * rows_each + padded - MLP_ROW, LANES), f32)]
        if last:
            scratch.append(pltpu.VMEM((TOKENS, D), f32))
        return call(
            functools.partial(mlp_backward, rows_each, last),
            "mlp_backward",
            ([present] if last else []) + [*place, incoming, *kept],
            [((carry_rows, LANES), f32), grads_shape, grads_shape, ((TOKENS, D), f32)],
            scratch,
            scalars=3 if last else 2,
            flops=32 * square,
        )

    def attend_back(g_hidden, kept):
        state, w_qkv, w_out, vectors, normed_one, qkv, probs, mixed = kept
        return call(
            attention_backward,
            "attention_backward",
            [g_hidden, w_out, qkv, probs, mixed],
            [((TOKENS, 3 * D), bf16), ((D, D), f32), ((8, D), f32)],
            [pltpu.VMEM((TOKENS, D), bf16)],
            flops=4 * square + 2 * core_flops,
        )

    def project_back(first, g_hidden, kept, *made):
        state, w_qkv, w_out, vectors, normed_one, qkv, probs, mixed = kept
        return call(
            functools.partial(projection_backward, rows_each, first),
            "projection_backward",
            [*place, g_hidden, state, w_qkv, vectors, normed_one, *made],
            [grads_shape, grads_shape, ((MICRO, SEQ, D) if first else (TOKENS, D), f32)],
            [pltpu.VMEM((MLP_ROW + carry_rows, LANES), f32)],
            scalars=2,
            flops=12 * square,
        )

    def top_gathered(shard, other):
        return jnp.stack([jnp.where(is_low, shard, other), jnp.where(is_low, other, shard)])[None]

    def moved(parts, step):
        return [swap(part, size, mask) for part, mask in zip(parts, planes[step])]

    def joined(parts, received):
        return [jnp.concatenate(pair) for pair in zip(parts, received)]

    def chained(chunks):
        for mask in chain[:-1]:
            chunks = jnp.concatenate([chunks, swap(chunks, size, mask)])
        return chunks, swap(chunks, size, chain[-1])

    def halved(chunks, received):
        chunks = jnp.concatenate([chunks, received])
        return chunks[:, 0], chunks[:, 1]

    other0 = swap(compact[0], size, size // 2)
    row1, other0 = together(compact[1], other0)
    other1 = swap(row1, size, size // 2)
    half0 = halved(*chained(top_gathered(compact[0], other0)))
    received0 = moved(half0, 0)
    *received0, other1 = together(*received0, other1)
    half0 = joined(half0, received0)
    received0 = moved(half0, 1)
    half1 = halved(*chained(top_gathered(row1, other1)))
    received1 = moved(half1, 0)
    *received0, received1[0], received1[1] = together(*received0, *received1)
    near0 = joined(half0, received0)
    far0 = [swap(part, size, 1) for part in near0]
    half1 = joined(half1, received1)
    received1 = moved(half1, 1)
    one0, hidden = attend(True, near0[0], far0[0], images)
    hidden, *received1 = together(hidden, *received1)
    near1 = joined(half1, received1)
    far1 = [swap(part, size, 1) for part in near1]
    two0, state = lift(False, near0[0], far0[0], near0[1], far0[1], hidden)
    state, *far1 = together(state, *far1)
    one1, hidden = attend(False, near1[0], far1[0], state)
    two1, outputs = lift(True, near1[0], far1[0], near1[1], far1[1], hidden)

    carry_rows = round_up(half * rows_each - MLP_ROW + padded - rows_each, 8)

    def to_plane(pairs, step):
        return [sent(added(pair), size, mask) for pair, mask in zip(pairs, planes[step])]

    def to_core(near, far):
        received = swap(far, size, 1)
        return [(near[quarter], received[quarter]) for quarter in range(2)]

    def along(pairs):
        parts = [added(pair) for pair in pairs]
        for mask in reversed(chain[1:]):
            parts = [added(sent(part, size, mask)) for part in parts]
        return parts

    def hold(pairs, *others):
        values = together(*[value for pair in pairs for value in pair], *others)
        count = 2 * len(pairs)
        return [values[i : i + 2] for i in range(0, count, 2)], *values[count:]

    def to_inner(low, high):
        kept = jnp.concatenate([jnp.where(is_first, *part) for part in (low, high)])
        given = jnp.concatenate([jnp.where(is_first, *part[::-1]) for part in (low, high)])
        return kept, swap(given, size, size // 4)

    def to_top(halves):
        kept = jnp.where(is_low, halves[0], halves[1])
        return kept, swap(jnp.where(is_low, halves[1], halves[0]), size, size // 2)

    carry, near, far, g_hidden = lift_back(True, cotangent, two1)
    high1 = to_core(near, far)
    made = attend_back(g_hidden, one1)
    high1, *made = hold(high1, *made)
    near, far, incoming = project_back(False, g_hidden, one1, *made, carry)
    high1 = to_plane(high1, 1)
    low1 = to_core(near, far)
    carry, near, far, g_hidden = lift_back(False, incoming, two0)
    held, g_hidden = hold(high1 + low1, g_hidden)
    high1, low1 = to_plane(held[:2], 0), to_plane(held[2:], 1)
    high0 = to_core(near, far)
    made = attend_back(g_hidden, one0)
    held, *made = hold(high1 + low1 + high0, *made)
    high1, low1, high0 = along(held[:2]), to_plane(held[2:4], 0), to_plane(held[4:], 1)
    near, far, input_grad = project_back(True, g_hidden, one0, *made, carry)
    low1, near, far = hold(low1, near, far)
    low0 = to_core(near, far)
    high0 = to_plane(high0, 0)
    inner1 = to_inner(along(low1), high1)
    low0, = hold(low0)
    low0 = to_plane(low0, 1)
    held, = hold(low0 + high0 + [inner1])
    low0, high0, top1 = to_plane(held[:2], 0), along(held[2:4]), to_top(added(held[4]))
    held, *high0 = hold(low0, *high0)
    inner0 = to_inner(along(held), high0)
    held, outputs, input_grad = hold([inner0, top1], outputs, input_grad)
    inner0, top1 = held
    top0 = to_top(added(inner0))
    sum0, sum1 = [pair[0].astype(f32) + pair[1].astype(f32) for pair in (top0, top1)]
    owned = [total[:rows_each].reshape(width) for total in (sum0, sum1)]

    grads = jnp.stack(owned)
    flags = flags[None, :] > 0
    rate = jnp.where(flags, rate_matrix, rate_vector)
    decay = jnp.where(flags, decay_matrix, 0.0)
    new_first = beta_one * first_moment + (1.0 - beta_one) * grads
    new_second = beta_two * second_moment + (1.0 - beta_two) * grads * grads
    first_hat = new_first / (1.0 - beta_one**STEP)
    second_hat = new_second / (1.0 - beta_two**STEP)
    new_params = params - rate * (first_hat / (jnp.sqrt(second_hat) + adam_eps) + decay * params)
    return (outputs, input_grad, new_params, new_first, new_second)


def solution(mesh):
    in_specs = (
        P("dp", None, None),
        P("dp", None, None),
        P("dp"),
        P(None, "dp"),
        P(None, "dp"),
        P(None, "dp"),
    )
    out_specs = (
        P("dp", None, None),
        P("dp", None, None),
        P(None, "dp"),
        P(None, "dp"),
        P(None, "dp"),
    )
    body = functools.partial(shards, mesh.shape["dp"])
    return jax.shard_map(body, mesh=mesh, in_specs=in_specs, out_specs=out_specs, check_vma=False)
```

```python
import functools
import math

import jax
import jax.numpy as jnp
from jax import lax
from jax.experimental import pallas as pl
from jax.experimental.pallas import tpu as pltpu
from jax.sharding import PartitionSpec as P

D = 384
FF = 1536
HEADS = 6
HEAD_DIM = 64
SEQ = 197
MICRO = 2
STEP = 10
P_SIZE = 1774080

LANES = 128
ROWS = 208
TOKENS = MICRO * ROWS
PAIRS = HEADS // 2
COST = 1
FORWARD_UNROLL = 6
BACKWARD_UNROLL = 2
VMEM_LIMIT = 10 * 1024 * 1024
BLOCK = 512

eps_norm = 1e-06
beta_one = 0.9
beta_two = 0.999
adam_eps = 1e-08
rate_matrix = 0.1
rate_vector = 0.5
decay_matrix = 0.05
sqrt_half = 0.7071067811865476
inverse_root_tau = 0.3989422804014327

f32 = jnp.float32
bf16 = jnp.bfloat16


def layout():
    return [
        ("ln1_gain", (D,)),
        ("ln1_shift", (D,)),
        ("w_qkv", (D, 3 * D)),
        ("bias_query", (D,)),
        ("bias_value", (D,)),
        ("w_attn_out", (D, D)),
        ("bias_attn_out", (D,)),
        ("ln2_gain", (D,)),
        ("ln2_shift", (D,)),
        ("w_lift", (D, FF)),
        ("bias_lift", (FF,)),
        ("w_drop", (FF, D)),
        ("bias_drop", (D,)),
    ]


def row_offsets():
    offsets, at = {}, 0
    for label, shape in layout():
        offsets[label] = at
        at += math.prod(shape) // LANES
    offsets["end"] = at
    return offsets


ROW = row_offsets()
MLP_ROW = ROW["ln2_gain"]


def matrix_flags(position):
    square = D * D
    lifted = D * FF
    bounds = [
        (2 * D, 2 * D + 3 * square),
        (4 * D + 3 * square, 4 * D + 4 * square),
        (7 * D + 4 * square, 7 * D + 4 * square + lifted),
        (7 * D + 4 * square + lifted + FF, 7 * D + 4 * square + 2 * lifted + FF),
    ]
    flags = jnp.zeros(position.shape, dtype=bool)
    for lower, upper in bounds:
        flags = flags | (position >= lower) & (position < upper)
    return flags


def round_up(value, step):
    return (value + step - 1) // step * step


def dot(a, b, dims):
    return lax.dot_general(a, b, ((dims[0], dims[1]), ((), ())), preferred_element_type=f32)


def dot_nn(a, b):
    return dot(a, b, ((1,), (0,)))


def dot_nt(a, b):
    return dot(a, b, ((1,), (1,)))


def dot_tn(a, b):
    return dot(a, b, ((0,), (0,)))


def read_vector(flat, row, count):
    parts = [flat[row + i : row + i + 1, :] for i in range(count)]
    return jnp.concatenate(parts, axis=1)


def write_vector(flat, row, values):
    for i in range(values.shape[1] // LANES):
        flat[row + i : row + i + 1, :] = values[:, i * LANES : (i + 1) * LANES]


def read_matrix(flat, row, out, depth, width):
    blocks = width // LANES
    for j in range(blocks):
        part = flat[pl.ds(row + j, depth, stride=blocks), :]
        out[:, j * LANES : (j + 1) * LANES] = part.astype(bf16)


def write_matrix(flat, row, values, blocks):
    depth, width = values.shape
    for j in range(width // LANES):
        flat[pl.ds(row + j, depth, stride=blocks), :] = values[:, j * LANES : (j + 1) * LANES]


def normalize(values):
    center = values - jnp.mean(values, -1, keepdims=True)
    rstd = lax.rsqrt(jnp.mean(center * center, -1, keepdims=True) + eps_norm)
    return center * rstd, rstd


def norm_back(incoming, unit, rstd, gain):
    scaled = incoming * gain
    inner = jnp.mean(scaled * unit, -1, keepdims=True)
    back = rstd * (scaled - jnp.mean(scaled, -1, keepdims=True) - unit * inner)
    gain_grad = jnp.sum(incoming * unit, 0, keepdims=True)
    return back, gain_grad, jnp.sum(incoming, 0, keepdims=True)


def head_mask(head):
    lane = lax.broadcasted_iota(jnp.int32, (1, LANES), 1)
    return lane < HEAD_DIM if head == 0 else lane >= HEAD_DIM


def pair_slices(step):
    image, pair = step // PAIRS, step % PAIRS
    rows = pl.ds(pl.multiple_of(image * ROWS, 16), ROWS)
    cols = [pl.ds(pl.multiple_of(t * D + pair * LANES, LANES), LANES) for t in range(3)]
    return rows, cols


def unpack(rows_each, base, chunks, parts, flat):
    def step(chunk, carry):
        begin = (chunks[2] + chunk) * rows_each - base
        for place, near, far in parts:
            count, padded = near.shape[0], near.shape[1]
            at = place[chunk]
            own = lax.rem(at, count)
            rows = jnp.where(at < count, near[own].astype(f32), far[own].astype(f32))
            flat[pl.ds(begin, padded), :] = rows
            begin = begin + padded
        return carry

    lax.fori_loop(chunks[0], chunks[1], step, 0)


def parts_of(places, refs):
    return [(place, refs[2 * i], refs[2 * i + 1]) for i, place in enumerate(places)], refs[2 * len(places) :]


def attention_forward(rows_each, first, count, *refs):
    parts, (state, *refs) = parts_of(refs[:count], refs[count:])
    if first:
        kept_state, refs = refs[0], refs[1:]
    w_qkv, w_out, vectors, normed_one, qkv, probs, mixed, hidden, flat = refs
    unpack(rows_each, 0, (0, -(-MLP_ROW // rows_each), 0), parts, flat)
    read_matrix(flat, ROW["w_qkv"], w_qkv, D, 3 * D)
    read_matrix(flat, ROW["w_attn_out"], w_out, D, D)
    labels = ["ln1_gain", "ln1_shift", "bias_query", "bias_value", "bias_attn_out"]
    for at, label in enumerate(labels):
        vectors[at : at + 1, :] = read_vector(flat, ROW[label], 3)
    gain, shift = vectors[0:1, :], vectors[1:2, :]
    if first:
        kept_state[...] = jnp.zeros_like(kept_state)
        for image in range(MICRO):
            kept_state[image * ROWS : image * ROWS + SEQ, :] = state[image].astype(f32)
        x = kept_state[...]
    else:
        x = state[...]
    unit, _ = normalize(x)
    normed_one[...] = (unit * gain + shift).astype(bf16)
    bias_query = vectors[2:3, :]
    bias = jnp.concatenate([bias_query, jnp.zeros_like(bias_query), vectors[3:4, :]], axis=1)
    for t in range(3):
        cols = slice(t * D, (t + 1) * D)
        product = dot_nn(normed_one[...], w_qkv[:, cols]) + bias[:, cols]
        qkv[:, cols] = product.astype(bf16)

    def step(at, carry):
        rows, cols = pair_slices(at)
        query, key_rows, value_rows = qkv[rows, cols[0]], qkv[rows, cols[1]], qkv[rows, cols[2]]
        real = lax.broadcasted_iota(jnp.int32, (ROWS, ROWS), 1) < SEQ
        sides = []
        for head in range(2):
            own_key = jnp.where(head_mask(head), key_rows, jnp.zeros_like(key_rows))
            raw = jnp.where(real, dot_nt(query, own_key), -1e30)
            powers = jnp.exp((raw - jnp.max(raw, -1, keepdims=True)) * HEAD_DIM ** (-0.5))
            weight = powers / jnp.sum(powers, -1, keepdims=True)
            weight = weight.astype(bf16)
            probs[at * 2 + head] = weight
            sides.append(dot_nn(weight, value_rows))
        mixed[rows, pl.ds(pl.multiple_of((at % PAIRS) * LANES, LANES), LANES)] = jnp.where(
            head_mask(0), sides[0], sides[1]
        ).astype(bf16)
        return carry

    lax.fori_loop(0, MICRO * PAIRS, step, 0, unroll=FORWARD_UNROLL)
    hidden[...] = x + dot_nn(mixed[...], w_out[...]) + vectors[4:5, :]


def mlp_forward(rows_each, last, half, count, *refs):
    low_places, high_places, refs = refs[:count], refs[count : 2 * count], refs[2 * count :]
    low, refs = parts_of(low_places, refs)
    high, (hidden, *refs) = parts_of(high_places, refs)
    w_lift, w_drop, vectors, normed_two, active, slope, result, flat = refs
    begin = MLP_ROW // rows_each
    base = begin * rows_each
    unpack(rows_each, base, (begin, half, 0), low, flat)
    unpack(rows_each, base, (0, half, half), high, flat)
    read_matrix(flat, ROW["w_lift"] - base, w_lift, D, FF)
    read_matrix(flat, ROW["w_drop"] - base, w_drop, FF, D)
    for at, label in enumerate(["ln2_gain", "ln2_shift", "bias_drop"]):
        vectors[at : at + 1, :] = read_vector(flat, ROW[label] - base, 3)
    bias_lift = read_vector(flat, ROW["bias_lift"] - base, FF // LANES)
    gain, shift = vectors[0:1, :], vectors[1:2, :]
    unit, _ = normalize(hidden[...])
    normed_two[...] = (unit * gain + shift).astype(bf16)
    total = hidden[...] + vectors[2:3, :]
    for at in range(0, FF, BLOCK):
        cols = slice(at, at + BLOCK)
        lifted = dot_nn(normed_two[...], w_lift[:, cols]) + bias_lift[:, cols]
        below = 0.5 * (1.0 + lax.erf(lifted * sqrt_half))
        active[:, cols] = (lifted * below).astype(bf16)
        bell = jnp.exp(-0.5 * lifted * lifted) * inverse_root_tau
        slope[:, cols] = (below + lifted * bell).astype(bf16)
        total += dot_nn(active[:, cols], w_drop[cols, :])
    if last:
        for image in range(MICRO):
            result[image] = total[image * ROWS : image * ROWS + SEQ, :]
    else:
        result[...] = total


def pack(flat, base, rows_each, first_chunk, places, near, far):
    count, padded = near.shape[1], near.shape[2]
    for quarter, place in enumerate(places):

        def step(chunk, carry):
            at = (first_chunk + quarter * 2 * count + chunk) * rows_each - base
            index = lax.rem(place[chunk], count)

            @pl.when(place[chunk] < count)
            def _():
                near[quarter, index] = flat[pl.ds(at, padded), :].astype(bf16)

            @pl.when(place[chunk] >= count)
            def _():
                far[quarter, index] = flat[pl.ds(at, padded), :].astype(bf16)

            return carry

        lax.fori_loop(0, 2 * count, step, 0)


def mlp_backward(rows_each, last, *refs):
    if last:
        present, refs = refs[0], refs[1:]
    places, refs = refs[:2], refs[2:]
    incoming, hidden, w_lift, w_drop, vectors, normed_two, active, slope = refs[:8]
    refs = refs[8:]
    carry, near, far, g_hidden, flat = refs[:5]
    count = 4 * near.shape[1]
    if last:
        kept = refs[5]
        kept[...] = jnp.zeros_like(kept)
        for image in range(MICRO):
            seed = incoming[image].astype(f32) * present[image].astype(f32)
            kept[image * ROWS : image * ROWS + SEQ, :] = seed
        g = kept[...]
    else:
        g = incoming[...]
    base = MLP_ROW
    end = ROW["end"] - base
    flat[end:, :] = jnp.zeros((flat.shape[0] - end, LANES), f32)
    g_out = g.astype(bf16)
    write_vector(flat, ROW["bias_drop"] - base, jnp.sum(g_out.astype(f32), 0, keepdims=True))
    d_normed = jnp.zeros((TOKENS, D), f32)
    for at in range(0, FF, BLOCK):
        cols = slice(at, at + BLOCK)
        row = ROW["w_drop"] - base + at * (D // LANES)
        write_matrix(flat, row, dot_tn(active[:, cols], g_out), D // LANES)
        d_lifted = (dot_nt(g_out, w_drop[cols, :]) * slope[:, cols].astype(f32)).astype(bf16)
        row = ROW["bias_lift"] - base + at // LANES
        write_vector(flat, row, jnp.sum(d_lifted.astype(f32), 0, keepdims=True))
        row = ROW["w_lift"] - base + at // LANES
        write_matrix(flat, row, dot_tn(normed_two[...], d_lifted), FF // LANES)
        d_normed += dot_nt(d_lifted, w_lift[:, cols])
    unit, rstd = normalize(hidden[...])
    back, gain_grad, shift_grad = norm_back(d_normed, unit, rstd, vectors[0:1, :])
    write_vector(flat, ROW["ln2_gain"] - base, gain_grad)
    write_vector(flat, ROW["ln2_shift"] - base, shift_grad)
    g_hidden[...] = g + back
    carry[...] = flat[: carry.shape[0], :]
    pack(flat, base, rows_each, count, places, near, far)


def attention_backward(g_hidden, w_out, qkv, probs, mixed, d_qkv, d_out, bias_out, d_mixed):
    g_att = g_hidden[...].astype(bf16)
    bias_out[...] = jnp.broadcast_to(jnp.sum(g_att.astype(f32), 0, keepdims=True), bias_out.shape)
    d_out[...] = dot_tn(mixed[...], g_att)
    d_mixed[...] = dot_nt(g_att, w_out[...]).astype(bf16)

    def step(at, carried):
        rows, cols = pair_slices(at)
        query, key_rows, value_rows = qkv[rows, cols[0]], qkv[rows, cols[1]], qkv[rows, cols[2]]
        mixed_grad = d_mixed[rows, pl.ds(pl.multiple_of((at % PAIRS) * LANES, LANES), LANES)]
        d_query, d_key, d_value = [], [], []
        for head in range(2):
            own = jnp.where(head_mask(head), mixed_grad, jnp.zeros_like(mixed_grad))
            weight = probs[at * 2 + head]
            d_value.append(dot_tn(weight, mixed_grad))
            weight = weight.astype(f32)
            d_probs = dot_nt(own, value_rows)
            inner = jnp.sum(weight * d_probs, -1, keepdims=True)
            d_scores = (weight * (d_probs - inner)).astype(bf16)
            d_query.append(dot_nn(d_scores, key_rows))
            d_key.append(dot_tn(d_scores, query))
        scale = HEAD_DIM ** (-0.5)
        mask = head_mask(0)
        d_qkv[rows, cols[0]] = (jnp.where(mask, d_query[0], d_query[1]) * scale).astype(bf16)
        d_qkv[rows, cols[1]] = (jnp.where(mask, d_key[0], d_key[1]) * scale).astype(bf16)
        d_qkv[rows, cols[2]] = jnp.where(mask, d_value[0], d_value[1]).astype(bf16)
        return carried

    lax.fori_loop(0, MICRO * PAIRS, step, 0, unroll=BACKWARD_UNROLL)

def projection_backward(rows_each, first, *refs):
    places, refs = refs[:2], refs[2:]
    g_hidden, state, w_qkv, vectors, normed_one, d_qkv, d_out, bias_out, carry = refs[:9]
    near, far, input_grad, flat = refs[9:]
    flat[MLP_ROW : MLP_ROW + carry.shape[0], :] = carry[...]
    write_vector(flat, ROW["bias_attn_out"], bias_out[0:1, :])
    write_matrix(flat, ROW["w_attn_out"], d_out[...], D // LANES)
    query_sum = jnp.sum(d_qkv[:, :D].astype(f32), 0, keepdims=True)
    write_vector(flat, ROW["bias_query"], query_sum)
    value_sum = jnp.sum(d_qkv[:, 2 * D :].astype(f32), 0, keepdims=True)
    write_vector(flat, ROW["bias_value"], value_sum)
    d_normed = jnp.zeros((TOKENS, D), f32)
    for t in range(3):
        cols = slice(t * D, (t + 1) * D)
        part = d_qkv[:, cols]
        row = ROW["w_qkv"] + t * (D // LANES)
        write_matrix(flat, row, dot_tn(normed_one[...], part), 3 * D // LANES)
        d_normed += dot_nt(part, w_qkv[:, cols])
    unit, rstd = normalize(state[...])
    back, gain_grad, shift_grad = norm_back(d_normed, unit, rstd, vectors[0:1, :])
    write_vector(flat, ROW["ln1_gain"], gain_grad)
    write_vector(flat, ROW["ln1_shift"], shift_grad)
    total = g_hidden[...] + back
    if first:
        for image in range(MICRO):
            input_grad[image] = total[image * ROWS : image * ROWS + SEQ, :]
    else:
        input_grad[...] = total
    pack(flat, 0, rows_each, 0, places, near, far)


def call(body, name, inputs, outputs, scratch, scalars=0, flops=0):
    in_specs = [pl.BlockSpec(memory_space=pltpu.SMEM)] * scalars
    in_specs += [pl.BlockSpec(memory_space=pltpu.VMEM)] * (len(inputs) - scalars)
    shapes = [jax.ShapeDtypeStruct(shape, dtype) for shape, dtype in outputs]
    moved = sum(math.prod(s.shape) * s.dtype.itemsize for s in list(inputs) + shapes)
    return pl.pallas_call(
        body,
        name=name,
        out_shape=shapes,
        in_specs=in_specs,
        out_specs=[pl.BlockSpec(memory_space=pltpu.VMEM)] * len(shapes),
        scratch_shapes=scratch,
        compiler_params=pltpu.CompilerParams(vmem_limit_bytes=VMEM_LIMIT),
        cost_estimate=pl.CostEstimate(flops=flops // COST, bytes_accessed=moved // COST, transcendentals=0),
    )(*inputs)


def tie(values, *before):
    return lax.optimization_barrier((values, before))[0]


def together(*values):
    return lax.optimization_barrier(values)


def swap(values, size, mask):
    return lax.ppermute(values, "dp", [(i, i ^ mask) for i in range(size)])


def gather_masks(bits):
    chain = [1 << bit for bit in range(bits - 2, 2, -1)]
    return [chain + [2, 4, 1], chain + [4, 2, 1]]


def places(me, size, masks):
    relative = me ^ jnp.arange(size // 2, dtype=jnp.int32)
    place = jnp.zeros_like(relative)
    for digit, mask in enumerate(masks):
        place = place | jnp.where(relative & mask != 0, 1 << digit, 0)
    return place


def sent(part, size, mask):
    middle = part.shape[0] // 2
    return part[:middle], swap(part[middle:], size, mask)


def added(pair):
    return (pair[0].astype(f32) + pair[1].astype(f32)).astype(bf16)


def shards(size, images, cotangent, present, params, first_moment, second_moment):
    bits = size.bit_length() - 1
    width = params.shape[1]
    rows_each = width // LANES
    padded = round_up(rows_each, 16)
    half = size // 2
    me = lax.axis_index("dp")
    chain = [1 << bit for bit in range(bits - 2, 2, -1)]
    planes = [(2, 4), (4, 2)]
    place_low, place_high = [places(me, size, chain + [mask, 6 - mask, 1]) for mask in planes[0]]
    place_wide = places(me, size, [2, 4] + chain + [1])
    place = [places(me, size // 2, chain[1:] + [mask, 6 - mask, 1]) for mask in planes[0]]

    is_low, is_first = (me >> (bits - 1)) & 1 == 0, (me >> (bits - 2)) & 1 == 0
    flags = matrix_flags(me * width + jnp.arange(width, dtype=jnp.int32)).astype(f32)
    early = together(params, is_low, is_first, flags, place_low, place_high, place_wide, *place)
    params, is_low, is_first, flags, place_low, place_high, place_wide, *place = early
    compact = params.astype(bf16).reshape(2, rows_each, LANES)
    compact = jnp.pad(compact, ((0, 0), (0, padded - rows_each), (0, 0)))

    low_flat = pltpu.VMEM((-(-MLP_ROW // rows_each) * rows_each + padded, LANES), f32)
    begin = MLP_ROW // rows_each
    high_flat = pltpu.VMEM(((size - begin) * rows_each + padded, LANES), f32)
    square = TOKENS * D * D
    core_flops = 2 * 2 * MICRO * HEADS * ROWS * ROWS * HEAD_DIM

    def attend(first, places, low, state):
        outputs = [((TOKENS, D), f32)] if first else []
        outputs += [
            ((D, 3 * D), bf16),
            ((D, D), bf16),
            ((8, D), f32),
            ((TOKENS, D), bf16),
            ((TOKENS, 3 * D), bf16),
            ((MICRO * HEADS, ROWS, ROWS), bf16),
            ((TOKENS, D), bf16),
            ((TOKENS, D), f32),
        ]
        made = call(
            functools.partial(attention_forward, rows_each, first, len(places)),
            "attention_forward",
            [*places, *low, state],
            outputs,
            [low_flat],
            scalars=len(places),
            flops=8 * square + core_flops,
        )
        made = made if first else [state, *made]
        return made[:-1], made[-1]

    def lift(last, low_places, high_places, low, high, hidden):
        made = call(
            functools.partial(mlp_forward, rows_each, last, half, len(low_places)),
            "mlp_forward",
            [*low_places, *high_places, *low, *high, hidden],
            [
                ((D, FF), bf16),
                ((FF, D), bf16),
                ((8, D), f32),
                ((TOKENS, D), bf16),
                ((TOKENS, FF), bf16),
                ((TOKENS, FF), bf16),
                ((MICRO, SEQ, D) if last else (TOKENS, D), f32),
            ],
            [high_flat],
            scalars=2 * len(low_places),
            flops=16 * square,
        )
        return (hidden, *made[:-1]), made[-1]

    grads_shape = ((2, size // 8, padded, LANES), bf16)

    def lift_back(last, incoming, kept):
        scratch = [pltpu.VMEM((size * rows_each + padded - MLP_ROW, LANES), f32)]
        if last:
            scratch.append(pltpu.VMEM((TOKENS, D), f32))
        return call(
            functools.partial(mlp_backward, rows_each, last),
            "mlp_backward",
            ([present] if last else []) + [*place, incoming, *kept],
            [((carry_rows, LANES), f32), grads_shape, grads_shape, ((TOKENS, D), f32)],
            scratch,
            scalars=3 if last else 2,
            flops=32 * square,
        )

    def attend_back(g_hidden, kept):
        state, w_qkv, w_out, vectors, normed_one, qkv, probs, mixed = kept
        return call(
            attention_backward,
            "attention_backward",
            [g_hidden, w_out, qkv, probs, mixed],
            [((TOKENS, 3 * D), bf16), ((D, D), f32), ((8, D), f32)],
            [pltpu.VMEM((TOKENS, D), bf16)],
            flops=4 * square + 2 * core_flops,
        )

    def project_back(first, g_hidden, kept, *made):
        state, w_qkv, w_out, vectors, normed_one, qkv, probs, mixed = kept
        return call(
            functools.partial(projection_backward, rows_each, first),
            "projection_backward",
            [*place, g_hidden, state, w_qkv, vectors, normed_one, *made],
            [grads_shape, grads_shape, ((MICRO, SEQ, D) if first else (TOKENS, D), f32)],
            [pltpu.VMEM((MLP_ROW + carry_rows, LANES), f32)],
            scalars=2,
            flops=12 * square,
        )

    def top_gathered(shard, other):
        return jnp.stack([jnp.where(is_low, shard, other), jnp.where(is_low, other, shard)])[None]

    def exchanged(*values):
        return [swap(value, size, bits) for value, bits in zip(values, (size // 4, size // 2, size // 4 * 3))]

    def moved(parts, step):
        return [swap(part, size, mask) for part, mask in zip(parts, planes[step])]

    def joined(parts, received):
        return [jnp.concatenate(pair) for pair in zip(parts, received)]

    def chained(chunks):
        for mask in chain[:-1]:
            chunks = jnp.concatenate([chunks, swap(chunks, size, mask)])
        return chunks, swap(chunks, size, chain[-1])

    def halved(chunks, received):
        chunks = jnp.concatenate([chunks, received])
        return chunks[:, 0], chunks[:, 1]

    cut = padded - round_up(padded * 5 // 14, 16)
    row1, wide = compact[1, :cut], compact[1, cut:][None]
    nearby, other0, far_other0 = exchanged(compact[0], compact[0], compact[0])
    received = swap(wide, size, 2)
    row1, nearby, other0, far_other0, received = together(row1, nearby, other0, far_other0, received)
    wide = jnp.concatenate([wide, received])
    other1 = swap(row1, size, size // 2)
    received = swap(wide, size, 4)
    chunks0 = top_gathered(jnp.stack([compact[0], nearby]), jnp.stack([other0, far_other0]))[0]
    half0 = chunks0[0], chunks0[1]
    for mask in chain[1:]:
        half0 = [jnp.concatenate([part, swap(part, size, mask)]) for part in half0]
    received0 = moved(half0, 0)
    *received0, other1, received = together(*received0, other1, received)
    wide = jnp.concatenate([wide, received])
    half0 = joined(half0, received0)
    received0 = moved(half0, 1)
    half1 = halved(*chained(top_gathered(row1, other1)))
    received1 = moved(half1, 0)
    received = swap(wide, size, size // 2)
    *received0, received1[0], received1[1], received = together(*received0, *received1, received)
    near0 = joined(half0, received0)
    far0 = [swap(part, size, 1) for part in near0]
    half1 = joined(half1, received1)
    received1 = moved(half1, 1)
    wide = jnp.stack([jnp.where(is_low, wide, received), jnp.where(is_low, received, wide)], axis=1)
    wide, received = chained(wide)
    one0, hidden = attend(True, [place_low], [near0[0], far0[0]], images)
    hidden, *received1, received = together(hidden, *received1, received)
    near1 = joined(half1, received1)
    near1 = [part for pair in zip(near1, halved(wide, received)) for part in pair]
    far1 = [swap(part, size, 1) for part in near1]
    two0, state = lift(False, [place_low], [place_high], [near0[0], far0[0]], [near0[1], far0[1]], hidden)
    state, *far1 = together(state, *far1)
    both1 = [part for pair in zip(near1, far1) for part in pair]
    low1, high1 = both1[:4], both1[4:]
    one1, hidden = attend(False, [place_low, place_wide], low1, state)
    two1, outputs = lift(True, [place_low, place_wide], [place_high, place_wide], low1, high1, hidden)

    carry_rows = round_up(half * rows_each - MLP_ROW + padded - rows_each, 8)

    def to_plane(pairs, step):
        return [sent(added(pair), size, mask) for pair, mask in zip(pairs, planes[step])]

    def to_core(near, far):
        received = swap(far, size, 1)
        return [(near[quarter], received[quarter]) for quarter in range(2)]

    def along(pairs):
        parts = [added(pair) for pair in pairs]
        for mask in reversed(chain[1:]):
            parts = [added(sent(part, size, mask)) for part in parts]
        return parts

    def hold(pairs, *others):
        values = together(*[value for pair in pairs for value in pair], *others)
        count = 2 * len(pairs)
        return [values[i : i + 2] for i in range(0, count, 2)], *values[count:]

    def to_inner(low, high):
        kept = jnp.concatenate([jnp.where(is_first, *part) for part in (low, high)])
        given = jnp.concatenate([jnp.where(is_first, *part[::-1]) for part in (low, high)])
        return kept, swap(given, size, size // 4)

    def to_top(halves):
        kept = jnp.where(is_low, halves[0], halves[1])
        return kept, swap(jnp.where(is_low, halves[1], halves[0]), size, size // 2)

    carry, near, far, g_hidden = lift_back(True, cotangent, two1)
    high1 = to_core(near, far)
    made = attend_back(g_hidden, one1)
    high1, *made = hold(high1, *made)
    near, far, incoming = project_back(False, g_hidden, one1, *made, carry)
    high1 = to_plane(high1, 1)
    low1 = to_core(near, far)
    carry, near, far, g_hidden = lift_back(False, incoming, two0)
    held, g_hidden = hold(high1 + low1, g_hidden)
    high1, low1 = to_plane(held[:2], 0), to_plane(held[2:], 1)
    high0 = to_core(near, far)
    made = attend_back(g_hidden, one0)
    held, *made = hold(high1 + low1 + high0, *made)
    high1, low1, high0 = along(held[:2]), to_plane(held[2:4], 0), to_plane(held[4:], 1)
    near, far, input_grad = project_back(True, g_hidden, one0, *made, carry)
    low1, near, far = hold(low1, near, far)
    low0 = to_core(near, far)
    high0 = to_plane(high0, 0)
    inner1 = to_inner(along(low1), high1)
    low0, = hold(low0)
    low0 = to_plane(low0, 1)
    held, = hold(low0 + high0 + [inner1])
    low0, high0, top1 = to_plane(held[:2], 0), along(held[2:4]), to_top(added(held[4]))
    held, *high0, outputs, input_grad = hold(low0, *high0, outputs, input_grad)
    low0 = along(held)
    here, there = [jnp.where(is_low, *pair) for pair in zip(low0, high0)], [jnp.where(is_low, *pair) for pair in zip(high0, low0)]
    here, there = [[jnp.where(is_first, *pair), jnp.where(is_first, *pair[::-1])] for pair in (here, there)]
    values = exchanged(here[1][0], there[0][0], there[1][0])
    (nearby, other, far_other), received = values, top1[1]
    sum0 = here[0][0].astype(f32) + nearby.astype(f32) + other.astype(f32) + far_other.astype(f32)
    sum1 = top1[0].astype(f32) + received.astype(f32)
    owned = [total[:rows_each].reshape(width) for total in (sum0, sum1)]

    grads = jnp.stack(owned)
    flags = flags[None, :] > 0
    rate = jnp.where(flags, rate_matrix, rate_vector)
    decay = jnp.where(flags, decay_matrix, 0.0)
    new_first = beta_one * first_moment + (1.0 - beta_one) * grads
    new_second = beta_two * second_moment + (1.0 - beta_two) * grads * grads
    first_hat = new_first / (1.0 - beta_one**STEP)
    second_hat = new_second / (1.0 - beta_two**STEP)
    new_params = params - rate * (first_hat / (jnp.sqrt(second_hat) + adam_eps) + decay * params)
    return (outputs, input_grad, new_params, new_first, new_second)


def solution(mesh):
    in_specs = (
        P("dp", None, None),
        P("dp", None, None),
        P("dp"),
        P(None, "dp"),
        P(None, "dp"),
        P(None, "dp"),
    )
    out_specs = (
        P("dp", None, None),
        P("dp", None, None),
        P(None, "dp"),
        P(None, "dp"),
        P(None, "dp"),
    )
    body = functools.partial(shards, mesh.shape["dp"])
    return jax.shard_map(body, mesh=mesh, in_specs=in_specs, out_specs=out_specs, check_vma=False)
```

```python
import functools
import math

import jax
import jax.numpy as jnp
from jax import lax
from jax.experimental import pallas as pl
from jax.experimental.pallas import tpu as pltpu
from jax.sharding import PartitionSpec as P

D = 384
FF = 1536
HEADS = 6
HEAD_DIM = 64
SEQ = 197
MICRO = 2
STEP = 10
P_SIZE = 1774080

LANES = 128
ROWS = 208
TOKENS = MICRO * ROWS
PAIRS = HEADS // 2
COST = 1
FORWARD_UNROLL = 6
BACKWARD_UNROLL = 2
VMEM_LIMIT = 10 * 1024 * 1024
BLOCK = 512

eps_norm = 1e-06
beta_one = 0.9
beta_two = 0.999
adam_eps = 1e-08
rate_matrix = 0.1
rate_vector = 0.5
decay_matrix = 0.05
sqrt_half = 0.7071067811865476
inverse_root_tau = 0.3989422804014327

f32 = jnp.float32
bf16 = jnp.bfloat16


def layout():
    return [
        ("ln1_gain", (D,)),
        ("ln1_shift", (D,)),
        ("w_qkv", (D, 3 * D)),
        ("bias_query", (D,)),
        ("bias_value", (D,)),
        ("w_attn_out", (D, D)),
        ("bias_attn_out", (D,)),
        ("ln2_gain", (D,)),
        ("ln2_shift", (D,)),
        ("w_lift", (D, FF)),
        ("bias_lift", (FF,)),
        ("w_drop", (FF, D)),
        ("bias_drop", (D,)),
    ]


def row_offsets():
    offsets, at = {}, 0
    for label, shape in layout():
        offsets[label] = at
        at += math.prod(shape) // LANES
    offsets["end"] = at
    return offsets


ROW = row_offsets()
MLP_ROW = ROW["ln2_gain"]


def matrix_flags(position):
    square = D * D
    lifted = D * FF
    bounds = [
        (2 * D, 2 * D + 3 * square),
        (4 * D + 3 * square, 4 * D + 4 * square),
        (7 * D + 4 * square, 7 * D + 4 * square + lifted),
        (7 * D + 4 * square + lifted + FF, 7 * D + 4 * square + 2 * lifted + FF),
    ]
    flags = jnp.zeros(position.shape, dtype=bool)
    for lower, upper in bounds:
        flags = flags | (position >= lower) & (position < upper)
    return flags


def round_up(value, step):
    return (value + step - 1) // step * step


def dot(a, b, dims):
    return lax.dot_general(a, b, ((dims[0], dims[1]), ((), ())), preferred_element_type=f32)


def dot_nn(a, b):
    return dot(a, b, ((1,), (0,)))


def dot_nt(a, b):
    return dot(a, b, ((1,), (1,)))


def dot_tn(a, b):
    return dot(a, b, ((0,), (0,)))


def read_vector(flat, row, count):
    parts = [flat[row + i : row + i + 1, :] for i in range(count)]
    return jnp.concatenate(parts, axis=1)


def write_vector(flat, row, values):
    for i in range(values.shape[1] // LANES):
        flat[row + i : row + i + 1, :] = values[:, i * LANES : (i + 1) * LANES]


def read_matrix(flat, row, out, depth, width):
    blocks = width // LANES
    for j in range(blocks):
        part = flat[pl.ds(row + j, depth, stride=blocks), :]
        out[:, j * LANES : (j + 1) * LANES] = part.astype(bf16)


def write_matrix(flat, row, values, blocks):
    depth, width = values.shape
    for j in range(width // LANES):
        flat[pl.ds(row + j, depth, stride=blocks), :] = values[:, j * LANES : (j + 1) * LANES]


def normalize(values):
    center = values - jnp.mean(values, -1, keepdims=True)
    rstd = lax.rsqrt(jnp.mean(center * center, -1, keepdims=True) + eps_norm)
    return center * rstd, rstd


def norm_back(incoming, unit, rstd, gain):
    scaled = incoming * gain
    inner = jnp.mean(scaled * unit, -1, keepdims=True)
    back = rstd * (scaled - jnp.mean(scaled, -1, keepdims=True) - unit * inner)
    gain_grad = jnp.sum(incoming * unit, 0, keepdims=True)
    return back, gain_grad, jnp.sum(incoming, 0, keepdims=True)


def head_mask(head):
    lane = lax.broadcasted_iota(jnp.int32, (1, LANES), 1)
    return lane < HEAD_DIM if head == 0 else lane >= HEAD_DIM


def pair_slices(step):
    image, pair = step // PAIRS, step % PAIRS
    rows = pl.ds(pl.multiple_of(image * ROWS, 16), ROWS)
    cols = [pl.ds(pl.multiple_of(t * D + pair * LANES, LANES), LANES) for t in range(3)]
    return rows, cols


def unpack(rows_each, base, chunks, parts, flat):
    def step(chunk, carry):
        begin = (chunks[2] + chunk) * rows_each - base
        for place, near, far in parts:
            count, padded = near.shape[0], near.shape[1]
            at = place[chunk]
            own = lax.rem(at, count)
            rows = jnp.where(at < count, near[own].astype(f32), far[own].astype(f32))
            flat[pl.ds(begin, padded), :] = rows
            begin = begin + padded
        return carry

    lax.fori_loop(chunks[0], chunks[1], step, 0)


def parts_of(places, refs):
    return [(place, refs[2 * i], refs[2 * i + 1]) for i, place in enumerate(places)], refs[2 * len(places) :]


def attention_forward(rows_each, first, count, *refs):
    parts, (state, *refs) = parts_of(refs[:count], refs[count:])
    if first:
        kept_state, refs = refs[0], refs[1:]
    w_qkv, w_out, vectors, normed_one, qkv, probs, mixed, hidden, flat = refs
    unpack(rows_each, 0, (0, -(-MLP_ROW // rows_each), 0), parts, flat)
    read_matrix(flat, ROW["w_qkv"], w_qkv, D, 3 * D)
    read_matrix(flat, ROW["w_attn_out"], w_out, D, D)
    labels = ["ln1_gain", "ln1_shift", "bias_query", "bias_value", "bias_attn_out"]
    for at, label in enumerate(labels):
        vectors[at : at + 1, :] = read_vector(flat, ROW[label], 3)
    gain, shift = vectors[0:1, :], vectors[1:2, :]
    if first:
        kept_state[...] = jnp.zeros_like(kept_state)
        for image in range(MICRO):
            kept_state[image * ROWS : image * ROWS + SEQ, :] = state[image].astype(f32)
        x = kept_state[...]
    else:
        x = state[...]
    unit, _ = normalize(x)
    normed_one[...] = (unit * gain + shift).astype(bf16)
    bias_query = vectors[2:3, :]
    bias = jnp.concatenate([bias_query, jnp.zeros_like(bias_query), vectors[3:4, :]], axis=1)
    for t in range(3):
        cols = slice(t * D, (t + 1) * D)
        product = dot_nn(normed_one[...], w_qkv[:, cols]) + bias[:, cols]
        qkv[:, cols] = product.astype(bf16)

    def step(at, carry):
        rows, cols = pair_slices(at)
        query, key_rows, value_rows = qkv[rows, cols[0]], qkv[rows, cols[1]], qkv[rows, cols[2]]
        real = lax.broadcasted_iota(jnp.int32, (ROWS, ROWS), 1) < SEQ
        sides = []
        for head in range(2):
            own_key = jnp.where(head_mask(head), key_rows, jnp.zeros_like(key_rows))
            raw = jnp.where(real, dot_nt(query, own_key), -1e30)
            powers = jnp.exp((raw - jnp.max(raw, -1, keepdims=True)) * HEAD_DIM ** (-0.5))
            weight = powers / jnp.sum(powers, -1, keepdims=True)
            weight = weight.astype(bf16)
            probs[at * 2 + head] = weight
            sides.append(dot_nn(weight, value_rows))
        mixed[rows, pl.ds(pl.multiple_of((at % PAIRS) * LANES, LANES), LANES)] = jnp.where(
            head_mask(0), sides[0], sides[1]
        ).astype(bf16)
        return carry

    lax.fori_loop(0, MICRO * PAIRS, step, 0, unroll=FORWARD_UNROLL)
    hidden[...] = x + dot_nn(mixed[...], w_out[...]) + vectors[4:5, :]


def mlp_forward(rows_each, last, half, count, *refs):
    low_places, high_places, refs = refs[:count], refs[count : 2 * count], refs[2 * count :]
    low, refs = parts_of(low_places, refs)
    high, (hidden, *refs) = parts_of(high_places, refs)
    w_lift, w_drop, vectors, normed_two, active, slope, result, flat = refs
    begin = MLP_ROW // rows_each
    base = begin * rows_each
    unpack(rows_each, base, (begin, half, 0), low, flat)
    unpack(rows_each, base, (0, half, half), high, flat)
    read_matrix(flat, ROW["w_lift"] - base, w_lift, D, FF)
    read_matrix(flat, ROW["w_drop"] - base, w_drop, FF, D)
    for at, label in enumerate(["ln2_gain", "ln2_shift", "bias_drop"]):
        vectors[at : at + 1, :] = read_vector(flat, ROW[label] - base, 3)
    bias_lift = read_vector(flat, ROW["bias_lift"] - base, FF // LANES)
    gain, shift = vectors[0:1, :], vectors[1:2, :]
    unit, _ = normalize(hidden[...])
    normed_two[...] = (unit * gain + shift).astype(bf16)
    total = hidden[...] + vectors[2:3, :]
    for at in range(0, FF, BLOCK):
        cols = slice(at, at + BLOCK)
        lifted = dot_nn(normed_two[...], w_lift[:, cols]) + bias_lift[:, cols]
        below = 0.5 * (1.0 + lax.erf(lifted * sqrt_half))
        active[:, cols] = (lifted * below).astype(bf16)
        bell = jnp.exp(-0.5 * lifted * lifted) * inverse_root_tau
        slope[:, cols] = (below + lifted * bell).astype(bf16)
        total += dot_nn(active[:, cols], w_drop[cols, :])
    if last:
        for image in range(MICRO):
            result[image] = total[image * ROWS : image * ROWS + SEQ, :]
    else:
        result[...] = total


def pack(flat, base, rows_each, first_chunk, places, near, far):
    count, padded = near.shape[1], near.shape[2]
    for quarter, place in enumerate(places):

        def step(chunk, carry):
            at = (first_chunk + quarter * 2 * count + chunk) * rows_each - base
            index = lax.rem(place[chunk], count)

            @pl.when(place[chunk] < count)
            def _():
                near[quarter, index] = flat[pl.ds(at, padded), :].astype(bf16)

            @pl.when(place[chunk] >= count)
            def _():
                far[quarter, index] = flat[pl.ds(at, padded), :].astype(bf16)

            return carry

        lax.fori_loop(0, 2 * count, step, 0)


def mlp_backward(rows_each, last, *refs):
    if last:
        present, refs = refs[0], refs[1:]
    places, refs = refs[:2], refs[2:]
    incoming, hidden, w_lift, w_drop, vectors, normed_two, active, slope = refs[:8]
    refs = refs[8:]
    carry, near, far, g_hidden, flat = refs[:5]
    count = 4 * near.shape[1]
    if last:
        kept = refs[5]
        kept[...] = jnp.zeros_like(kept)
        for image in range(MICRO):
            seed = incoming[image].astype(f32) * present[image].astype(f32)
            kept[image * ROWS : image * ROWS + SEQ, :] = seed
        g = kept[...]
    else:
        g = incoming[...]
    base = MLP_ROW
    end = ROW["end"] - base
    flat[end:, :] = jnp.zeros((flat.shape[0] - end, LANES), f32)
    g_out = g.astype(bf16)
    write_vector(flat, ROW["bias_drop"] - base, jnp.sum(g_out.astype(f32), 0, keepdims=True))
    d_normed = jnp.zeros((TOKENS, D), f32)
    for at in range(0, FF, BLOCK):
        cols = slice(at, at + BLOCK)
        row = ROW["w_drop"] - base + at * (D // LANES)
        write_matrix(flat, row, dot_tn(active[:, cols], g_out), D // LANES)
        d_lifted = (dot_nt(g_out, w_drop[cols, :]) * slope[:, cols].astype(f32)).astype(bf16)
        row = ROW["bias_lift"] - base + at // LANES
        write_vector(flat, row, jnp.sum(d_lifted.astype(f32), 0, keepdims=True))
        row = ROW["w_lift"] - base + at // LANES
        write_matrix(flat, row, dot_tn(normed_two[...], d_lifted), FF // LANES)
        d_normed += dot_nt(d_lifted, w_lift[:, cols])
    unit, rstd = normalize(hidden[...])
    back, gain_grad, shift_grad = norm_back(d_normed, unit, rstd, vectors[0:1, :])
    write_vector(flat, ROW["ln2_gain"] - base, gain_grad)
    write_vector(flat, ROW["ln2_shift"] - base, shift_grad)
    g_hidden[...] = g + back
    carry[...] = flat[: carry.shape[0], :]
    pack(flat, base, rows_each, count, places, near, far)


def attention_backward(g_hidden, w_out, qkv, probs, mixed, d_qkv, d_out, bias_out, d_mixed):
    g_att = g_hidden[...].astype(bf16)
    bias_out[...] = jnp.broadcast_to(jnp.sum(g_att.astype(f32), 0, keepdims=True), bias_out.shape)
    d_out[...] = dot_tn(mixed[...], g_att)
    d_mixed[...] = dot_nt(g_att, w_out[...]).astype(bf16)

    def step(at, carried):
        rows, cols = pair_slices(at)
        query, key_rows, value_rows = qkv[rows, cols[0]], qkv[rows, cols[1]], qkv[rows, cols[2]]
        mixed_grad = d_mixed[rows, pl.ds(pl.multiple_of((at % PAIRS) * LANES, LANES), LANES)]
        d_query, d_key, d_value = [], [], []
        for head in range(2):
            own = jnp.where(head_mask(head), mixed_grad, jnp.zeros_like(mixed_grad))
            weight = probs[at * 2 + head]
            d_value.append(dot_tn(weight, mixed_grad))
            weight = weight.astype(f32)
            d_probs = dot_nt(own, value_rows)
            inner = jnp.sum(weight * d_probs, -1, keepdims=True)
            d_scores = (weight * (d_probs - inner)).astype(bf16)
            d_query.append(dot_nn(d_scores, key_rows))
            d_key.append(dot_tn(d_scores, query))
        scale = HEAD_DIM ** (-0.5)
        mask = head_mask(0)
        d_qkv[rows, cols[0]] = (jnp.where(mask, d_query[0], d_query[1]) * scale).astype(bf16)
        d_qkv[rows, cols[1]] = (jnp.where(mask, d_key[0], d_key[1]) * scale).astype(bf16)
        d_qkv[rows, cols[2]] = jnp.where(mask, d_value[0], d_value[1]).astype(bf16)
        return carried

    lax.fori_loop(0, MICRO * PAIRS, step, 0, unroll=BACKWARD_UNROLL)

def projection_backward(rows_each, first, *refs):
    places, refs = refs[:2], refs[2:]
    g_hidden, state, w_qkv, vectors, normed_one, d_qkv, d_out, bias_out, carry = refs[:9]
    near, far, input_grad, flat = refs[9:]
    flat[MLP_ROW : MLP_ROW + carry.shape[0], :] = carry[...]
    write_vector(flat, ROW["bias_attn_out"], bias_out[0:1, :])
    write_matrix(flat, ROW["w_attn_out"], d_out[...], D // LANES)
    query_sum = jnp.sum(d_qkv[:, :D].astype(f32), 0, keepdims=True)
    write_vector(flat, ROW["bias_query"], query_sum)
    value_sum = jnp.sum(d_qkv[:, 2 * D :].astype(f32), 0, keepdims=True)
    write_vector(flat, ROW["bias_value"], value_sum)
    d_normed = jnp.zeros((TOKENS, D), f32)
    for t in range(3):
        cols = slice(t * D, (t + 1) * D)
        part = d_qkv[:, cols]
        row = ROW["w_qkv"] + t * (D // LANES)
        write_matrix(flat, row, dot_tn(normed_one[...], part), 3 * D // LANES)
        d_normed += dot_nt(part, w_qkv[:, cols])
    unit, rstd = normalize(state[...])
    back, gain_grad, shift_grad = norm_back(d_normed, unit, rstd, vectors[0:1, :])
    write_vector(flat, ROW["ln1_gain"], gain_grad)
    write_vector(flat, ROW["ln1_shift"], shift_grad)
    total = g_hidden[...] + back
    if first:
        for image in range(MICRO):
            input_grad[image] = total[image * ROWS : image * ROWS + SEQ, :]
    else:
        input_grad[...] = total
    pack(flat, 0, rows_each, 0, places, near, far)


def adam(rows_each, *refs):
    offset, refs = refs[0], refs[1:]
    parts0, parts1, refs = refs[:4], refs[4:6], refs[6:]
    params, first_moment, second_moment, new_params, new_first, new_second = refs
    shape = (rows_each, LANES)
    row = lax.broadcasted_iota(jnp.int32, shape, 0)
    flags = matrix_flags((offset[0] + row) * LANES + lax.broadcasted_iota(jnp.int32, shape, 1))
    rate = jnp.where(flags, rate_matrix, rate_vector)
    decay = jnp.where(flags, decay_matrix, 0.0)
    for layer, parts in enumerate((parts0, parts1)):
        grads = sum(part[:rows_each, :].astype(f32) for part in parts)
        first = beta_one * first_moment[:, layer, :] + (1.0 - beta_one) * grads
        second = beta_two * second_moment[:, layer, :] + (1.0 - beta_two) * grads * grads
        new_first[:, layer, :] = first
        new_second[:, layer, :] = second
        first_hat = first / (1.0 - beta_one**STEP)
        second_hat = second / (1.0 - beta_two**STEP)
        old = params[:, layer, :]
        new_params[:, layer, :] = old - rate * (first_hat / (jnp.sqrt(second_hat) + adam_eps) + decay * old)


def call(body, name, inputs, outputs, scratch, scalars=0, flops=0):
    in_specs = [pl.BlockSpec(memory_space=pltpu.SMEM)] * scalars
    in_specs += [pl.BlockSpec(memory_space=pltpu.VMEM)] * (len(inputs) - scalars)
    shapes = [jax.ShapeDtypeStruct(shape, dtype) for shape, dtype in outputs]
    moved = sum(math.prod(s.shape) * s.dtype.itemsize for s in list(inputs) + shapes)
    return pl.pallas_call(
        body,
        name=name,
        out_shape=shapes,
        in_specs=in_specs,
        out_specs=[pl.BlockSpec(memory_space=pltpu.VMEM)] * len(shapes),
        scratch_shapes=scratch,
        compiler_params=pltpu.CompilerParams(vmem_limit_bytes=VMEM_LIMIT),
        cost_estimate=pl.CostEstimate(flops=flops // COST, bytes_accessed=moved // COST, transcendentals=0),
    )(*inputs)


def tie(values, *before):
    return lax.optimization_barrier((values, before))[0]


def together(*values):
    return lax.optimization_barrier(values)


def swap(values, size, mask):
    return lax.ppermute(values, "dp", [(i, i ^ mask) for i in range(size)])


def gather_masks(bits):
    chain = [1 << bit for bit in range(bits - 2, 2, -1)]
    return [chain + [2, 4, 1], chain + [4, 2, 1]]


def places(me, size, masks):
    relative = me ^ jnp.arange(size // 2, dtype=jnp.int32)
    place = jnp.zeros_like(relative)
    for digit, mask in enumerate(masks):
        place = place | jnp.where(relative & mask != 0, 1 << digit, 0)
    return place


def sent(part, size, mask):
    middle = part.shape[0] // 2
    return part[:middle], swap(part[middle:], size, mask)


def added(pair):
    return (pair[0].astype(f32) + pair[1].astype(f32)).astype(bf16)


def shards(size, images, cotangent, present, params, first_moment, second_moment):
    bits = size.bit_length() - 1
    width = params.shape[1]
    rows_each = width // LANES
    padded = round_up(rows_each, 16)
    half = size // 2
    me = lax.axis_index("dp")
    chain = [1 << bit for bit in range(bits - 2, 2, -1)]
    planes = [(2, 4), (4, 2)]
    place_low, place_high = [places(me, size, chain + [mask, 6 - mask, 1]) for mask in planes[0]]
    place_wide = places(me, size, [2, 4] + chain + [1])
    place = [places(me, size // 2, chain[1:] + [mask, 6 - mask, 1]) for mask in planes[0]]

    def alternating(value):
        return jnp.swapaxes(value.reshape(2, rows_each, LANES), 0, 1)

    is_low, is_first = (me >> (bits - 1)) & 1 == 0, (me >> (bits - 2)) & 1 == 0
    offset = me[None] * rows_each
    early = together(params, is_low, is_first, offset, place_low, place_high, place_wide, *place)
    params, is_low, is_first, offset, place_low, place_high, place_wide, *place = early
    compact = params.astype(bf16).reshape(2, rows_each, LANES)
    compact = jnp.pad(compact, ((0, 0), (0, padded - rows_each), (0, 0)))

    low_flat = pltpu.VMEM((-(-MLP_ROW // rows_each) * rows_each + padded, LANES), f32)
    begin = MLP_ROW // rows_each
    high_flat = pltpu.VMEM(((size - begin) * rows_each + padded, LANES), f32)
    square = TOKENS * D * D
    core_flops = 2 * 2 * MICRO * HEADS * ROWS * ROWS * HEAD_DIM

    def attend(first, places, low, state):
        outputs = [((TOKENS, D), f32)] if first else []
        outputs += [
            ((D, 3 * D), bf16),
            ((D, D), bf16),
            ((8, D), f32),
            ((TOKENS, D), bf16),
            ((TOKENS, 3 * D), bf16),
            ((MICRO * HEADS, ROWS, ROWS), bf16),
            ((TOKENS, D), bf16),
            ((TOKENS, D), f32),
        ]
        made = call(
            functools.partial(attention_forward, rows_each, first, len(places)),
            "attention_forward",
            [*places, *low, state],
            outputs,
            [low_flat],
            scalars=len(places),
            flops=8 * square + core_flops,
        )
        made = made if first else [state, *made]
        return made[:-1], made[-1]

    def lift(last, low_places, high_places, low, high, hidden):
        made = call(
            functools.partial(mlp_forward, rows_each, last, half, len(low_places)),
            "mlp_forward",
            [*low_places, *high_places, *low, *high, hidden],
            [
                ((D, FF), bf16),
                ((FF, D), bf16),
                ((8, D), f32),
                ((TOKENS, D), bf16),
                ((TOKENS, FF), bf16),
                ((TOKENS, FF), bf16),
                ((MICRO, SEQ, D) if last else (TOKENS, D), f32),
            ],
            [high_flat],
            scalars=2 * len(low_places),
            flops=16 * square,
        )
        return (hidden, *made[:-1]), made[-1]

    grads_shape = ((2, size // 8, padded, LANES), bf16)

    def lift_back(last, incoming, kept):
        scratch = [pltpu.VMEM((size * rows_each + padded - MLP_ROW, LANES), f32)]
        if last:
            scratch.append(pltpu.VMEM((TOKENS, D), f32))
        return call(
            functools.partial(mlp_backward, rows_each, last),
            "mlp_backward",
            ([present] if last else []) + [*place, incoming, *kept],
            [((carry_rows, LANES), f32), grads_shape, grads_shape, ((TOKENS, D), f32)],
            scratch,
            scalars=3 if last else 2,
            flops=32 * square,
        )

    def attend_back(g_hidden, kept):
        state, w_qkv, w_out, vectors, normed_one, qkv, probs, mixed = kept
        return call(
            attention_backward,
            "attention_backward",
            [g_hidden, w_out, qkv, probs, mixed],
            [((TOKENS, 3 * D), bf16), ((D, D), f32), ((8, D), f32)],
            [pltpu.VMEM((TOKENS, D), bf16)],
            flops=4 * square + 2 * core_flops,
        )

    def project_back(first, g_hidden, kept, *made):
        state, w_qkv, w_out, vectors, normed_one, qkv, probs, mixed = kept
        return call(
            functools.partial(projection_backward, rows_each, first),
            "projection_backward",
            [*place, g_hidden, state, w_qkv, vectors, normed_one, *made],
            [grads_shape, grads_shape, ((MICRO, SEQ, D) if first else (TOKENS, D), f32)],
            [pltpu.VMEM((MLP_ROW + carry_rows, LANES), f32)],
            scalars=2,
            flops=12 * square,
        )

    def top_gathered(shard, other):
        return jnp.stack([jnp.where(is_low, shard, other), jnp.where(is_low, other, shard)])[None]

    def exchanged(*values):
        return [swap(value, size, bits) for value, bits in zip(values, (size // 4, size // 2, size // 4 * 3))]

    def moved(parts, step):
        return [swap(part, size, mask) for part, mask in zip(parts, planes[step])]

    def joined(parts, received):
        return [jnp.concatenate(pair) for pair in zip(parts, received)]

    def chained(chunks):
        for mask in chain[:-1]:
            chunks = jnp.concatenate([chunks, swap(chunks, size, mask)])
        return chunks, swap(chunks, size, chain[-1])

    def halved(chunks, received):
        chunks = jnp.concatenate([chunks, received])
        return chunks[:, 0], chunks[:, 1]

    cut = padded - round_up(padded * 5 // 14, 16)
    row1, wide = compact[1, :cut], compact[1, cut:][None]
    nearby, other0, far_other0 = exchanged(compact[0], compact[0], compact[0])
    received = swap(wide, size, 2)
    row1, nearby, other0, far_other0, received = together(row1, nearby, other0, far_other0, received)
    wide = jnp.concatenate([wide, received])
    other1 = swap(row1, size, size // 2)
    received = swap(wide, size, 4)
    chunks0 = top_gathered(jnp.stack([compact[0], nearby]), jnp.stack([other0, far_other0]))[0]
    half0 = chunks0[0], chunks0[1]
    for mask in chain[1:]:
        half0 = [jnp.concatenate([part, swap(part, size, mask)]) for part in half0]
    received0 = moved(half0, 0)
    *received0, other1, received = together(*received0, other1, received)
    wide = jnp.concatenate([wide, received])
    half0 = joined(half0, received0)
    received0 = moved(half0, 1)
    half1 = halved(*chained(top_gathered(row1, other1)))
    received1 = moved(half1, 0)
    received = swap(wide, size, size // 2)
    *received0, received1[0], received1[1], received = together(*received0, *received1, received)
    near0 = joined(half0, received0)
    far0 = [swap(part, size, 1) for part in near0]
    half1 = joined(half1, received1)
    received1 = moved(half1, 1)
    wide = jnp.stack([jnp.where(is_low, wide, received), jnp.where(is_low, received, wide)], axis=1)
    wide, received = chained(wide)
    one0, hidden = attend(True, [place_low], [near0[0], far0[0]], images)
    hidden, *received1, received = together(hidden, *received1, received)
    near1 = joined(half1, received1)
    near1 = [part for pair in zip(near1, halved(wide, received)) for part in pair]
    far1 = [swap(part, size, 1) for part in near1]
    two0, state = lift(False, [place_low], [place_high], [near0[0], far0[0]], [near0[1], far0[1]], hidden)
    state, *far1 = together(state, *far1)
    both1 = [part for pair in zip(near1, far1) for part in pair]
    low1, high1 = both1[:4], both1[4:]
    one1, hidden = attend(False, [place_low, place_wide], low1, state)
    two1, outputs = lift(True, [place_low, place_wide], [place_high, place_wide], low1, high1, hidden)

    carry_rows = round_up(half * rows_each - MLP_ROW + padded - rows_each, 8)

    def to_plane(pairs, step):
        return [sent(added(pair), size, mask) for pair, mask in zip(pairs, planes[step])]

    def to_core(near, far):
        received = swap(far, size, 1)
        return [(near[quarter], received[quarter]) for quarter in range(2)]

    def along(pairs):
        parts = [added(pair) for pair in pairs]
        for mask in reversed(chain[1:]):
            parts = [added(sent(part, size, mask)) for part in parts]
        return parts

    def hold(pairs, *others):
        values = together(*[value for pair in pairs for value in pair], *others)
        count = 2 * len(pairs)
        return [values[i : i + 2] for i in range(0, count, 2)], *values[count:]

    def to_inner(low, high):
        kept = jnp.concatenate([jnp.where(is_first, *part) for part in (low, high)])
        given = jnp.concatenate([jnp.where(is_first, *part[::-1]) for part in (low, high)])
        return kept, swap(given, size, size // 4)

    def to_top(halves):
        kept = jnp.where(is_low, halves[0], halves[1])
        return kept, swap(jnp.where(is_low, halves[1], halves[0]), size, size // 2)

    carry, near, far, g_hidden = lift_back(True, cotangent, two1)
    high1 = to_core(near, far)
    made = attend_back(g_hidden, one1)
    high1, *made = hold(high1, *made)
    near, far, incoming = project_back(False, g_hidden, one1, *made, carry)
    high1 = to_plane(high1, 1)
    low1 = to_core(near, far)
    carry, near, far, g_hidden = lift_back(False, incoming, two0)
    held, g_hidden = hold(high1 + low1, g_hidden)
    high1, low1 = to_plane(held[:2], 0), to_plane(held[2:], 1)
    high0 = to_core(near, far)
    made = attend_back(g_hidden, one0)
    held, *made = hold(high1 + low1 + high0, *made)
    high1, low1, high0 = along(held[:2]), to_plane(held[2:4], 0), to_plane(held[4:], 1)
    near, far, input_grad = project_back(True, g_hidden, one0, *made, carry)
    low1, near, far = hold(low1, near, far)
    low0 = to_core(near, far)
    high0 = to_plane(high0, 0)
    inner1 = to_inner(along(low1), high1)
    low0, = hold(low0)
    low0 = to_plane(low0, 1)
    held, = hold(low0 + high0 + [to_top(added(inner1))])
    low0, high0, top1 = to_plane(held[:2], 0), along(held[2:4]), held[4]
    held, *high0, outputs, input_grad = hold(low0, *high0, outputs, input_grad)
    low0 = along(held)
    here, there = [jnp.where(is_low, *pair) for pair in zip(low0, high0)], [jnp.where(is_low, *pair) for pair in zip(high0, low0)]
    here, there = [[jnp.where(is_first, *pair), jnp.where(is_first, *pair[::-1])] for pair in (here, there)]
    values = exchanged(here[1][0], there[0][0], there[1][0])
    (nearby, other, far_other), received = values, top1[1]
    updated = call(
        functools.partial(adam, rows_each),
        "adam",
        [offset, here[0][0], nearby, other, far_other, top1[0], received, *map(alternating, (params, first_moment, second_moment))],
        [((rows_each, 2, LANES), f32)] * 3,
        [],
        scalars=1,
    )
    new_params, new_first, new_second = [
        jnp.swapaxes(value, 0, 1).reshape(2, width) for value in updated
    ]
    return (outputs, input_grad, new_params, new_first, new_second)


def solution(mesh):
    in_specs = (
        P("dp", None, None),
        P("dp", None, None),
        P("dp"),
        P(None, "dp"),
        P(None, "dp"),
        P(None, "dp"),
    )
    out_specs = (
        P("dp", None, None),
        P("dp", None, None),
        P(None, "dp"),
        P(None, "dp"),
        P(None, "dp"),
    )
    body = functools.partial(shards, mesh.shape["dp"])
    return jax.shard_map(body, mesh=mesh, in_specs=in_specs, out_specs=out_specs, check_vma=False)
```

```python
import functools
import math

import jax
import jax.numpy as jnp
from jax import lax
from jax.experimental import pallas as pl
from jax.experimental.pallas import tpu as pltpu
from jax.sharding import PartitionSpec as P

D = 384
FF = 1536
HEADS = 6
HEAD_DIM = 64
SEQ = 197
MICRO = 2
STEP = 10
P_SIZE = 1774080

LANES = 128
ROWS = 208
TOKENS = MICRO * ROWS
PAIRS = HEADS // 2
COST = 1
FORWARD_UNROLL = 6
BACKWARD_UNROLL = 2
VMEM_LIMIT = 10 * 1024 * 1024
BLOCK = 512

eps_norm = 1e-06
beta_one = 0.9
beta_two = 0.999
adam_eps = 1e-08
rate_matrix = 0.1
rate_vector = 0.5
decay_matrix = 0.05
sqrt_half = 0.7071067811865476
inverse_root_tau = 0.3989422804014327

f32 = jnp.float32
bf16 = jnp.bfloat16


def layout():
    return [
        ("ln1_gain", (D,)),
        ("ln1_shift", (D,)),
        ("w_qkv", (D, 3 * D)),
        ("bias_query", (D,)),
        ("bias_value", (D,)),
        ("w_attn_out", (D, D)),
        ("bias_attn_out", (D,)),
        ("ln2_gain", (D,)),
        ("ln2_shift", (D,)),
        ("w_lift", (D, FF)),
        ("bias_lift", (FF,)),
        ("w_drop", (FF, D)),
        ("bias_drop", (D,)),
    ]


def row_offsets():
    offsets, at = {}, 0
    for label, shape in layout():
        offsets[label] = at
        at += math.prod(shape) // LANES
    offsets["end"] = at
    return offsets


ROW = row_offsets()
MLP_ROW = ROW["ln2_gain"]


def matrix_flags(position):
    square = D * D
    lifted = D * FF
    bounds = [
        (2 * D, 2 * D + 3 * square),
        (4 * D + 3 * square, 4 * D + 4 * square),
        (7 * D + 4 * square, 7 * D + 4 * square + lifted),
        (7 * D + 4 * square + lifted + FF, 7 * D + 4 * square + 2 * lifted + FF),
    ]
    flags = jnp.zeros(position.shape, dtype=bool)
    for lower, upper in bounds:
        flags = flags | (position >= lower) & (position < upper)
    return flags


def round_up(value, step):
    return (value + step - 1) // step * step


def dot(a, b, dims):
    return lax.dot_general(a, b, ((dims[0], dims[1]), ((), ())), preferred_element_type=f32)


def dot_nn(a, b):
    return dot(a, b, ((1,), (0,)))


def dot_nt(a, b):
    return dot(a, b, ((1,), (1,)))


def dot_tn(a, b):
    return dot(a, b, ((0,), (0,)))


def read_vector(flat, row, count):
    parts = [flat[row + i : row + i + 1, :] for i in range(count)]
    return jnp.concatenate(parts, axis=1)


def write_vector(flat, row, values):
    for i in range(values.shape[1] // LANES):
        flat[row + i : row + i + 1, :] = values[:, i * LANES : (i + 1) * LANES]


def read_matrix(flat, row, out, depth, width):
    blocks = width // LANES
    for j in range(blocks):
        part = flat[pl.ds(row + j, depth, stride=blocks), :]
        out[:, j * LANES : (j + 1) * LANES] = part.astype(bf16)


def write_matrix(flat, row, values, blocks):
    depth, width = values.shape
    for j in range(width // LANES):
        flat[pl.ds(row + j, depth, stride=blocks), :] = values[:, j * LANES : (j + 1) * LANES]


def normalize(values):
    center = values - jnp.mean(values, -1, keepdims=True)
    rstd = lax.rsqrt(jnp.mean(center * center, -1, keepdims=True) + eps_norm)
    return center * rstd, rstd


def norm_back(incoming, unit, rstd, gain):
    scaled = incoming * gain
    inner = jnp.mean(scaled * unit, -1, keepdims=True)
    back = rstd * (scaled - jnp.mean(scaled, -1, keepdims=True) - unit * inner)
    gain_grad = jnp.sum(incoming * unit, 0, keepdims=True)
    return back, gain_grad, jnp.sum(incoming, 0, keepdims=True)


def head_mask(head):
    lane = lax.broadcasted_iota(jnp.int32, (1, LANES), 1)
    return lane < HEAD_DIM if head == 0 else lane >= HEAD_DIM


def pair_slices(step):
    image, pair = step // PAIRS, step % PAIRS
    rows = pl.ds(pl.multiple_of(image * ROWS, 16), ROWS)
    cols = [pl.ds(pl.multiple_of(t * D + pair * LANES, LANES), LANES) for t in range(3)]
    return rows, cols


def unpack(rows_each, base, chunks, parts, flat):
    def step(chunk, carry):
        begin = (chunks[2] + chunk) * rows_each - base
        for place, near, far in parts:
            count, padded = near.shape[0], near.shape[1]
            at = place[chunk]
            own = lax.rem(at, count)
            rows = jnp.where(at < count, near[own].astype(f32), far[own].astype(f32))
            flat[pl.ds(begin, padded), :] = rows
            begin = begin + padded
        return carry

    lax.fori_loop(chunks[0], chunks[1], step, 0)


def parts_of(places, refs):
    return [(place, refs[2 * i], refs[2 * i + 1]) for i, place in enumerate(places)], refs[2 * len(places) :]


def attention_forward(rows_each, first, count, *refs):
    parts, (state, *refs) = parts_of(refs[:count], refs[count:])
    if first:
        kept_state, refs = refs[0], refs[1:]
    w_qkv, w_out, vectors, normed_one, qkv, probs, mixed, hidden, flat = refs
    unpack(rows_each, 0, (0, -(-MLP_ROW // rows_each), 0), parts, flat)
    read_matrix(flat, ROW["w_qkv"], w_qkv, D, 3 * D)
    read_matrix(flat, ROW["w_attn_out"], w_out, D, D)
    labels = ["ln1_gain", "ln1_shift", "bias_query", "bias_value", "bias_attn_out"]
    for at, label in enumerate(labels):
        vectors[at : at + 1, :] = read_vector(flat, ROW[label], 3)
    gain, shift = vectors[0:1, :], vectors[1:2, :]
    if first:
        kept_state[...] = jnp.zeros_like(kept_state)
        for image in range(MICRO):
            kept_state[image * ROWS : image * ROWS + SEQ, :] = state[image].astype(f32)
        x = kept_state[...]
    else:
        x = state[...]
    unit, _ = normalize(x)
    normed_one[...] = (unit * gain + shift).astype(bf16)
    bias_query = vectors[2:3, :]
    bias = jnp.concatenate([bias_query, jnp.zeros_like(bias_query), vectors[3:4, :]], axis=1)
    for t in range(3):
        cols = slice(t * D, (t + 1) * D)
        product = dot_nn(normed_one[...], w_qkv[:, cols]) + bias[:, cols]
        qkv[:, cols] = product.astype(bf16)

    def step(at, carry):
        rows, cols = pair_slices(at)
        query, key_rows, value_rows = qkv[rows, cols[0]], qkv[rows, cols[1]], qkv[rows, cols[2]]
        real = lax.broadcasted_iota(jnp.int32, (ROWS, ROWS), 1) < SEQ
        sides = []
        for head in range(2):
            own_key = jnp.where(head_mask(head), key_rows, jnp.zeros_like(key_rows))
            raw = jnp.where(real, dot_nt(query, own_key), -1e30)
            powers = jnp.exp((raw - jnp.max(raw, -1, keepdims=True)) * HEAD_DIM ** (-0.5))
            weight = powers / jnp.sum(powers, -1, keepdims=True)
            weight = weight.astype(bf16)
            probs[at * 2 + head] = weight
            sides.append(dot_nn(weight, value_rows))
        mixed[rows, pl.ds(pl.multiple_of((at % PAIRS) * LANES, LANES), LANES)] = jnp.where(
            head_mask(0), sides[0], sides[1]
        ).astype(bf16)
        return carry

    lax.fori_loop(0, MICRO * PAIRS, step, 0, unroll=FORWARD_UNROLL)
    hidden[...] = x + dot_nn(mixed[...], w_out[...]) + vectors[4:5, :]


def mlp_forward(rows_each, last, half, count, *refs):
    low_places, high_places, refs = refs[:count], refs[count : 2 * count], refs[2 * count :]
    low, refs = parts_of(low_places, refs)
    high, (hidden, *refs) = parts_of(high_places, refs)
    w_lift, w_drop, vectors, normed_two, active, slope, result, flat = refs
    begin = MLP_ROW // rows_each
    base = begin * rows_each
    unpack(rows_each, base, (begin, half, 0), low, flat)
    unpack(rows_each, base, (0, half, half), high, flat)
    read_matrix(flat, ROW["w_lift"] - base, w_lift, D, FF)
    read_matrix(flat, ROW["w_drop"] - base, w_drop, FF, D)
    for at, label in enumerate(["ln2_gain", "ln2_shift", "bias_drop"]):
        vectors[at : at + 1, :] = read_vector(flat, ROW[label] - base, 3)
    bias_lift = read_vector(flat, ROW["bias_lift"] - base, FF // LANES)
    gain, shift = vectors[0:1, :], vectors[1:2, :]
    unit, _ = normalize(hidden[...])
    normed_two[...] = (unit * gain + shift).astype(bf16)
    total = hidden[...] + vectors[2:3, :]
    for at in range(0, FF, BLOCK):
        cols = slice(at, at + BLOCK)
        lifted = dot_nn(normed_two[...], w_lift[:, cols]) + bias_lift[:, cols]
        below = 0.5 * (1.0 + lax.erf(lifted * sqrt_half))
        active[:, cols] = (lifted * below).astype(bf16)
        bell = jnp.exp(-0.5 * lifted * lifted) * inverse_root_tau
        slope[:, cols] = (below + lifted * bell).astype(bf16)
        total += dot_nn(active[:, cols], w_drop[cols, :])
    if last:
        for image in range(MICRO):
            result[image] = total[image * ROWS : image * ROWS + SEQ, :]
    else:
        result[...] = total


def pack(flat, base, rows_each, first_chunk, places, near, far):
    count, padded = near.shape[1], near.shape[2]
    for quarter, place in enumerate(places):

        def step(chunk, carry):
            at = (first_chunk + quarter * 2 * count + chunk) * rows_each - base
            index = lax.rem(place[chunk], count)

            @pl.when(place[chunk] < count)
            def _():
                near[quarter, index] = flat[pl.ds(at, padded), :].astype(bf16)

            @pl.when(place[chunk] >= count)
            def _():
                far[quarter, index] = flat[pl.ds(at, padded), :].astype(bf16)

            return carry

        lax.fori_loop(0, 2 * count, step, 0)


def mlp_backward(rows_each, last, *refs):
    if last:
        present, refs = refs[0], refs[1:]
    places, refs = refs[:2], refs[2:]
    incoming, hidden, w_lift, w_drop, vectors, normed_two, active, slope = refs[:8]
    refs = refs[8:]
    carry, near, far, g_hidden, flat = refs[:5]
    count = 4 * near.shape[1]
    if last:
        kept = refs[5]
        kept[...] = jnp.zeros_like(kept)
        for image in range(MICRO):
            seed = incoming[image].astype(f32) * present[image].astype(f32)
            kept[image * ROWS : image * ROWS + SEQ, :] = seed
        g = kept[...]
    else:
        g = incoming[...]
    base = MLP_ROW
    end = ROW["end"] - base
    flat[end:, :] = jnp.zeros((flat.shape[0] - end, LANES), f32)
    g_out = g.astype(bf16)
    write_vector(flat, ROW["bias_drop"] - base, jnp.sum(g_out.astype(f32), 0, keepdims=True))
    d_normed = jnp.zeros((TOKENS, D), f32)
    for at in range(0, FF, BLOCK):
        cols = slice(at, at + BLOCK)
        row = ROW["w_drop"] - base + at * (D // LANES)
        write_matrix(flat, row, dot_tn(active[:, cols], g_out), D // LANES)
        d_lifted = (dot_nt(g_out, w_drop[cols, :]) * slope[:, cols].astype(f32)).astype(bf16)
        row = ROW["bias_lift"] - base + at // LANES
        write_vector(flat, row, jnp.sum(d_lifted.astype(f32), 0, keepdims=True))
        row = ROW["w_lift"] - base + at // LANES
        write_matrix(flat, row, dot_tn(normed_two[...], d_lifted), FF // LANES)
        d_normed += dot_nt(d_lifted, w_lift[:, cols])
    unit, rstd = normalize(hidden[...])
    back, gain_grad, shift_grad = norm_back(d_normed, unit, rstd, vectors[0:1, :])
    write_vector(flat, ROW["ln2_gain"] - base, gain_grad)
    write_vector(flat, ROW["ln2_shift"] - base, shift_grad)
    g_hidden[...] = g + back
    carry[...] = flat[: carry.shape[0], :]
    pack(flat, base, rows_each, count, places, near, far)


def attention_backward(g_hidden, w_out, qkv, probs, mixed, d_qkv, d_out, bias_out, d_mixed):
    g_att = g_hidden[...].astype(bf16)
    bias_out[...] = jnp.broadcast_to(jnp.sum(g_att.astype(f32), 0, keepdims=True), bias_out.shape)
    d_out[...] = dot_tn(mixed[...], g_att)
    d_mixed[...] = dot_nt(g_att, w_out[...]).astype(bf16)

    def step(at, carried):
        rows, cols = pair_slices(at)
        query, key_rows, value_rows = qkv[rows, cols[0]], qkv[rows, cols[1]], qkv[rows, cols[2]]
        mixed_grad = d_mixed[rows, pl.ds(pl.multiple_of((at % PAIRS) * LANES, LANES), LANES)]
        d_query, d_key, d_value = [], [], []
        for head in range(2):
            own = jnp.where(head_mask(head), mixed_grad, jnp.zeros_like(mixed_grad))
            weight = probs[at * 2 + head]
            d_value.append(dot_tn(weight, mixed_grad))
            weight = weight.astype(f32)
            d_probs = dot_nt(own, value_rows)
            inner = jnp.sum(weight * d_probs, -1, keepdims=True)
            d_scores = (weight * (d_probs - inner)).astype(bf16)
            d_query.append(dot_nn(d_scores, key_rows))
            d_key.append(dot_tn(d_scores, query))
        scale = HEAD_DIM ** (-0.5)
        mask = head_mask(0)
        d_qkv[rows, cols[0]] = (jnp.where(mask, d_query[0], d_query[1]) * scale).astype(bf16)
        d_qkv[rows, cols[1]] = (jnp.where(mask, d_key[0], d_key[1]) * scale).astype(bf16)
        d_qkv[rows, cols[2]] = jnp.where(mask, d_value[0], d_value[1]).astype(bf16)
        return carried

    lax.fori_loop(0, MICRO * PAIRS, step, 0, unroll=BACKWARD_UNROLL)

def projection_backward(rows_each, first, *refs):
    places, refs = refs[:2], refs[2:]
    g_hidden, state, w_qkv, vectors, normed_one, d_qkv, d_out, bias_out, carry = refs[:9]
    near, far, input_grad, flat = refs[9:]
    flat[MLP_ROW : MLP_ROW + carry.shape[0], :] = carry[...]
    write_vector(flat, ROW["bias_attn_out"], bias_out[0:1, :])
    write_matrix(flat, ROW["w_attn_out"], d_out[...], D // LANES)
    query_sum = jnp.sum(d_qkv[:, :D].astype(f32), 0, keepdims=True)
    write_vector(flat, ROW["bias_query"], query_sum)
    value_sum = jnp.sum(d_qkv[:, 2 * D :].astype(f32), 0, keepdims=True)
    write_vector(flat, ROW["bias_value"], value_sum)
    d_normed = jnp.zeros((TOKENS, D), f32)
    for t in range(3):
        cols = slice(t * D, (t + 1) * D)
        part = d_qkv[:, cols]
        row = ROW["w_qkv"] + t * (D // LANES)
        write_matrix(flat, row, dot_tn(normed_one[...], part), 3 * D // LANES)
        d_normed += dot_nt(part, w_qkv[:, cols])
    unit, rstd = normalize(state[...])
    back, gain_grad, shift_grad = norm_back(d_normed, unit, rstd, vectors[0:1, :])
    write_vector(flat, ROW["ln1_gain"], gain_grad)
    write_vector(flat, ROW["ln1_shift"], shift_grad)
    total = g_hidden[...] + back
    if first:
        for image in range(MICRO):
            input_grad[image] = total[image * ROWS : image * ROWS + SEQ, :]
    else:
        input_grad[...] = total
    pack(flat, 0, rows_each, 0, places, near, far)


def updated(offset, grads, params, first_moment, second_moment):
    shape = grads.shape
    row = lax.broadcasted_iota(jnp.int32, shape, 0)
    flags = matrix_flags((offset[0] + row) * LANES + lax.broadcasted_iota(jnp.int32, shape, 1))
    rate = jnp.where(flags, rate_matrix, rate_vector)
    decay = jnp.where(flags, decay_matrix, 0.0)
    first = beta_one * first_moment + (1.0 - beta_one) * grads
    second = beta_two * second_moment + (1.0 - beta_two) * grads * grads
    first_hat = first / (1.0 - beta_one**STEP)
    second_hat = second / (1.0 - beta_two**STEP)
    moved = rate * (first_hat / (jnp.sqrt(second_hat) + adam_eps) + decay * params)
    return params - moved, first, second


def adam_early(rows_each, offset, kept, received, *refs):
    old, new1, old0 = refs[:3], refs[3:6], refs[6:9]
    grads = kept[:rows_each, :].astype(f32) + received[:rows_each, :].astype(f32)
    for out, value in zip(new1, updated(offset, grads, *[ref[:, 1, :] for ref in old])):
        out[...] = value
    for out, ref in zip(old0, old):
        out[...] = ref[:, 0, :]


def adam_late(rows_each, offset, *refs):
    parts, new1, old0, new = refs[:4], refs[4:7], refs[7:10], refs[10:13]
    grads = sum(part[:rows_each, :].astype(f32) for part in parts)
    for out, value in zip(new, updated(offset, grads, *[ref[...] for ref in old0])):
        out[:, 0, :] = value
    for out, ref in zip(new, new1):
        out[:, 1, :] = ref[...]


def call(body, name, inputs, outputs, scratch, scalars=0, flops=0):
    in_specs = [pl.BlockSpec(memory_space=pltpu.SMEM)] * scalars
    in_specs += [pl.BlockSpec(memory_space=pltpu.VMEM)] * (len(inputs) - scalars)
    shapes = [jax.ShapeDtypeStruct(shape, dtype) for shape, dtype in outputs]
    moved = sum(math.prod(s.shape) * s.dtype.itemsize for s in list(inputs) + shapes)
    return pl.pallas_call(
        body,
        name=name,
        out_shape=shapes,
        in_specs=in_specs,
        out_specs=[pl.BlockSpec(memory_space=pltpu.VMEM)] * len(shapes),
        scratch_shapes=scratch,
        compiler_params=pltpu.CompilerParams(vmem_limit_bytes=VMEM_LIMIT),
        cost_estimate=pl.CostEstimate(flops=flops // COST, bytes_accessed=moved // COST, transcendentals=0),
    )(*inputs)


def tie(values, *before):
    return lax.optimization_barrier((values, before))[0]


def together(*values):
    return lax.optimization_barrier(values)


def swap(values, size, mask):
    return lax.ppermute(values, "dp", [(i, i ^ mask) for i in range(size)])


def gather_masks(bits):
    chain = [1 << bit for bit in range(bits - 2, 2, -1)]
    return [chain + [2, 4, 1], chain + [4, 2, 1]]


def places(me, size, masks):
    relative = me ^ jnp.arange(size // 2, dtype=jnp.int32)
    place = jnp.zeros_like(relative)
    for digit, mask in enumerate(masks):
        place = place | jnp.where(relative & mask != 0, 1 << digit, 0)
    return place


def sent(part, size, mask):
    middle = part.shape[0] // 2
    return part[:middle], swap(part[middle:], size, mask)


def added(pair):
    return (pair[0].astype(f32) + pair[1].astype(f32)).astype(bf16)


def shards(size, images, cotangent, present, params, first_moment, second_moment):
    bits = size.bit_length() - 1
    width = params.shape[1]
    rows_each = width // LANES
    padded = round_up(rows_each, 16)
    half = size // 2
    me = lax.axis_index("dp")
    chain = [1 << bit for bit in range(bits - 2, 2, -1)]
    planes = [(2, 4), (4, 2)]
    place_low, place_high = [places(me, size, chain + [mask, 6 - mask, 1]) for mask in planes[0]]
    place_wide = places(me, size, [2, 4] + chain + [1])
    place = [places(me, size // 2, chain[1:] + [mask, 6 - mask, 1]) for mask in planes[0]]

    def alternating(value):
        return jnp.swapaxes(value.reshape(2, rows_each, LANES), 0, 1)

    is_low, is_first = (me >> (bits - 1)) & 1 == 0, (me >> (bits - 2)) & 1 == 0
    offset = me[None] * rows_each
    early = together(params, is_low, is_first, offset, place_low, place_high, place_wide, *place)
    params, is_low, is_first, offset, place_low, place_high, place_wide, *place = early
    compact = params.astype(bf16).reshape(2, rows_each, LANES)
    compact = jnp.pad(compact, ((0, 0), (0, padded - rows_each), (0, 0)))

    low_flat = pltpu.VMEM((-(-MLP_ROW // rows_each) * rows_each + padded, LANES), f32)
    begin = MLP_ROW // rows_each
    high_flat = pltpu.VMEM(((size - begin) * rows_each + padded, LANES), f32)
    square = TOKENS * D * D
    core_flops = 2 * 2 * MICRO * HEADS * ROWS * ROWS * HEAD_DIM

    def attend(first, places, low, state):
        outputs = [((TOKENS, D), f32)] if first else []
        outputs += [
            ((D, 3 * D), bf16),
            ((D, D), bf16),
            ((8, D), f32),
            ((TOKENS, D), bf16),
            ((TOKENS, 3 * D), bf16),
            ((MICRO * HEADS, ROWS, ROWS), bf16),
            ((TOKENS, D), bf16),
            ((TOKENS, D), f32),
        ]
        made = call(
            functools.partial(attention_forward, rows_each, first, len(places)),
            "attention_forward",
            [*places, *low, state],
            outputs,
            [low_flat],
            scalars=len(places),
            flops=8 * square + core_flops,
        )
        made = made if first else [state, *made]
        return made[:-1], made[-1]

    def lift(last, low_places, high_places, low, high, hidden):
        made = call(
            functools.partial(mlp_forward, rows_each, last, half, len(low_places)),
            "mlp_forward",
            [*low_places, *high_places, *low, *high, hidden],
            [
                ((D, FF), bf16),
                ((FF, D), bf16),
                ((8, D), f32),
                ((TOKENS, D), bf16),
                ((TOKENS, FF), bf16),
                ((TOKENS, FF), bf16),
                ((MICRO, SEQ, D) if last else (TOKENS, D), f32),
            ],
            [high_flat],
            scalars=2 * len(low_places),
            flops=16 * square,
        )
        return (hidden, *made[:-1]), made[-1]

    grads_shape = ((2, size // 8, padded, LANES), bf16)

    def lift_back(last, incoming, kept):
        scratch = [pltpu.VMEM((size * rows_each + padded - MLP_ROW, LANES), f32)]
        if last:
            scratch.append(pltpu.VMEM((TOKENS, D), f32))
        return call(
            functools.partial(mlp_backward, rows_each, last),
            "mlp_backward",
            ([present] if last else []) + [*place, incoming, *kept],
            [((carry_rows, LANES), f32), grads_shape, grads_shape, ((TOKENS, D), f32)],
            scratch,
            scalars=3 if last else 2,
            flops=32 * square,
        )

    def attend_back(g_hidden, kept):
        state, w_qkv, w_out, vectors, normed_one, qkv, probs, mixed = kept
        return call(
            attention_backward,
            "attention_backward",
            [g_hidden, w_out, qkv, probs, mixed],
            [((TOKENS, 3 * D), bf16), ((D, D), f32), ((8, D), f32)],
            [pltpu.VMEM((TOKENS, D), bf16)],
            flops=4 * square + 2 * core_flops,
        )

    def project_back(first, g_hidden, kept, *made):
        state, w_qkv, w_out, vectors, normed_one, qkv, probs, mixed = kept
        return call(
            functools.partial(projection_backward, rows_each, first),
            "projection_backward",
            [*place, g_hidden, state, w_qkv, vectors, normed_one, *made],
            [grads_shape, grads_shape, ((MICRO, SEQ, D) if first else (TOKENS, D), f32)],
            [pltpu.VMEM((MLP_ROW + carry_rows, LANES), f32)],
            scalars=2,
            flops=12 * square,
        )

    def top_gathered(shard, other):
        return jnp.stack([jnp.where(is_low, shard, other), jnp.where(is_low, other, shard)])[None]

    def exchanged(*values):
        return [swap(value, size, bits) for value, bits in zip(values, (size // 4, size // 2, size // 4 * 3))]

    def moved(parts, step):
        return [swap(part, size, mask) for part, mask in zip(parts, planes[step])]

    def joined(parts, received):
        return [jnp.concatenate(pair) for pair in zip(parts, received)]

    def chained(chunks):
        for mask in chain[:-1]:
            chunks = jnp.concatenate([chunks, swap(chunks, size, mask)])
        return chunks, swap(chunks, size, chain[-1])

    def halved(chunks, received):
        chunks = jnp.concatenate([chunks, received])
        return chunks[:, 0], chunks[:, 1]

    cut = padded - round_up(padded * 5 // 14, 16)
    row1, wide = compact[1, :cut], compact[1, cut:][None]
    nearby, other0, far_other0 = exchanged(compact[0], compact[0], compact[0])
    received = swap(wide, size, 2)
    row1, nearby, other0, far_other0, received = together(row1, nearby, other0, far_other0, received)
    wide = jnp.concatenate([wide, received])
    other1 = swap(row1, size, size // 2)
    received = swap(wide, size, 4)
    chunks0 = top_gathered(jnp.stack([compact[0], nearby]), jnp.stack([other0, far_other0]))[0]
    half0 = chunks0[0], chunks0[1]
    for mask in chain[1:]:
        half0 = [jnp.concatenate([part, swap(part, size, mask)]) for part in half0]
    received0 = moved(half0, 0)
    *received0, other1, received = together(*received0, other1, received)
    wide = jnp.concatenate([wide, received])
    half0 = joined(half0, received0)
    received0 = moved(half0, 1)
    half1 = halved(*chained(top_gathered(row1, other1)))
    received1 = moved(half1, 0)
    received = swap(wide, size, size // 2)
    *received0, received1[0], received1[1], received = together(*received0, *received1, received)
    near0 = joined(half0, received0)
    far0 = [swap(part, size, 1) for part in near0]
    half1 = joined(half1, received1)
    received1 = moved(half1, 1)
    wide = jnp.stack([jnp.where(is_low, wide, received), jnp.where(is_low, received, wide)], axis=1)
    wide, received = chained(wide)
    one0, hidden = attend(True, [place_low], [near0[0], far0[0]], images)
    hidden, *received1, received = together(hidden, *received1, received)
    near1 = joined(half1, received1)
    near1 = [part for pair in zip(near1, halved(wide, received)) for part in pair]
    far1 = [swap(part, size, 1) for part in near1]
    two0, state = lift(False, [place_low], [place_high], [near0[0], far0[0]], [near0[1], far0[1]], hidden)
    state, *far1 = together(state, *far1)
    both1 = [part for pair in zip(near1, far1) for part in pair]
    low1, high1 = both1[:4], both1[4:]
    one1, hidden = attend(False, [place_low, place_wide], low1, state)
    two1, outputs = lift(True, [place_low, place_wide], [place_high, place_wide], low1, high1, hidden)

    carry_rows = round_up(half * rows_each - MLP_ROW + padded - rows_each, 8)

    def to_plane(pairs, step):
        return [sent(added(pair), size, mask) for pair, mask in zip(pairs, planes[step])]

    def to_core(near, far):
        received = swap(far, size, 1)
        return [(near[quarter], received[quarter]) for quarter in range(2)]

    def along(pairs):
        parts = [added(pair) for pair in pairs]
        for mask in reversed(chain[1:]):
            parts = [added(sent(part, size, mask)) for part in parts]
        return parts

    def hold(pairs, *others):
        values = together(*[value for pair in pairs for value in pair], *others)
        count = 2 * len(pairs)
        return [values[i : i + 2] for i in range(0, count, 2)], *values[count:]

    def to_inner(low, high):
        kept = jnp.concatenate([jnp.where(is_first, *part) for part in (low, high)])
        given = jnp.concatenate([jnp.where(is_first, *part[::-1]) for part in (low, high)])
        return kept, swap(given, size, size // 4)

    def to_top(halves):
        kept = jnp.where(is_low, halves[0], halves[1])
        return kept, swap(jnp.where(is_low, halves[1], halves[0]), size, size // 2)

    carry, near, far, g_hidden = lift_back(True, cotangent, two1)
    high1 = to_core(near, far)
    made = attend_back(g_hidden, one1)
    high1, *made = hold(high1, *made)
    near, far, incoming = project_back(False, g_hidden, one1, *made, carry)
    high1 = to_plane(high1, 1)
    low1 = to_core(near, far)
    carry, near, far, g_hidden = lift_back(False, incoming, two0)
    held, g_hidden = hold(high1 + low1, g_hidden)
    high1, low1 = to_plane(held[:2], 0), to_plane(held[2:], 1)
    high0 = to_core(near, far)
    made = attend_back(g_hidden, one0)
    held, *made = hold(high1 + low1 + high0, *made)
    high1, low1, high0 = along(held[:2]), to_plane(held[2:4], 0), to_plane(held[4:], 1)
    near, far, input_grad = project_back(True, g_hidden, one0, *made, carry)
    low1, near, far = hold(low1, near, far)
    low0 = to_core(near, far)
    high0 = to_plane(high0, 0)
    inner1 = to_inner(along(low1), high1)
    low0, = hold(low0)
    low0 = to_plane(low0, 1)
    held, = hold(low0 + high0 + [to_top(added(inner1))])
    low0, high0, top1 = to_plane(held[:2], 0), along(held[2:4]), held[4]
    held, *high0, outputs, input_grad = hold(low0, *high0, outputs, input_grad)
    low0 = along(held)
    here, there = [jnp.where(is_low, *pair) for pair in zip(low0, high0)], [jnp.where(is_low, *pair) for pair in zip(high0, low0)]
    here, there = [[jnp.where(is_first, *pair), jnp.where(is_first, *pair[::-1])] for pair in (here, there)]
    values = exchanged(here[1][0], there[0][0], there[1][0])
    (nearby, other, far_other), received = values, top1[1]
    early = call(
        functools.partial(adam_early, rows_each),
        "adam_early",
        [offset, top1[0], received, *map(alternating, (params, first_moment, second_moment))],
        [((rows_each, LANES), f32)] * 6,
        [],
        scalars=1,
    )
    nearby, other, far_other, *early = together(nearby, other, far_other, *early)
    results = call(
        functools.partial(adam_late, rows_each),
        "adam_late",
        [offset, here[0][0], nearby, other, far_other, *early],
        [((rows_each, 2, LANES), f32)] * 3,
        [],
        scalars=1,
    )
    new_params, new_first, new_second = [
        jnp.swapaxes(value, 0, 1).reshape(2, width) for value in results
    ]
    return (outputs, input_grad, new_params, new_first, new_second)


def solution(mesh):
    in_specs = (
        P("dp", None, None),
        P("dp", None, None),
        P("dp"),
        P(None, "dp"),
        P(None, "dp"),
        P(None, "dp"),
    )
    out_specs = (
        P("dp", None, None),
        P("dp", None, None),
        P(None, "dp"),
        P(None, "dp"),
        P(None, "dp"),
    )
    body = functools.partial(shards, mesh.shape["dp"])
    return jax.shard_map(body, mesh=mesh, in_specs=in_specs, out_specs=out_specs, check_vma=False)
```

```python
import functools
import math

import jax
import jax.numpy as jnp
from jax import lax
from jax.experimental import pallas as pl
from jax.experimental.pallas import tpu as pltpu
from jax.sharding import PartitionSpec as P

D = 384
FF = 1536
HEADS = 6
HEAD_DIM = 64
SEQ = 197
MICRO = 2
STEP = 10
P_SIZE = 1774080

LANES = 128
ROWS = 208
TOKENS = MICRO * ROWS
PAIRS = HEADS // 2
COST = 1
FORWARD_UNROLL = 6
BACKWARD_UNROLL = 3
VMEM_LIMIT = 14 * 1024 * 1024
BLOCK = 768

eps_norm = 1e-06
beta_one = 0.9
beta_two = 0.999
adam_eps = 1e-08
rate_matrix = 0.1
rate_vector = 0.5
decay_matrix = 0.05
sqrt_half = 0.7071067811865476
inverse_root_tau = 0.3989422804014327

f32 = jnp.float32
bf16 = jnp.bfloat16


def layout():
    return [
        ("ln1_gain", (D,)),
        ("ln1_shift", (D,)),
        ("w_qkv", (D, 3 * D)),
        ("bias_query", (D,)),
        ("bias_value", (D,)),
        ("w_attn_out", (D, D)),
        ("bias_attn_out", (D,)),
        ("ln2_gain", (D,)),
        ("ln2_shift", (D,)),
        ("w_lift", (D, FF)),
        ("bias_lift", (FF,)),
        ("w_drop", (FF, D)),
        ("bias_drop", (D,)),
    ]


def row_offsets():
    offsets, at = {}, 0
    for label, shape in layout():
        offsets[label] = at
        at += math.prod(shape) // LANES
    offsets["end"] = at
    return offsets


ROW = row_offsets()
MLP_ROW = ROW["ln2_gain"]


def matrix_flags(position):
    square = D * D
    lifted = D * FF
    bounds = [
        (2 * D, 2 * D + 3 * square),
        (4 * D + 3 * square, 4 * D + 4 * square),
        (7 * D + 4 * square, 7 * D + 4 * square + lifted),
        (7 * D + 4 * square + lifted + FF, 7 * D + 4 * square + 2 * lifted + FF),
    ]
    flags = jnp.zeros(position.shape, dtype=bool)
    for lower, upper in bounds:
        flags = flags | (position >= lower) & (position < upper)
    return flags


def round_up(value, step):
    return (value + step - 1) // step * step


def dot(a, b, dims):
    return lax.dot_general(a, b, ((dims[0], dims[1]), ((), ())), preferred_element_type=f32)


def dot_nn(a, b):
    return dot(a, b, ((1,), (0,)))


def dot_nt(a, b):
    return dot(a, b, ((1,), (1,)))


def dot_tn(a, b):
    return dot(a, b, ((0,), (0,)))


def read_vector(flat, row, count):
    parts = [flat[row + i : row + i + 1, :] for i in range(count)]
    return jnp.concatenate(parts, axis=1)


def write_vector(flat, row, values):
    for i in range(values.shape[1] // LANES):
        flat[row + i : row + i + 1, :] = values[:, i * LANES : (i + 1) * LANES]


def read_matrix(flat, row, out, depth, width):
    blocks = width // LANES
    for j in range(blocks):
        part = flat[pl.ds(row + j, depth, stride=blocks), :]
        out[:, j * LANES : (j + 1) * LANES] = part.astype(bf16)


def write_matrix(flat, row, values, blocks):
    depth, width = values.shape
    for j in range(width // LANES):
        flat[pl.ds(row + j, depth, stride=blocks), :] = values[:, j * LANES : (j + 1) * LANES]


def normalize(values):
    center = values - jnp.mean(values, -1, keepdims=True)
    rstd = lax.rsqrt(jnp.mean(center * center, -1, keepdims=True) + eps_norm)
    return center * rstd, rstd


def norm_back(incoming, unit, rstd, gain):
    scaled = incoming * gain
    inner = jnp.mean(scaled * unit, -1, keepdims=True)
    back = rstd * (scaled - jnp.mean(scaled, -1, keepdims=True) - unit * inner)
    gain_grad = jnp.sum(incoming * unit, 0, keepdims=True)
    return back, gain_grad, jnp.sum(incoming, 0, keepdims=True)


def head_mask(head):
    lane = lax.broadcasted_iota(jnp.int32, (1, LANES), 1)
    return lane < HEAD_DIM if head == 0 else lane >= HEAD_DIM


def pair_slices(step):
    image, pair = step // PAIRS, step % PAIRS
    rows = pl.ds(pl.multiple_of(image * ROWS, 16), ROWS)
    cols = [pl.ds(pl.multiple_of(t * D + pair * LANES, LANES), LANES) for t in range(3)]
    return rows, cols


def unpack(rows_each, base, chunks, parts, flat):
    def step(chunk, carry):
        begin = (chunks[2] + chunk) * rows_each - base
        for place, near, far in parts:
            count, padded = near.shape[0], near.shape[1]
            at = place[chunk]
            own = lax.rem(at, count)
            rows = jnp.where(at < count, near[own].astype(f32), far[own].astype(f32))
            flat[pl.ds(begin, padded), :] = rows
            begin = begin + padded
        return carry

    lax.fori_loop(chunks[0], chunks[1], step, 0)


def parts_of(places, refs):
    return [(place, refs[2 * i], refs[2 * i + 1]) for i, place in enumerate(places)], refs[2 * len(places) :]


def attention_forward(rows_each, first, count, *refs):
    parts, (state, *refs) = parts_of(refs[:count], refs[count:])
    if first:
        kept_state, refs = refs[0], refs[1:]
    w_qkv, w_out, vectors, normed_one, qkv, probs, mixed, hidden, flat = refs
    unpack(rows_each, 0, (0, -(-MLP_ROW // rows_each), 0), parts, flat)
    read_matrix(flat, ROW["w_qkv"], w_qkv, D, 3 * D)
    read_matrix(flat, ROW["w_attn_out"], w_out, D, D)
    labels = ["ln1_gain", "ln1_shift", "bias_query", "bias_value", "bias_attn_out"]
    for at, label in enumerate(labels):
        vectors[at : at + 1, :] = read_vector(flat, ROW[label], 3)
    gain, shift = vectors[0:1, :], vectors[1:2, :]
    if first:
        kept_state[...] = jnp.zeros_like(kept_state)
        for image in range(MICRO):
            kept_state[image * ROWS : image * ROWS + SEQ, :] = state[image].astype(f32)
        x = kept_state[...]
    else:
        x = state[...]
    unit, _ = normalize(x)
    normed_one[...] = (unit * gain + shift).astype(bf16)
    bias_query = vectors[2:3, :]
    bias = jnp.concatenate([bias_query, jnp.zeros_like(bias_query), vectors[3:4, :]], axis=1)
    qkv[...] = (dot_nn(normed_one[...], w_qkv[...]) + bias).astype(bf16)

    def step(at, carry):
        rows, cols = pair_slices(at)
        query, key_rows, value_rows = qkv[rows, cols[0]], qkv[rows, cols[1]], qkv[rows, cols[2]]
        real = lax.broadcasted_iota(jnp.int32, (ROWS, ROWS), 1) < SEQ
        sides = []
        for head in range(2):
            own_key = jnp.where(head_mask(head), key_rows, jnp.zeros_like(key_rows))
            raw = jnp.where(real, dot_nt(query, own_key), -1e30)
            powers = jnp.exp((raw - jnp.max(raw, -1, keepdims=True)) * HEAD_DIM ** (-0.5))
            weight = powers / jnp.sum(powers, -1, keepdims=True)
            weight = weight.astype(bf16)
            probs[at * 2 + head] = weight
            sides.append(dot_nn(weight, value_rows))
        mixed[rows, pl.ds(pl.multiple_of((at % PAIRS) * LANES, LANES), LANES)] = jnp.where(
            head_mask(0), sides[0], sides[1]
        ).astype(bf16)
        return carry

    lax.fori_loop(0, MICRO * PAIRS, step, 0, unroll=FORWARD_UNROLL)
    hidden[...] = x + dot_nn(mixed[...], w_out[...]) + vectors[4:5, :]


def mlp_forward(rows_each, last, half, count, *refs):
    low_places, high_places, refs = refs[:count], refs[count : 2 * count], refs[2 * count :]
    low, refs = parts_of(low_places, refs)
    high, (hidden, *refs) = parts_of(high_places, refs)
    w_lift, w_drop, vectors, normed_two, active, slope, result, flat = refs
    begin = MLP_ROW // rows_each
    base = begin * rows_each
    unpack(rows_each, base, (begin, half, 0), low, flat)
    unpack(rows_each, base, (0, half, half), high, flat)
    read_matrix(flat, ROW["w_lift"] - base, w_lift, D, FF)
    read_matrix(flat, ROW["w_drop"] - base, w_drop, FF, D)
    for at, label in enumerate(["ln2_gain", "ln2_shift", "bias_drop"]):
        vectors[at : at + 1, :] = read_vector(flat, ROW[label] - base, 3)
    bias_lift = read_vector(flat, ROW["bias_lift"] - base, FF // LANES)
    gain, shift = vectors[0:1, :], vectors[1:2, :]
    unit, _ = normalize(hidden[...])
    normed_two[...] = (unit * gain + shift).astype(bf16)
    total = hidden[...] + vectors[2:3, :]
    for at in range(0, FF, BLOCK):
        cols = slice(at, at + BLOCK)
        lifted = dot_nn(normed_two[...], w_lift[:, cols]) + bias_lift[:, cols]
        below = 0.5 * (1.0 + lax.erf(lifted * sqrt_half))
        active[:, cols] = (lifted * below).astype(bf16)
        bell = jnp.exp(-0.5 * lifted * lifted) * inverse_root_tau
        slope[:, cols] = (below + lifted * bell).astype(bf16)
        total += dot_nn(active[:, cols], w_drop[cols, :])
    if last:
        for image in range(MICRO):
            result[image] = total[image * ROWS : image * ROWS + SEQ, :]
    else:
        result[...] = total


def pack(flat, base, rows_each, first_chunk, places, near, far):
    count, padded = near.shape[1], near.shape[2]
    for quarter, place in enumerate(places):

        def step(chunk, carry):
            at = (first_chunk + quarter * 2 * count + chunk) * rows_each - base
            index = lax.rem(place[chunk], count)

            @pl.when(place[chunk] < count)
            def _():
                near[quarter, index] = flat[pl.ds(at, padded), :].astype(bf16)

            @pl.when(place[chunk] >= count)
            def _():
                far[quarter, index] = flat[pl.ds(at, padded), :].astype(bf16)

            return carry

        lax.fori_loop(0, 2 * count, step, 0)


def mlp_backward(rows_each, last, *refs):
    if last:
        present, refs = refs[0], refs[1:]
    places, refs = refs[:2], refs[2:]
    incoming, hidden, w_lift, w_drop, vectors, normed_two, active, slope = refs[:8]
    refs = refs[8:]
    carry, near, far, g_hidden, flat = refs[:5]
    count = 4 * near.shape[1]
    if last:
        kept = refs[5]
        kept[...] = jnp.zeros_like(kept)
        for image in range(MICRO):
            seed = incoming[image].astype(f32) * present[image].astype(f32)
            kept[image * ROWS : image * ROWS + SEQ, :] = seed
        g = kept[...]
    else:
        g = incoming[...]
    base = MLP_ROW
    end = ROW["end"] - base
    flat[end:, :] = jnp.zeros((flat.shape[0] - end, LANES), f32)
    g_out = g.astype(bf16)
    write_vector(flat, ROW["bias_drop"] - base, jnp.sum(g_out.astype(f32), 0, keepdims=True))
    d_normed = jnp.zeros((TOKENS, D), f32)
    for at in range(0, FF, BLOCK):
        cols = slice(at, at + BLOCK)
        row = ROW["w_drop"] - base + at * (D // LANES)
        write_matrix(flat, row, dot_tn(active[:, cols], g_out), D // LANES)
        d_lifted = (dot_nt(g_out, w_drop[cols, :]) * slope[:, cols].astype(f32)).astype(bf16)
        row = ROW["bias_lift"] - base + at // LANES
        write_vector(flat, row, jnp.sum(d_lifted.astype(f32), 0, keepdims=True))
        row = ROW["w_lift"] - base + at // LANES
        write_matrix(flat, row, dot_tn(normed_two[...], d_lifted), FF // LANES)
        d_normed += dot_nt(d_lifted, w_lift[:, cols])
    unit, rstd = normalize(hidden[...])
    back, gain_grad, shift_grad = norm_back(d_normed, unit, rstd, vectors[0:1, :])
    write_vector(flat, ROW["ln2_gain"] - base, gain_grad)
    write_vector(flat, ROW["ln2_shift"] - base, shift_grad)
    g_hidden[...] = g + back
    carry[...] = flat[: carry.shape[0], :]
    pack(flat, base, rows_each, count, places, near, far)


def attention_backward(g_hidden, w_out, qkv, probs, mixed, d_qkv, d_out, bias_out, d_mixed):
    g_att = g_hidden[...].astype(bf16)
    bias_out[...] = jnp.broadcast_to(jnp.sum(g_att.astype(f32), 0, keepdims=True), bias_out.shape)
    d_out[...] = dot_tn(mixed[...], g_att)
    d_mixed[...] = dot_nt(g_att, w_out[...]).astype(bf16)

    def step(at, carried):
        rows, cols = pair_slices(at)
        query, key_rows, value_rows = qkv[rows, cols[0]], qkv[rows, cols[1]], qkv[rows, cols[2]]
        mixed_grad = d_mixed[rows, pl.ds(pl.multiple_of((at % PAIRS) * LANES, LANES), LANES)]
        d_query, d_key, d_value = [], [], []
        for head in range(2):
            own = jnp.where(head_mask(head), mixed_grad, jnp.zeros_like(mixed_grad))
            weight = probs[at * 2 + head]
            d_value.append(dot_tn(weight, mixed_grad))
            weight = weight.astype(f32)
            d_probs = dot_nt(own, value_rows)
            inner = jnp.sum(weight * d_probs, -1, keepdims=True)
            d_scores = (weight * (d_probs - inner)).astype(bf16)
            d_query.append(dot_nn(d_scores, key_rows))
            d_key.append(dot_tn(d_scores, query))
        scale = HEAD_DIM ** (-0.5)
        mask = head_mask(0)
        d_qkv[rows, cols[0]] = (jnp.where(mask, d_query[0], d_query[1]) * scale).astype(bf16)
        d_qkv[rows, cols[1]] = (jnp.where(mask, d_key[0], d_key[1]) * scale).astype(bf16)
        d_qkv[rows, cols[2]] = jnp.where(mask, d_value[0], d_value[1]).astype(bf16)
        return carried

    lax.fori_loop(0, MICRO * PAIRS, step, 0, unroll=BACKWARD_UNROLL)

def projection_backward(rows_each, first, *refs):
    places, refs = refs[:2], refs[2:]
    g_hidden, state, w_qkv, vectors, normed_one, d_qkv, d_out, bias_out, carry = refs[:9]
    near, far, input_grad, flat = refs[9:]
    flat[MLP_ROW : MLP_ROW + carry.shape[0], :] = carry[...]
    write_vector(flat, ROW["bias_attn_out"], bias_out[0:1, :])
    write_matrix(flat, ROW["w_attn_out"], d_out[...], D // LANES)
    query_sum = jnp.sum(d_qkv[:, :D].astype(f32), 0, keepdims=True)
    write_vector(flat, ROW["bias_query"], query_sum)
    value_sum = jnp.sum(d_qkv[:, 2 * D :].astype(f32), 0, keepdims=True)
    write_vector(flat, ROW["bias_value"], value_sum)
    write_matrix(flat, ROW["w_qkv"], dot_tn(normed_one[...], d_qkv[...]), 3 * D // LANES)
    d_normed = dot_nt(d_qkv[...], w_qkv[...])
    unit, rstd = normalize(state[...])
    back, gain_grad, shift_grad = norm_back(d_normed, unit, rstd, vectors[0:1, :])
    write_vector(flat, ROW["ln1_gain"], gain_grad)
    write_vector(flat, ROW["ln1_shift"], shift_grad)
    total = g_hidden[...] + back
    if first:
        for image in range(MICRO):
            input_grad[image] = total[image * ROWS : image * ROWS + SEQ, :]
    else:
        input_grad[...] = total
    pack(flat, 0, rows_each, 0, places, near, far)


def updated(offset, grads, params, first_moment, second_moment):
    shape = grads.shape
    row = lax.broadcasted_iota(jnp.int32, shape, 0)
    flags = matrix_flags((offset[0] + row) * LANES + lax.broadcasted_iota(jnp.int32, shape, 1))
    rate = jnp.where(flags, rate_matrix, rate_vector)
    decay = jnp.where(flags, decay_matrix, 0.0)
    first = beta_one * first_moment + (1.0 - beta_one) * grads
    second = beta_two * second_moment + (1.0 - beta_two) * grads * grads
    first_hat = first / (1.0 - beta_one**STEP)
    second_hat = second / (1.0 - beta_two**STEP)
    moved = rate * (first_hat / (jnp.sqrt(second_hat) + adam_eps) + decay * params)
    return params - moved, first, second


def adam_early(rows_each, offset, kept, received, *refs):
    old, new1, old0 = refs[:3], refs[3:6], refs[6:9]
    grads = kept[:rows_each, :].astype(f32) + received[:rows_each, :].astype(f32)
    for out, value in zip(new1, updated(offset, grads, *[ref[:, 1, :] for ref in old])):
        out[...] = value
    for out, ref in zip(old0, old):
        out[...] = ref[:, 0, :]


def adam_late(rows_each, offset, *refs):
    parts, new1, old0, new = refs[:4], refs[4:7], refs[7:10], refs[10:13]
    grads = sum(part[:rows_each, :].astype(f32) for part in parts)
    for out, value in zip(new, updated(offset, grads, *[ref[...] for ref in old0])):
        out[:, 0, :] = value
    for out, ref in zip(new, new1):
        out[:, 1, :] = ref[...]


def call(body, name, inputs, outputs, scratch, scalars=0, flops=0):
    in_specs = [pl.BlockSpec(memory_space=pltpu.SMEM)] * scalars
    in_specs += [pl.BlockSpec(memory_space=pltpu.VMEM)] * (len(inputs) - scalars)
    shapes = [jax.ShapeDtypeStruct(shape, dtype) for shape, dtype in outputs]
    moved = sum(math.prod(s.shape) * s.dtype.itemsize for s in list(inputs) + shapes)
    return pl.pallas_call(
        body,
        name=name,
        out_shape=shapes,
        in_specs=in_specs,
        out_specs=[pl.BlockSpec(memory_space=pltpu.VMEM)] * len(shapes),
        scratch_shapes=scratch,
        compiler_params=pltpu.CompilerParams(vmem_limit_bytes=VMEM_LIMIT),
        cost_estimate=pl.CostEstimate(flops=flops // COST, bytes_accessed=moved // COST, transcendentals=0),
    )(*inputs)


def tie(values, *before):
    return lax.optimization_barrier((values, before))[0]


def together(*values):
    return lax.optimization_barrier(values)


def swap(values, size, mask):
    return lax.ppermute(values, "dp", [(i, i ^ mask) for i in range(size)])


def gather_masks(bits):
    chain = [1 << bit for bit in range(bits - 2, 2, -1)]
    return [chain + [2, 4, 1], chain + [4, 2, 1]]


def places(me, size, masks):
    relative = me ^ jnp.arange(size // 2, dtype=jnp.int32)
    place = jnp.zeros_like(relative)
    for digit, mask in enumerate(masks):
        place = place | jnp.where(relative & mask != 0, 1 << digit, 0)
    return place


def sent(part, size, mask):
    middle = part.shape[0] // 2
    return part[:middle], swap(part[middle:], size, mask)


def added(pair):
    return (pair[0].astype(f32) + pair[1].astype(f32)).astype(bf16)


def shards(size, images, cotangent, present, params, first_moment, second_moment):
    bits = size.bit_length() - 1
    width = params.shape[1]
    rows_each = width // LANES
    padded = round_up(rows_each, 16)
    half = size // 2
    me = lax.axis_index("dp")
    chain = [1 << bit for bit in range(bits - 2, 2, -1)]
    planes = [(2, 4), (4, 2)]
    place_low, place_high = [places(me, size, chain + [mask, 6 - mask, 1]) for mask in planes[0]]
    place_wide = places(me, size, [2, 4] + chain + [1])
    place = [places(me, size // 2, chain[1:] + [mask, 6 - mask, 1]) for mask in planes[0]]

    def alternating(value):
        return jnp.swapaxes(value.reshape(2, rows_each, LANES), 0, 1)

    is_low, is_first = (me >> (bits - 1)) & 1 == 0, (me >> (bits - 2)) & 1 == 0
    offset = me[None] * rows_each
    early = together(params, is_low, is_first, offset, place_low, place_high, place_wide, *place)
    params, is_low, is_first, offset, place_low, place_high, place_wide, *place = early
    compact = params.astype(bf16).reshape(2, rows_each, LANES)
    compact = jnp.pad(compact, ((0, 0), (0, padded - rows_each), (0, 0)))

    low_flat = pltpu.VMEM((-(-MLP_ROW // rows_each) * rows_each + padded, LANES), f32)
    begin = MLP_ROW // rows_each
    high_flat = pltpu.VMEM(((size - begin) * rows_each + padded, LANES), f32)
    square = TOKENS * D * D
    core_flops = 2 * 2 * MICRO * HEADS * ROWS * ROWS * HEAD_DIM

    def attend(first, places, low, state):
        outputs = [((TOKENS, D), f32)] if first else []
        outputs += [
            ((D, 3 * D), bf16),
            ((D, D), bf16),
            ((8, D), f32),
            ((TOKENS, D), bf16),
            ((TOKENS, 3 * D), bf16),
            ((MICRO * HEADS, ROWS, ROWS), bf16),
            ((TOKENS, D), bf16),
            ((TOKENS, D), f32),
        ]
        made = call(
            functools.partial(attention_forward, rows_each, first, len(places)),
            "attention_forward",
            [*places, *low, state],
            outputs,
            [low_flat],
            scalars=len(places),
            flops=8 * square + core_flops,
        )
        made = made if first else [state, *made]
        return made[:-1], made[-1]

    def lift(last, low_places, high_places, low, high, hidden):
        made = call(
            functools.partial(mlp_forward, rows_each, last, half, len(low_places)),
            "mlp_forward",
            [*low_places, *high_places, *low, *high, hidden],
            [
                ((D, FF), bf16),
                ((FF, D), bf16),
                ((8, D), f32),
                ((TOKENS, D), bf16),
                ((TOKENS, FF), bf16),
                ((TOKENS, FF), bf16),
                ((MICRO, SEQ, D) if last else (TOKENS, D), f32),
            ],
            [high_flat],
            scalars=2 * len(low_places),
            flops=16 * square,
        )
        return (hidden, *made[:-1]), made[-1]

    grads_shape = ((2, size // 8, padded, LANES), bf16)

    def lift_back(last, incoming, kept):
        scratch = [pltpu.VMEM((size * rows_each + padded - MLP_ROW, LANES), f32)]
        if last:
            scratch.append(pltpu.VMEM((TOKENS, D), f32))
        return call(
            functools.partial(mlp_backward, rows_each, last),
            "mlp_backward",
            ([present] if last else []) + [*place, incoming, *kept],
            [((carry_rows, LANES), f32), grads_shape, grads_shape, ((TOKENS, D), f32)],
            scratch,
            scalars=3 if last else 2,
            flops=32 * square,
        )

    def attend_back(g_hidden, kept):
        state, w_qkv, w_out, vectors, normed_one, qkv, probs, mixed = kept
        return call(
            attention_backward,
            "attention_backward",
            [g_hidden, w_out, qkv, probs, mixed],
            [((TOKENS, 3 * D), bf16), ((D, D), f32), ((8, D), f32)],
            [pltpu.VMEM((TOKENS, D), bf16)],
            flops=4 * square + 2 * core_flops,
        )

    def project_back(first, g_hidden, kept, *made):
        state, w_qkv, w_out, vectors, normed_one, qkv, probs, mixed = kept
        return call(
            functools.partial(projection_backward, rows_each, first),
            "projection_backward",
            [*place, g_hidden, state, w_qkv, vectors, normed_one, *made],
            [grads_shape, grads_shape, ((MICRO, SEQ, D) if first else (TOKENS, D), f32)],
            [pltpu.VMEM((MLP_ROW + carry_rows, LANES), f32)],
            scalars=2,
            flops=12 * square,
        )

    def top_gathered(shard, other):
        return jnp.stack([jnp.where(is_low, shard, other), jnp.where(is_low, other, shard)])[None]

    def exchanged(*values):
        return [swap(value, size, bits) for value, bits in zip(values, (size // 4, size // 2, size // 4 * 3))]

    def moved(parts, step):
        return [swap(part, size, mask) for part, mask in zip(parts, planes[step])]

    def joined(parts, received):
        return [jnp.concatenate(pair) for pair in zip(parts, received)]

    def chained(chunks):
        for mask in chain[:-1]:
            chunks = jnp.concatenate([chunks, swap(chunks, size, mask)])
        return chunks, swap(chunks, size, chain[-1])

    def halved(chunks, received):
        chunks = jnp.concatenate([chunks, received])
        return chunks[:, 0], chunks[:, 1]

    cut = padded - round_up(padded * 5 // 14, 16)
    row1, wide = compact[1, :cut], compact[1, cut:][None]
    nearby, other0, far_other0 = exchanged(compact[0], compact[0], compact[0])
    received = swap(wide, size, 2)
    row1, nearby, other0, far_other0, received = together(row1, nearby, other0, far_other0, received)
    wide = jnp.concatenate([wide, received])
    other1 = swap(row1, size, size // 2)
    received = swap(wide, size, 4)
    chunks0 = top_gathered(jnp.stack([compact[0], nearby]), jnp.stack([other0, far_other0]))[0]
    half0 = chunks0[0], chunks0[1]
    for mask in chain[1:]:
        half0 = [jnp.concatenate([part, swap(part, size, mask)]) for part in half0]
    received0 = moved(half0, 0)
    *received0, other1, received = together(*received0, other1, received)
    wide = jnp.concatenate([wide, received])
    half0 = joined(half0, received0)
    received0 = moved(half0, 1)
    half1 = halved(*chained(top_gathered(row1, other1)))
    received1 = moved(half1, 0)
    received = swap(wide, size, size // 2)
    *received0, received1[0], received1[1], received = together(*received0, *received1, received)
    near0 = joined(half0, received0)
    far0 = [swap(part, size, 1) for part in near0]
    half1 = joined(half1, received1)
    received1 = moved(half1, 1)
    wide = jnp.stack([jnp.where(is_low, wide, received), jnp.where(is_low, received, wide)], axis=1)
    wide, received = chained(wide)
    one0, hidden = attend(True, [place_low], [near0[0], far0[0]], images)
    hidden, *received1, received = together(hidden, *received1, received)
    near1 = joined(half1, received1)
    near1 = [part for pair in zip(near1, halved(wide, received)) for part in pair]
    far1 = [swap(part, size, 1) for part in near1]
    two0, state = lift(False, [place_low], [place_high], [near0[0], far0[0]], [near0[1], far0[1]], hidden)
    state, *far1 = together(state, *far1)
    both1 = [part for pair in zip(near1, far1) for part in pair]
    low1, high1 = both1[:4], both1[4:]
    one1, hidden = attend(False, [place_low, place_wide], low1, state)
    two1, outputs = lift(True, [place_low, place_wide], [place_high, place_wide], low1, high1, hidden)

    carry_rows = round_up(half * rows_each - MLP_ROW + padded - rows_each, 8)

    def to_plane(pairs, step):
        return [sent(added(pair), size, mask) for pair, mask in zip(pairs, planes[step])]

    def to_core(near, far):
        received = swap(far, size, 1)
        return [(near[quarter], received[quarter]) for quarter in range(2)]

    def along(pairs):
        parts = [added(pair) for pair in pairs]
        for mask in reversed(chain[1:]):
            parts = [added(sent(part, size, mask)) for part in parts]
        return parts

    def hold(pairs, *others):
        values = together(*[value for pair in pairs for value in pair], *others)
        count = 2 * len(pairs)
        return [values[i : i + 2] for i in range(0, count, 2)], *values[count:]

    def to_inner(low, high):
        kept = jnp.concatenate([jnp.where(is_first, *part) for part in (low, high)])
        given = jnp.concatenate([jnp.where(is_first, *part[::-1]) for part in (low, high)])
        return kept, swap(given, size, size // 4)

    def to_top(halves):
        kept = jnp.where(is_low, halves[0], halves[1])
        return kept, swap(jnp.where(is_low, halves[1], halves[0]), size, size // 2)

    carry, near, far, g_hidden = lift_back(True, cotangent, two1)
    high1 = to_core(near, far)
    made = attend_back(g_hidden, one1)
    high1, *made = hold(high1, *made)
    near, far, incoming = project_back(False, g_hidden, one1, *made, carry)
    high1 = to_plane(high1, 1)
    low1 = to_core(near, far)
    carry, near, far, g_hidden = lift_back(False, incoming, two0)
    held, g_hidden = hold(high1 + low1, g_hidden)
    high1, low1 = to_plane(held[:2], 0), to_plane(held[2:], 1)
    high0 = to_core(near, far)
    made = attend_back(g_hidden, one0)
    held, *made = hold(high1 + low1 + high0, *made)
    high1, low1, high0 = along(held[:2]), to_plane(held[2:4], 0), to_plane(held[4:], 1)
    near, far, input_grad = project_back(True, g_hidden, one0, *made, carry)
    low1, near, far = hold(low1, near, far)
    low0 = to_core(near, far)
    high0 = to_plane(high0, 0)
    inner1 = to_inner(along(low1), high1)
    low0, = hold(low0)
    low0 = to_plane(low0, 1)
    held, = hold(low0 + high0 + [to_top(added(inner1))])
    low0, high0, top1 = to_plane(held[:2], 0), along(held[2:4]), held[4]
    held, *high0, outputs, input_grad = hold(low0, *high0, outputs, input_grad)
    low0 = along(held)
    here, there = [jnp.where(is_low, *pair) for pair in zip(low0, high0)], [jnp.where(is_low, *pair) for pair in zip(high0, low0)]
    here, there = [[jnp.where(is_first, *pair), jnp.where(is_first, *pair[::-1])] for pair in (here, there)]
    values = exchanged(here[1][0], there[0][0], there[1][0])
    (nearby, other, far_other), received = values, top1[1]
    early = call(
        functools.partial(adam_early, rows_each),
        "adam_early",
        [offset, top1[0], received, *map(alternating, (params, first_moment, second_moment))],
        [((rows_each, LANES), f32)] * 6,
        [],
        scalars=1,
    )
    nearby, other, far_other, *early = together(nearby, other, far_other, *early)
    results = call(
        functools.partial(adam_late, rows_each),
        "adam_late",
        [offset, here[0][0], nearby, other, far_other, *early],
        [((rows_each, 2, LANES), f32)] * 3,
        [],
        scalars=1,
    )
    new_params, new_first, new_second = [
        jnp.swapaxes(value, 0, 1).reshape(2, width) for value in results
    ]
    return (outputs, input_grad, new_params, new_first, new_second)


def solution(mesh):
    in_specs = (
        P("dp", None, None),
        P("dp", None, None),
        P("dp"),
        P(None, "dp"),
        P(None, "dp"),
        P(None, "dp"),
    )
    out_specs = (
        P("dp", None, None),
        P("dp", None, None),
        P(None, "dp"),
        P(None, "dp"),
        P(None, "dp"),
    )
    body = functools.partial(shards, mesh.shape["dp"])
    return jax.shard_map(body, mesh=mesh, in_specs=in_specs, out_specs=out_specs, check_vma=False)
```

```python
import functools
import math

import jax
import jax.numpy as jnp
from jax import lax
from jax.experimental import pallas as pl
from jax.experimental.pallas import tpu as pltpu
from jax.sharding import PartitionSpec as P

D = 384
FF = 1536
HEADS = 6
HEAD_DIM = 64
SEQ = 197
MICRO = 2
STEP = 10
P_SIZE = 1774080

LANES = 128
ROWS = 208
TOKENS = MICRO * ROWS
PAIRS = HEADS // 2
COST = 1
FORWARD_UNROLL = 6
BACKWARD_UNROLL = 3
VMEM_LIMIT = 14 * 1024 * 1024
BLOCK = 1536

eps_norm = 1e-06
beta_one = 0.9
beta_two = 0.999
adam_eps = 1e-08
rate_matrix = 0.1
rate_vector = 0.5
decay_matrix = 0.05
sqrt_half = 0.7071067811865476
inverse_root_tau = 0.3989422804014327

f32 = jnp.float32
bf16 = jnp.bfloat16


def layout():
    return [
        ("ln1_gain", (D,)),
        ("ln1_shift", (D,)),
        ("w_qkv", (D, 3 * D)),
        ("bias_query", (D,)),
        ("bias_value", (D,)),
        ("w_attn_out", (D, D)),
        ("bias_attn_out", (D,)),
        ("ln2_gain", (D,)),
        ("ln2_shift", (D,)),
        ("w_lift", (D, FF)),
        ("bias_lift", (FF,)),
        ("w_drop", (FF, D)),
        ("bias_drop", (D,)),
    ]


def row_offsets():
    offsets, at = {}, 0
    for label, shape in layout():
        offsets[label] = at
        at += math.prod(shape) // LANES
    offsets["end"] = at
    return offsets


ROW = row_offsets()
MLP_ROW = ROW["ln2_gain"]


def matrix_flags(position):
    square = D * D
    lifted = D * FF
    bounds = [
        (2 * D, 2 * D + 3 * square),
        (4 * D + 3 * square, 4 * D + 4 * square),
        (7 * D + 4 * square, 7 * D + 4 * square + lifted),
        (7 * D + 4 * square + lifted + FF, 7 * D + 4 * square + 2 * lifted + FF),
    ]
    flags = jnp.zeros(position.shape, dtype=bool)
    for lower, upper in bounds:
        flags = flags | (position >= lower) & (position < upper)
    return flags


def round_up(value, step):
    return (value + step - 1) // step * step


def dot(a, b, dims):
    return lax.dot_general(a, b, ((dims[0], dims[1]), ((), ())), preferred_element_type=f32)


def dot_nn(a, b):
    return dot(a, b, ((1,), (0,)))


def dot_nt(a, b):
    return dot(a, b, ((1,), (1,)))


def dot_tn(a, b):
    return dot(a, b, ((0,), (0,)))


def read_vector(flat, row, count):
    parts = [flat[row + i : row + i + 1, :] for i in range(count)]
    return jnp.concatenate(parts, axis=1)


def write_vector(flat, row, values):
    for i in range(values.shape[1] // LANES):
        flat[row + i : row + i + 1, :] = values[:, i * LANES : (i + 1) * LANES]


def read_matrix(flat, row, out, depth, width):
    blocks = width // LANES
    for j in range(blocks):
        part = flat[pl.ds(row + j, depth, stride=blocks), :]
        out[:, j * LANES : (j + 1) * LANES] = part.astype(bf16)


def write_matrix(flat, row, values, blocks):
    depth, width = values.shape
    for j in range(width // LANES):
        flat[pl.ds(row + j, depth, stride=blocks), :] = values[:, j * LANES : (j + 1) * LANES]


def normalize(values):
    center = values - jnp.mean(values, -1, keepdims=True)
    rstd = lax.rsqrt(jnp.mean(center * center, -1, keepdims=True) + eps_norm)
    return center * rstd, rstd


def norm_back(incoming, unit, rstd, gain):
    scaled = incoming * gain
    inner = jnp.mean(scaled * unit, -1, keepdims=True)
    back = rstd * (scaled - jnp.mean(scaled, -1, keepdims=True) - unit * inner)
    gain_grad = jnp.sum(incoming * unit, 0, keepdims=True)
    return back, gain_grad, jnp.sum(incoming, 0, keepdims=True)


def head_mask(head):
    lane = lax.broadcasted_iota(jnp.int32, (1, LANES), 1)
    return lane < HEAD_DIM if head == 0 else lane >= HEAD_DIM


def pair_slices(step):
    image, pair = step // PAIRS, step % PAIRS
    rows = pl.ds(pl.multiple_of(image * ROWS, 16), ROWS)
    cols = [pl.ds(pl.multiple_of(t * D + pair * LANES, LANES), LANES) for t in range(3)]
    return rows, cols


def unpack(rows_each, base, chunks, parts, flat):
    def step(chunk, carry):
        begin = (chunks[2] + chunk) * rows_each - base
        for place, near, far in parts:
            count, padded = near.shape[0], near.shape[1]
            at = place[chunk]
            own = lax.rem(at, count)
            rows = jnp.where(at < count, near[own].astype(f32), far[own].astype(f32))
            flat[pl.ds(begin, padded), :] = rows
            begin = begin + padded
        return carry

    lax.fori_loop(chunks[0], chunks[1], step, 0)


def parts_of(places, refs):
    return [(place, refs[2 * i], refs[2 * i + 1]) for i, place in enumerate(places)], refs[2 * len(places) :]


def attention_forward(rows_each, first, count, *refs):
    parts, (state, *refs) = parts_of(refs[:count], refs[count:])
    if first:
        kept_state, refs = refs[0], refs[1:]
    w_qkv, w_out, vectors, normed_one, qkv, probs, mixed, hidden, flat = refs
    unpack(rows_each, 0, (0, -(-MLP_ROW // rows_each), 0), parts, flat)
    read_matrix(flat, ROW["w_qkv"], w_qkv, D, 3 * D)
    read_matrix(flat, ROW["w_attn_out"], w_out, D, D)
    labels = ["ln1_gain", "ln1_shift", "bias_query", "bias_value", "bias_attn_out"]
    for at, label in enumerate(labels):
        vectors[at : at + 1, :] = read_vector(flat, ROW[label], 3)
    gain, shift = vectors[0:1, :], vectors[1:2, :]
    if first:
        kept_state[...] = jnp.zeros_like(kept_state)
        for image in range(MICRO):
            kept_state[image * ROWS : image * ROWS + SEQ, :] = state[image].astype(f32)
        x = kept_state[...]
    else:
        x = state[...]
    unit, _ = normalize(x)
    normed_one[...] = (unit * gain + shift).astype(bf16)
    bias_query = vectors[2:3, :]
    bias = jnp.concatenate([bias_query, jnp.zeros_like(bias_query), vectors[3:4, :]], axis=1)
    qkv[...] = (dot_nn(normed_one[...], w_qkv[...]) + bias).astype(bf16)

    def step(at, carry):
        rows, cols = pair_slices(at)
        query, key_rows, value_rows = qkv[rows, cols[0]], qkv[rows, cols[1]], qkv[rows, cols[2]]
        real = lax.broadcasted_iota(jnp.int32, (ROWS, ROWS), 1) < SEQ
        sides = []
        for head in range(2):
            own_key = jnp.where(head_mask(head), key_rows, jnp.zeros_like(key_rows))
            raw = jnp.where(real, dot_nt(query, own_key), -1e30)
            powers = jnp.exp((raw - jnp.max(raw, -1, keepdims=True)) * HEAD_DIM ** (-0.5))
            weight = powers / jnp.sum(powers, -1, keepdims=True)
            weight = weight.astype(bf16)
            probs[at * 2 + head] = weight
            sides.append(dot_nn(weight, value_rows))
        mixed[rows, pl.ds(pl.multiple_of((at % PAIRS) * LANES, LANES), LANES)] = jnp.where(
            head_mask(0), sides[0], sides[1]
        ).astype(bf16)
        return carry

    lax.fori_loop(0, MICRO * PAIRS, step, 0, unroll=FORWARD_UNROLL)
    hidden[...] = x + dot_nn(mixed[...], w_out[...]) + vectors[4:5, :]


def mlp_forward(rows_each, last, half, count, *refs):
    low_places, high_places, refs = refs[:count], refs[count : 2 * count], refs[2 * count :]
    low, refs = parts_of(low_places, refs)
    high, (hidden, *refs) = parts_of(high_places, refs)
    w_lift, w_drop, vectors, normed_two, active, slope, result, flat = refs
    begin = MLP_ROW // rows_each
    base = begin * rows_each
    unpack(rows_each, base, (begin, half, 0), low, flat)
    unpack(rows_each, base, (0, half, half), high, flat)
    read_matrix(flat, ROW["w_lift"] - base, w_lift, D, FF)
    read_matrix(flat, ROW["w_drop"] - base, w_drop, FF, D)
    for at, label in enumerate(["ln2_gain", "ln2_shift", "bias_drop"]):
        vectors[at : at + 1, :] = read_vector(flat, ROW[label] - base, 3)
    bias_lift = read_vector(flat, ROW["bias_lift"] - base, FF // LANES)
    gain, shift = vectors[0:1, :], vectors[1:2, :]
    unit, _ = normalize(hidden[...])
    normed_two[...] = (unit * gain + shift).astype(bf16)
    total = hidden[...] + vectors[2:3, :]
    for at in range(0, FF, BLOCK):
        cols = slice(at, at + BLOCK)
        lifted = dot_nn(normed_two[...], w_lift[:, cols]) + bias_lift[:, cols]
        below = 0.5 * (1.0 + lax.erf(lifted * sqrt_half))
        active[:, cols] = (lifted * below).astype(bf16)
        bell = jnp.exp(-0.5 * lifted * lifted) * inverse_root_tau
        slope[:, cols] = (below + lifted * bell).astype(bf16)
        total += dot_nn(active[:, cols], w_drop[cols, :])
    if last:
        for image in range(MICRO):
            result[image] = total[image * ROWS : image * ROWS + SEQ, :]
    else:
        result[...] = total


def pack(flat, base, rows_each, first_chunk, places, near, far):
    count, padded = near.shape[1], near.shape[2]
    for quarter, place in enumerate(places):

        def step(chunk, carry):
            at = (first_chunk + quarter * 2 * count + chunk) * rows_each - base
            index = lax.rem(place[chunk], count)

            @pl.when(place[chunk] < count)
            def _():
                near[quarter, index] = flat[pl.ds(at, padded), :].astype(bf16)

            @pl.when(place[chunk] >= count)
            def _():
                far[quarter, index] = flat[pl.ds(at, padded), :].astype(bf16)

            return carry

        lax.fori_loop(0, 2 * count, step, 0)


def mlp_backward(rows_each, last, *refs):
    if last:
        present, refs = refs[0], refs[1:]
    places, refs = refs[:2], refs[2:]
    incoming, hidden, w_lift, w_drop, vectors, normed_two, active, slope = refs[:8]
    refs = refs[8:]
    carry, near, far, g_hidden, flat = refs[:5]
    count = 4 * near.shape[1]
    if last:
        kept = refs[5]
        kept[...] = jnp.zeros_like(kept)
        for image in range(MICRO):
            seed = incoming[image].astype(f32) * present[image].astype(f32)
            kept[image * ROWS : image * ROWS + SEQ, :] = seed
        g = kept[...]
    else:
        g = incoming[...]
    base = MLP_ROW
    end = ROW["end"] - base
    flat[end:, :] = jnp.zeros((flat.shape[0] - end, LANES), f32)
    g_out = g.astype(bf16)
    write_vector(flat, ROW["bias_drop"] - base, jnp.sum(g_out.astype(f32), 0, keepdims=True))
    d_normed = jnp.zeros((TOKENS, D), f32)
    for at in range(0, FF, BLOCK):
        cols = slice(at, at + BLOCK)
        row = ROW["w_drop"] - base + at * (D // LANES)
        write_matrix(flat, row, dot_tn(active[:, cols], g_out), D // LANES)
        d_lifted = (dot_nt(g_out, w_drop[cols, :]) * slope[:, cols].astype(f32)).astype(bf16)
        row = ROW["bias_lift"] - base + at // LANES
        write_vector(flat, row, jnp.sum(d_lifted.astype(f32), 0, keepdims=True))
        row = ROW["w_lift"] - base + at // LANES
        write_matrix(flat, row, dot_tn(normed_two[...], d_lifted), FF // LANES)
        d_normed += dot_nt(d_lifted, w_lift[:, cols])
    unit, rstd = normalize(hidden[...])
    back, gain_grad, shift_grad = norm_back(d_normed, unit, rstd, vectors[0:1, :])
    write_vector(flat, ROW["ln2_gain"] - base, gain_grad)
    write_vector(flat, ROW["ln2_shift"] - base, shift_grad)
    g_hidden[...] = g + back
    carry[...] = flat[: carry.shape[0], :]
    pack(flat, base, rows_each, count, places, near, far)


def attention_backward(g_hidden, w_out, qkv, probs, mixed, d_qkv, d_out, bias_out, d_mixed):
    g_att = g_hidden[...].astype(bf16)
    bias_out[...] = jnp.broadcast_to(jnp.sum(g_att.astype(f32), 0, keepdims=True), bias_out.shape)
    d_out[...] = dot_tn(mixed[...], g_att)
    d_mixed[...] = dot_nt(g_att, w_out[...]).astype(bf16)

    def step(at, carried):
        rows, cols = pair_slices(at)
        query, key_rows, value_rows = qkv[rows, cols[0]], qkv[rows, cols[1]], qkv[rows, cols[2]]
        mixed_grad = d_mixed[rows, pl.ds(pl.multiple_of((at % PAIRS) * LANES, LANES), LANES)]
        d_query, d_key, d_value = [], [], []
        for head in range(2):
            own = jnp.where(head_mask(head), mixed_grad, jnp.zeros_like(mixed_grad))
            weight = probs[at * 2 + head]
            d_value.append(dot_tn(weight, mixed_grad))
            weight = weight.astype(f32)
            d_probs = dot_nt(own, value_rows)
            inner = jnp.sum(weight * d_probs, -1, keepdims=True)
            d_scores = (weight * (d_probs - inner)).astype(bf16)
            d_query.append(dot_nn(d_scores, key_rows))
            d_key.append(dot_tn(d_scores, query))
        scale = HEAD_DIM ** (-0.5)
        mask = head_mask(0)
        d_qkv[rows, cols[0]] = (jnp.where(mask, d_query[0], d_query[1]) * scale).astype(bf16)
        d_qkv[rows, cols[1]] = (jnp.where(mask, d_key[0], d_key[1]) * scale).astype(bf16)
        d_qkv[rows, cols[2]] = jnp.where(mask, d_value[0], d_value[1]).astype(bf16)
        return carried

    lax.fori_loop(0, MICRO * PAIRS, step, 0, unroll=BACKWARD_UNROLL)

def projection_backward(rows_each, first, *refs):
    places, refs = refs[:2], refs[2:]
    g_hidden, state, w_qkv, vectors, normed_one, d_qkv, d_out, bias_out, carry = refs[:9]
    near, far, input_grad, flat = refs[9:]
    flat[MLP_ROW : MLP_ROW + carry.shape[0], :] = carry[...]
    write_vector(flat, ROW["bias_attn_out"], bias_out[0:1, :])
    write_matrix(flat, ROW["w_attn_out"], d_out[...], D // LANES)
    query_sum = jnp.sum(d_qkv[:, :D].astype(f32), 0, keepdims=True)
    write_vector(flat, ROW["bias_query"], query_sum)
    value_sum = jnp.sum(d_qkv[:, 2 * D :].astype(f32), 0, keepdims=True)
    write_vector(flat, ROW["bias_value"], value_sum)
    write_matrix(flat, ROW["w_qkv"], dot_tn(normed_one[...], d_qkv[...]), 3 * D // LANES)
    d_normed = dot_nt(d_qkv[...], w_qkv[...])
    unit, rstd = normalize(state[...])
    back, gain_grad, shift_grad = norm_back(d_normed, unit, rstd, vectors[0:1, :])
    write_vector(flat, ROW["ln1_gain"], gain_grad)
    write_vector(flat, ROW["ln1_shift"], shift_grad)
    total = g_hidden[...] + back
    if first:
        for image in range(MICRO):
            input_grad[image] = total[image * ROWS : image * ROWS + SEQ, :]
    else:
        input_grad[...] = total
    pack(flat, 0, rows_each, 0, places, near, far)


def updated(offset, grads, params, first_moment, second_moment):
    shape = grads.shape
    row = lax.broadcasted_iota(jnp.int32, shape, 0)
    flags = matrix_flags((offset[0] + row) * LANES + lax.broadcasted_iota(jnp.int32, shape, 1))
    rate = jnp.where(flags, rate_matrix, rate_vector)
    decay = jnp.where(flags, decay_matrix, 0.0)
    first = beta_one * first_moment + (1.0 - beta_one) * grads
    second = beta_two * second_moment + (1.0 - beta_two) * grads * grads
    first_hat = first / (1.0 - beta_one**STEP)
    second_hat = second / (1.0 - beta_two**STEP)
    moved = rate * (first_hat / (jnp.sqrt(second_hat) + adam_eps) + decay * params)
    return params - moved, first, second


def adam_early(rows_each, offset, kept, received, *refs):
    old, new1, old0 = refs[:3], refs[3:6], refs[6:9]
    grads = kept[:rows_each, :].astype(f32) + received[:rows_each, :].astype(f32)
    for out, value in zip(new1, updated(offset, grads, *[ref[:, 1, :] for ref in old])):
        out[...] = value
    for out, ref in zip(old0, old):
        out[...] = ref[:, 0, :]


def adam_late(rows_each, offset, *refs):
    parts, new1, old0, new = refs[:4], refs[4:7], refs[7:10], refs[10:13]
    grads = sum(part[:rows_each, :].astype(f32) for part in parts)
    for out, value in zip(new, updated(offset, grads, *[ref[...] for ref in old0])):
        out[:, 0, :] = value
    for out, ref in zip(new, new1):
        out[:, 1, :] = ref[...]


def call(body, name, inputs, outputs, scratch, scalars=0, flops=0):
    in_specs = [pl.BlockSpec(memory_space=pltpu.SMEM)] * scalars
    in_specs += [pl.BlockSpec(memory_space=pltpu.VMEM)] * (len(inputs) - scalars)
    shapes = [jax.ShapeDtypeStruct(shape, dtype) for shape, dtype in outputs]
    moved = sum(math.prod(s.shape) * s.dtype.itemsize for s in list(inputs) + shapes)
    return pl.pallas_call(
        body,
        name=name,
        out_shape=shapes,
        in_specs=in_specs,
        out_specs=[pl.BlockSpec(memory_space=pltpu.VMEM)] * len(shapes),
        scratch_shapes=scratch,
        compiler_params=pltpu.CompilerParams(vmem_limit_bytes=VMEM_LIMIT),
        cost_estimate=pl.CostEstimate(flops=flops // COST, bytes_accessed=moved // COST, transcendentals=0),
    )(*inputs)


def tie(values, *before):
    return lax.optimization_barrier((values, before))[0]


def together(*values):
    return lax.optimization_barrier(values)


def swap(values, size, mask):
    return lax.ppermute(values, "dp", [(i, i ^ mask) for i in range(size)])


def gather_masks(bits):
    chain = [1 << bit for bit in range(bits - 2, 2, -1)]
    return [chain + [2, 4, 1], chain + [4, 2, 1]]


def places(me, size, masks):
    relative = me ^ jnp.arange(size // 2, dtype=jnp.int32)
    place = jnp.zeros_like(relative)
    for digit, mask in enumerate(masks):
        place = place | jnp.where(relative & mask != 0, 1 << digit, 0)
    return place


def sent(part, size, mask):
    middle = part.shape[0] // 2
    return part[:middle], swap(part[middle:], size, mask)


def added(pair):
    return (pair[0].astype(f32) + pair[1].astype(f32)).astype(bf16)


def shards(size, images, cotangent, present, params, first_moment, second_moment):
    bits = size.bit_length() - 1
    width = params.shape[1]
    rows_each = width // LANES
    padded = round_up(rows_each, 16)
    half = size // 2
    me = lax.axis_index("dp")
    chain = [1 << bit for bit in range(bits - 2, 2, -1)]
    planes = [(2, 4), (4, 2)]
    place_low, place_high = [places(me, size, chain + [mask, 6 - mask, 1]) for mask in planes[0]]
    place_wide = places(me, size, [2, 4] + chain + [1])
    place = [places(me, size // 2, chain[1:] + [mask, 6 - mask, 1]) for mask in planes[0]]

    def alternating(value):
        return jnp.swapaxes(value.reshape(2, rows_each, LANES), 0, 1)

    is_low, is_first = (me >> (bits - 1)) & 1 == 0, (me >> (bits - 2)) & 1 == 0
    offset = me[None] * rows_each
    early = together(params, is_low, is_first, offset, place_low, place_high, place_wide, *place)
    params, is_low, is_first, offset, place_low, place_high, place_wide, *place = early
    compact = params.astype(bf16).reshape(2, rows_each, LANES)
    compact = jnp.pad(compact, ((0, 0), (0, padded - rows_each), (0, 0)))

    low_flat = pltpu.VMEM((-(-MLP_ROW // rows_each) * rows_each + padded, LANES), f32)
    begin = MLP_ROW // rows_each
    high_flat = pltpu.VMEM(((size - begin) * rows_each + padded, LANES), f32)
    square = TOKENS * D * D
    core_flops = 2 * 2 * MICRO * HEADS * ROWS * ROWS * HEAD_DIM

    def attend(first, places, low, state):
        outputs = [((TOKENS, D), f32)] if first else []
        outputs += [
            ((D, 3 * D), bf16),
            ((D, D), bf16),
            ((8, D), f32),
            ((TOKENS, D), bf16),
            ((TOKENS, 3 * D), bf16),
            ((MICRO * HEADS, ROWS, ROWS), bf16),
            ((TOKENS, D), bf16),
            ((TOKENS, D), f32),
        ]
        made = call(
            functools.partial(attention_forward, rows_each, first, len(places)),
            "attention_forward",
            [*places, *low, state],
            outputs,
            [low_flat],
            scalars=len(places),
            flops=8 * square + core_flops,
        )
        made = made if first else [state, *made]
        return made[:-1], made[-1]

    def lift(last, low_places, high_places, low, high, hidden):
        made = call(
            functools.partial(mlp_forward, rows_each, last, half, len(low_places)),
            "mlp_forward",
            [*low_places, *high_places, *low, *high, hidden],
            [
                ((D, FF), bf16),
                ((FF, D), bf16),
                ((8, D), f32),
                ((TOKENS, D), bf16),
                ((TOKENS, FF), bf16),
                ((TOKENS, FF), bf16),
                ((MICRO, SEQ, D) if last else (TOKENS, D), f32),
            ],
            [high_flat],
            scalars=2 * len(low_places),
            flops=16 * square,
        )
        return (hidden, *made[:-1]), made[-1]

    grads_shape = ((2, size // 8, padded, LANES), bf16)

    def lift_back(last, incoming, kept):
        scratch = [pltpu.VMEM((size * rows_each + padded - MLP_ROW, LANES), f32)]
        if last:
            scratch.append(pltpu.VMEM((TOKENS, D), f32))
        return call(
            functools.partial(mlp_backward, rows_each, last),
            "mlp_backward",
            ([present] if last else []) + [*place, incoming, *kept],
            [((carry_rows, LANES), f32), grads_shape, grads_shape, ((TOKENS, D), f32)],
            scratch,
            scalars=3 if last else 2,
            flops=32 * square,
        )

    def attend_back(g_hidden, kept):
        state, w_qkv, w_out, vectors, normed_one, qkv, probs, mixed = kept
        return call(
            attention_backward,
            "attention_backward",
            [g_hidden, w_out, qkv, probs, mixed],
            [((TOKENS, 3 * D), bf16), ((D, D), f32), ((8, D), f32)],
            [pltpu.VMEM((TOKENS, D), bf16)],
            flops=4 * square + 2 * core_flops,
        )

    def project_back(first, g_hidden, kept, *made):
        state, w_qkv, w_out, vectors, normed_one, qkv, probs, mixed = kept
        return call(
            functools.partial(projection_backward, rows_each, first),
            "projection_backward",
            [*place, g_hidden, state, w_qkv, vectors, normed_one, *made],
            [grads_shape, grads_shape, ((MICRO, SEQ, D) if first else (TOKENS, D), f32)],
            [pltpu.VMEM((MLP_ROW + carry_rows, LANES), f32)],
            scalars=2,
            flops=12 * square,
        )

    def top_gathered(shard, other):
        return jnp.stack([jnp.where(is_low, shard, other), jnp.where(is_low, other, shard)])[None]

    def exchanged(*values):
        return [swap(value, size, bits) for value, bits in zip(values, (size // 4, size // 2, size // 4 * 3))]

    def moved(parts, step):
        return [swap(part, size, mask) for part, mask in zip(parts, planes[step])]

    def joined(parts, received):
        return [jnp.concatenate(pair) for pair in zip(parts, received)]

    def chained(chunks):
        for mask in chain[:-1]:
            chunks = jnp.concatenate([chunks, swap(chunks, size, mask)])
        return chunks, swap(chunks, size, chain[-1])

    def halved(chunks, received):
        chunks = jnp.concatenate([chunks, received])
        return chunks[:, 0], chunks[:, 1]

    cut = padded - round_up(padded * 5 // 14, 16)
    row1, wide = compact[1, :cut], compact[1, cut:][None]
    nearby, other0, far_other0 = exchanged(compact[0], compact[0], compact[0])
    received = swap(wide, size, 2)
    row1, nearby, other0, far_other0, received = together(row1, nearby, other0, far_other0, received)
    wide = jnp.concatenate([wide, received])
    other1 = swap(row1, size, size // 2)
    received = swap(wide, size, 4)
    chunks0 = top_gathered(jnp.stack([compact[0], nearby]), jnp.stack([other0, far_other0]))[0]
    half0 = chunks0[0], chunks0[1]
    for mask in chain[1:]:
        half0 = [jnp.concatenate([part, swap(part, size, mask)]) for part in half0]
    received0 = moved(half0, 0)
    *received0, other1, received = together(*received0, other1, received)
    wide = jnp.concatenate([wide, received])
    half0 = joined(half0, received0)
    received0 = moved(half0, 1)
    half1 = halved(*chained(top_gathered(row1, other1)))
    received1 = moved(half1, 0)
    received = swap(wide, size, size // 2)
    *received0, received1[0], received1[1], received = together(*received0, *received1, received)
    near0 = joined(half0, received0)
    far0 = [swap(part, size, 1) for part in near0]
    half1 = joined(half1, received1)
    received1 = moved(half1, 1)
    wide = jnp.stack([jnp.where(is_low, wide, received), jnp.where(is_low, received, wide)], axis=1)
    wide, received = chained(wide)
    one0, hidden = attend(True, [place_low], [near0[0], far0[0]], images)
    hidden, *received1, received = together(hidden, *received1, received)
    near1 = joined(half1, received1)
    near1 = [part for pair in zip(near1, halved(wide, received)) for part in pair]
    far1 = [swap(part, size, 1) for part in near1]
    two0, state = lift(False, [place_low], [place_high], [near0[0], far0[0]], [near0[1], far0[1]], hidden)
    state, *far1 = together(state, *far1)
    both1 = [part for pair in zip(near1, far1) for part in pair]
    low1, high1 = both1[:4], both1[4:]
    one1, hidden = attend(False, [place_low, place_wide], low1, state)
    two1, outputs = lift(True, [place_low, place_wide], [place_high, place_wide], low1, high1, hidden)

    carry_rows = round_up(half * rows_each - MLP_ROW + padded - rows_each, 8)

    def to_plane(pairs, step):
        return [sent(added(pair), size, mask) for pair, mask in zip(pairs, planes[step])]

    def to_core(near, far):
        received = swap(far, size, 1)
        return [(near[quarter], received[quarter]) for quarter in range(2)]

    def along(pairs):
        parts = [added(pair) for pair in pairs]
        for mask in reversed(chain[1:]):
            parts = [added(sent(part, size, mask)) for part in parts]
        return parts

    def hold(pairs, *others):
        values = together(*[value for pair in pairs for value in pair], *others)
        count = 2 * len(pairs)
        return [values[i : i + 2] for i in range(0, count, 2)], *values[count:]

    def to_inner(low, high):
        kept = jnp.concatenate([jnp.where(is_first, *part) for part in (low, high)])
        given = jnp.concatenate([jnp.where(is_first, *part[::-1]) for part in (low, high)])
        return kept, swap(given, size, size // 4)

    def to_top(halves):
        kept = jnp.where(is_low, halves[0], halves[1])
        return kept, swap(jnp.where(is_low, halves[1], halves[0]), size, size // 2)

    carry, near, far, g_hidden = lift_back(True, cotangent, two1)
    high1 = to_core(near, far)
    made = attend_back(g_hidden, one1)
    high1, *made = hold(high1, *made)
    near, far, incoming = project_back(False, g_hidden, one1, *made, carry)
    high1 = to_plane(high1, 1)
    low1 = to_core(near, far)
    carry, near, far, g_hidden = lift_back(False, incoming, two0)
    held, g_hidden = hold(high1 + low1, g_hidden)
    high1, low1 = to_plane(held[:2], 0), to_plane(held[2:], 1)
    high0 = to_core(near, far)
    made = attend_back(g_hidden, one0)
    held, *made = hold(high1 + low1 + high0, *made)
    high1, low1, high0 = along(held[:2]), to_plane(held[2:4], 0), to_plane(held[4:], 1)
    near, far, input_grad = project_back(True, g_hidden, one0, *made, carry)
    low1, near, far = hold(low1, near, far)
    low0 = to_core(near, far)
    high0 = to_plane(high0, 0)
    inner1 = to_inner(along(low1), high1)
    low0, = hold(low0)
    low0 = to_plane(low0, 1)
    held, = hold(low0 + high0 + [to_top(added(inner1))])
    low0, high0, top1 = to_plane(held[:2], 0), along(held[2:4]), held[4]
    held, *high0, outputs, input_grad = hold(low0, *high0, outputs, input_grad)
    low0 = along(held)
    here, there = [jnp.where(is_low, *pair) for pair in zip(low0, high0)], [jnp.where(is_low, *pair) for pair in zip(high0, low0)]
    here, there = [[jnp.where(is_first, *pair), jnp.where(is_first, *pair[::-1])] for pair in (here, there)]
    values = exchanged(here[1][0], there[0][0], there[1][0])
    (nearby, other, far_other), received = values, top1[1]
    early = call(
        functools.partial(adam_early, rows_each),
        "adam_early",
        [offset, top1[0], received, *map(alternating, (params, first_moment, second_moment))],
        [((rows_each, LANES), f32)] * 6,
        [],
        scalars=1,
    )
    nearby, other, far_other, *early = together(nearby, other, far_other, *early)
    results = call(
        functools.partial(adam_late, rows_each),
        "adam_late",
        [offset, here[0][0], nearby, other, far_other, *early],
        [((rows_each, 2, LANES), f32)] * 3,
        [],
        scalars=1,
    )
    new_params, new_first, new_second = [
        jnp.swapaxes(value, 0, 1).reshape(2, width) for value in results
    ]
    return (outputs, input_grad, new_params, new_first, new_second)


def solution(mesh):
    in_specs = (
        P("dp", None, None),
        P("dp", None, None),
        P("dp"),
        P(None, "dp"),
        P(None, "dp"),
        P(None, "dp"),
    )
    out_specs = (
        P("dp", None, None),
        P("dp", None, None),
        P(None, "dp"),
        P(None, "dp"),
        P(None, "dp"),
    )
    body = functools.partial(shards, mesh.shape["dp"])
    return jax.shard_map(body, mesh=mesh, in_specs=in_specs, out_specs=out_specs, check_vma=False)
```
